32 devices in a mesh: dp: 4 (over y, core), ctx: 2 (over x), tensor: 4 (over z).
Axes of the slice: x: 2, y: 2, z: 4, core: 2. Of those that a mesh axis runs over, the one named last changes fastest.
Arguments:
- layer_input: bfloat16 [4, 1024, 2304], P('dp', 'ctx'), may hold values from -6 to 6
- query_weight: bfloat16 [2304, 2048], P(('dp', 'ctx'), 'tensor'), may hold values from -0.125 to 0.125
- key_weight: bfloat16 [2304, 1024], P(('dp', 'ctx'), 'tensor'), may hold values from -0.125 to 0.125
- value_weight: bfloat16 [2304, 1024], P(('dp', 'ctx'), 'tensor'), may hold values from -0.125 to 0.125
- output_weight: bfloat16 [2304, 2048], P(('dp', 'ctx'), 'tensor'), may hold values from -0.125 to 0.125
- gate_weight: bfloat16 [2304, 9216], P(('dp', 'ctx'), 'tensor'), may hold values from -0.125 to 0.125
- up_weight: bfloat16 [2304, 9216], P(('dp', 'ctx'), 'tensor'), may hold values from -0.125 to 0.125
- down_weight: bfloat16 [2304, 9216], P(('dp', 'ctx'), 'tensor'), may hold values from -0.0625 to 0.0625
- attn_in_gain: bfloat16 [2304], P(('dp', 'ctx')), may hold values from -0.5 to 0.5
- attn_out_gain: bfloat16 [2304], P(('dp', 'ctx')), may hold values from -0.5 to 0.5
- ffn_in_gain: bfloat16 [2304], P(('dp', 'ctx')), may hold values from -0.5 to 0.5
- ffn_out_gain: bfloat16 [2304], P(('dp', 'ctx')), may hold values from -0.5 to 0.5
- out_cotangent: bfloat16 [4, 1024, 2304], P('dp', 'ctx'), may hold values from -6 to 6
- segment_ids: int32 [4, 1024], P('dp', 'ctx'), may hold values from 0 to 3, as said below
- live_mask: int32 [4, 1024], P('dp', 'ctx'), may hold values from 0 to 1, as said below
Outputs:
- layer_output: bfloat16 [4, 1024, 2304], P('dp', 'ctx')
- input_grad: float32 [4, 1024, 2304], P('dp', 'ctx')
- query_grad: float32 [2304, 2048], P(('dp', 'ctx'), 'tensor')
- key_grad: float32 [2304, 1024], P(('dp', 'ctx'), 'tensor')
- value_grad: float32 [2304, 1024], P(('dp', 'ctx'), 'tensor')
- output_grad: float32 [2304, 2048], P(('dp', 'ctx'), 'tensor')
- gate_grad: float32 [2304, 9216], P(('dp', 'ctx'), 'tensor')
- up_grad: float32 [2304, 9216], P(('dp', 'ctx'), 'tensor')
- down_grad: float32 [2304, 9216], P(('dp', 'ctx'), 'tensor')
- attn_in_gain_grad: float32 [2304], P(('dp', 'ctx'))
- attn_out_gain_grad: float32 [2304], P(('dp', 'ctx'))
- ffn_in_gain_grad: float32 [2304], P(('dp', 'ctx'))
- ffn_out_gain_grad: float32 [2304], P(('dp', 'ctx'))
The draws below stay inside these ranges and needn't reach their ends.
Inputs may be any that keep to these rules, and one draw needn't show every extreme that they name: `segment_ids`: each row holds four documents numbered 0 to 3 in order; document 1 starts within the first 256 positions of its row and its last position lies within the last 512 positions of its row. `live_mask`: the zeros form a nonempty run of at most 256 positions that ends each row, inside document 3, which keeps at least one real token.
All inputs are finite; a program needn't handle non-finite values.
Results may differ from the reference program's by a relative error of at most 0.017.
Values may be sent and summed in bfloat16 or wider, within the bound.
No kernel may reach another device: no remote copies, remote signals or barrier semaphores. Data moves between devices by JAX's collectives and lax.ppermute only.
A program may use at most 192 MiB of HBM per device.

```python
import math
import jax
import jax.numpy as jnp
from jax import lax

D = 2304
FF = 9216
QH = 8
KVH = 4
HD = 256
TOK_DEV = 512
ROWS = 4
LEN = 1024


def doc_layout(key):
    key_first, key_padding, key_margin, key_cut = jax.random.split(key, 4)
    first_end = jax.random.randint(key_first, (ROWS,), 1, TOK_DEV // 2)
    padding = jax.random.randint(key_padding, (ROWS,), 1, TOK_DEV // 2 + 1)
    margin = jax.random.randint(key_margin, (ROWS,), 2, TOK_DEV // 4 + 2)
    long_end = LEN - padding - margin
    last_start = jax.random.randint(key_cut, (ROWS,), long_end + 1, long_end + margin)
    indices = jnp.arange(LEN, dtype=jnp.int32)[None, :]
    segments = (indices >= first_end[:, None]).astype(jnp.int32) + (indices >= long_end[:, None]).astype(jnp.int32) + (indices >= last_start[:, None]).astype(jnp.int32)
    live = (indices < (LEN - padding)[:, None]).astype(jnp.int32)
    return (segments, live)


def draw_segment_ids(key, part):
    segments, live = doc_layout(key)
    return segments


def draw_live_mask(key, part):
    segments, live = doc_layout(key)
    return live


def block_levels(own_key, dims, cuts, low, high):
    level = 1.0
    for dim, shards_of in cuts:
        steps = jax.random.uniform(jax.random.fold_in(jax.random.fold_in(own_key, 6), dim), (shards_of,), jnp.float32, low / len(cuts), high / len(cuts))
        level = level * jnp.repeat(jnp.exp(steps), dims[dim] // shards_of).reshape((-1,) + (1,) * (len(dims) - 1 - dim))
    return level


def gaussian(stream_key, dims, spread, limit, cuts=(), held_as=jnp.bfloat16):
    level = block_levels(stream_key, dims, cuts, -0.22, 0.18) if cuts else 1.0
    entries = jax.random.normal(stream_key, dims, jnp.float32) * spread * level
    return jnp.minimum(jnp.maximum(entries, -limit), limit).astype(held_as)


def setup_inputs(seed: int = 0) -> dict:
    seeds = jax.random.split(jax.random.key(seed), 16)
    return {
        "layer_input": gaussian(seeds[0], (ROWS, LEN, D), 1.0, 6.0, ((0, 4), (1, 2))),
        "query_weight": gaussian(seeds[1], (D, QH * HD), D ** -0.5, 0.125, ((0, 8), (1, 4))),
        "key_weight": gaussian(seeds[2], (D, KVH * HD), D ** -0.5, 0.125, ((0, 8), (1, 4))),
        "value_weight": gaussian(seeds[3], (D, KVH * HD), D ** -0.5, 0.125, ((0, 8), (1, 4))),
        "output_weight": gaussian(seeds[4], (D, QH * HD), (QH * HD) ** -0.5, 0.125, ((0, 8), (1, 4))),
        "gate_weight": gaussian(seeds[5], (D, FF), D ** -0.5, 0.125, ((0, 8), (1, 4))),
        "up_weight": gaussian(seeds[6], (D, FF), D ** -0.5, 0.125, ((0, 8), (1, 4))),
        "down_weight": gaussian(seeds[7], (D, FF), FF ** -0.5, 0.0625, ((0, 8), (1, 4))),
        "attn_in_gain": jnp.clip(jax.random.uniform(seeds[8], (D,), jnp.float32, -0.5, 0.5) * block_levels(seeds[8], (D,), ((0, 8),), -0.4, 0.0), -0.5, 0.5).astype(jnp.bfloat16),
        "attn_out_gain": jnp.clip(jax.random.uniform(seeds[9], (D,), jnp.float32, -0.5, 0.5) * block_levels(seeds[9], (D,), ((0, 8),), -0.4, 0.0), -0.5, 0.5).astype(jnp.bfloat16),
        "ffn_in_gain": jnp.clip(jax.random.uniform(seeds[10], (D,), jnp.float32, -0.5, 0.5) * block_levels(seeds[10], (D,), ((0, 8),), -0.4, 0.0), -0.5, 0.5).astype(jnp.bfloat16),
        "ffn_out_gain": jnp.clip(jax.random.uniform(seeds[11], (D,), jnp.float32, -0.5, 0.5) * block_levels(seeds[11], (D,), ((0, 8),), -0.4, 0.0), -0.5, 0.5).astype(jnp.bfloat16),
        "out_cotangent": gaussian(seeds[12], (ROWS, LEN, D), 1.0, 6.0, ((0, 4), (1, 2))),
        "segment_ids": draw_segment_ids(jax.random.fold_in(seeds[15], 71), 0),
        "live_mask": draw_live_mask(jax.random.fold_in(seeds[15], 71), 0),
    }


NORM_EPSILON = 1e-06
SOFT_CAP = 50.0
MASKED_SCORE = -1e+30
HIGHEST = lax.Precision.HIGHEST

@jax.custom_vjp
def low(v):
    return lax.optimization_barrier(v.astype(jnp.bfloat16)).astype(jnp.float32)

@jax.custom_vjp
def low_back(v):
    return v

def low_keep(v):
    return (low(v), None)

def low_pass(kept, grad):
    return (grad,)

def back_keep(v):
    return (v, None)

def back_low(kept, grad):
    return (low(grad),)
low.defvjp(low_keep, low_pass)
low_back.defvjp(back_keep, back_low)

def rms_norm(values, gain):
    factor = lax.rsqrt(lax.optimization_barrier(jnp.mean(values * values, axis=-1, keepdims=True)) + NORM_EPSILON)
    return values * factor * (1.0 + gain)

def gelu_tanh(values):
    tanh_input = math.sqrt(2.0 / math.pi) * (values + 0.044715 * values * values * values)
    return 0.5 * values * (1.0 + jnp.tanh(tanh_input))

def doc_positions(segments):
    length = segments.shape[1]
    indices = jnp.arange(length, dtype=jnp.int32)[None, :]
    boundary = jnp.concatenate([jnp.ones((segments.shape[0], 1), dtype=bool), segments[:, 1:] != segments[:, :-1]], axis=1)
    starts = lax.cummax(jnp.where(boundary, indices, jnp.zeros_like(indices)), axis=1)
    return indices - starts

def rotary_tables(positions, head_size):
    half_size = head_size // 2
    frequency = jnp.exp(jnp.arange(half_size, dtype=jnp.float32) * (-2.0 * math.log(10000.0) / head_size))
    angles = positions.astype(jnp.float32)[..., None] * frequency
    return (jnp.cos(angles), jnp.sin(angles))

def rotate(values, cos_table, sin_table):
    half_size = values.shape[-1] // 2
    front_half = values[..., :half_size]
    back_half = values[..., half_size:]
    return jnp.concatenate([front_half * cos_table - back_half * sin_table, back_half * cos_table + front_half * sin_table], axis=-1)

def product(left, right):
    return jnp.dot(left, right, precision=HIGHEST)

def product_rows(left, right):
    return jnp.einsum('ti,di->td', left, right, precision=HIGHEST)

def forward(inputs, query_weight, key_weight, value_weight, output_weight, gate_weight, up_weight, down_weight, attn_in_gain, attn_out_gain, ffn_in_gain, ffn_out_gain, segment_ids, live_mask):
    row_count, length, model_width = inputs.shape
    token_total = row_count * length
    group_size = QH // KVH
    block_rows = math.gcd(length, 512)
    block_count = length // block_rows
    positions = doc_positions(segment_ids)
    cos_table, sin_table = rotary_tables(positions, HD)
    flat_input = inputs.reshape(token_total, model_width)
    attn_input = low(rms_norm(flat_input, attn_in_gain))
    query_raw = low_back(product(attn_input, query_weight)).reshape(row_count, length, KVH, group_size, HD)
    key_raw = low_back(product(attn_input, key_weight)).reshape(row_count, length, KVH, HD)
    value_rows = low(low_back(product(attn_input, value_weight))).reshape(row_count, length, KVH, HD)
    queries = low(rotate(query_raw, cos_table[:, :, None, None, :], sin_table[:, :, None, None, :]) * (1.0 / math.sqrt(HD)))
    key_rows = low(rotate(key_raw, cos_table[:, :, None, :], sin_table[:, :, None, :]))
    key_index = jnp.arange(length, dtype=jnp.int32)

    def one_block(block_index):
        row_index = block_index // block_count
        offset = block_index % block_count * block_rows
        row_queries = lax.dynamic_index_in_dim(queries, row_index, 0, keepdims=False)
        query_block = lax.dynamic_slice_in_dim(row_queries, offset, block_rows, 0)
        row_keys = lax.dynamic_index_in_dim(key_rows, row_index, 0, keepdims=False)
        row_values = lax.dynamic_index_in_dim(value_rows, row_index, 0, keepdims=False)
        row_segments = lax.dynamic_index_in_dim(segment_ids, row_index, 0, keepdims=False)
        row_live = lax.dynamic_index_in_dim(live_mask, row_index, 0, keepdims=False)
        query_segments = lax.dynamic_slice_in_dim(row_segments, offset, block_rows, 0)
        query_index = offset + jnp.arange(block_rows, dtype=jnp.int32)
        allowed = (key_index[None, :] <= query_index[:, None]) & (row_segments[None, :] == query_segments[:, None])
        allowed = allowed & ((row_live[None, :] == 1) | (key_index[None, :] == query_index[:, None]))
        raw_scores = low_back(jnp.einsum('tkgd,lkd->kgtl', query_block, row_keys, precision=HIGHEST))
        capped = jnp.where(allowed, SOFT_CAP * jnp.tanh(raw_scores / SOFT_CAP), MASKED_SCORE)
        row_peak = lax.optimization_barrier(jnp.max(capped, axis=-1, keepdims=True))
        exp_scores = jnp.exp(capped - row_peak)
        attn_probs = exp_scores / lax.optimization_barrier(jnp.sum(exp_scores, axis=-1, keepdims=True))
        return jnp.einsum('kgtl,lkd->tkgd', low(attn_probs), row_values, precision=HIGHEST)
    blocks = lax.map(jax.checkpoint(one_block), jnp.arange(row_count * block_count, dtype=jnp.int32))
    heads_out = low(low_back(blocks.reshape(token_total, QH * HD)))
    attn_out = low_back(product_rows(heads_out, output_weight))
    mid_rows = flat_input + rms_norm(attn_out, attn_out_gain)
    ffn_input = low(rms_norm(mid_rows, ffn_in_gain))
    gate_act = low_back(product(ffn_input, gate_weight))
    up_act = low_back(product(ffn_input, up_weight))
    hidden = low(gelu_tanh(gate_act) * up_act)
    ffn_out = low_back(product_rows(hidden, down_weight))
    return (mid_rows + rms_norm(ffn_out, ffn_out_gain)).reshape(row_count, length, model_width)

def reference(layer_input, query_weight, key_weight, value_weight, output_weight, gate_weight, up_weight, down_weight, attn_in_gain, attn_out_gain, ffn_in_gain, ffn_out_gain, out_cotangent, segment_ids, live_mask):
    floats = tuple((operand.astype(jnp.float32) for operand in (layer_input, query_weight, key_weight, value_weight, output_weight, gate_weight, up_weight, down_weight, attn_in_gain, attn_out_gain, ffn_in_gain, ffn_out_gain)))

    def apply_layer(*operands):
        return forward(*operands, segment_ids, live_mask)
    result, pullback = jax.vjp(apply_layer, *floats)
    gradients = pullback(out_cotangent.astype(jnp.float32))
    return (result.astype(jnp.bfloat16), gradients[0], gradients[1], gradients[2], gradients[3], gradients[4], gradients[5], gradients[6], gradients[7], gradients[8], gradients[9], gradients[10], gradients[11])
```

```python
import math

import jax
import jax.numpy as jnp
from jax import lax
from jax.sharding import Mesh
from jax.sharding import PartitionSpec as P

QH = 8
KVH = 4
HD = 256

NORM_EPSILON = 1e-06
SOFT_CAP = 50.0
MASKED_SCORE = -1e30
SWAP = [(0, 1), (1, 0)]
LOW = jnp.bfloat16
F32 = jnp.float32


def wide(a):
    return a.astype(F32)


def norm_factor(v):
    return lax.rsqrt(jnp.mean(v * v, axis=-1, keepdims=True) + NORM_EPSILON)


def norm_back(v, gain, grad):
    r = norm_factor(v)
    w = (1.0 + gain) * grad
    dv = r * w - v * (r * r * r) * jnp.mean(v * w, axis=-1, keepdims=True)
    dg = jnp.sum(grad * v * r, axis=0, keepdims=True)
    return dv, dg


def gelu_parts(u):
    k = math.sqrt(2.0 / math.pi)
    th = jnp.tanh(k * (u + 0.044715 * u * u * u))
    g = 0.5 * u * (1.0 + th)
    dg = 0.5 * (1.0 + th) + 0.5 * u * (1.0 - th * th) * k * (1.0 + 3 * 0.044715 * u * u)
    return g, dg


def dot(a, b):
    return jnp.dot(a, b, preferred_element_type=F32)


def dot_t(a, b):
    return jnp.einsum("ti,di->td", a, b, preferred_element_type=F32)


def outer(a, b):
    return jnp.einsum("td,ti->di", a, b, preferred_element_type=F32)


def to_ctx(a):
    return lax.ppermute(a, "ctx", SWAP)


def to_y(a):
    return lax.ppermute(a, "y", SWAP)


def to_core(a):
    return lax.ppermute(a, "core", SWAP)


def rotate(v, c, s):
    h = HD // 2
    a, b = v[..., :h], v[..., h:]
    return jnp.concatenate([a * c - b * s, b * c + a * s], axis=-1)


def rotate_back(v, c, s):
    h = HD // 2
    a, b = v[..., :h], v[..., h:]
    return jnp.concatenate([a * c + b * s, b * c - a * s], axis=-1)


def make_local(ny, nx):
    square = ny == 2 and nx == 2

    def order(v, back=False):
        blk = v.shape[1] // (2 * ny * nx)
        me_c = lax.axis_index("core")
        cut = lambda j: lax.slice_in_dim(v, j * blk, (j + 1) * blk, axis=1)
        if back:
            parts = {
                (c, y, x): cut((c * ny + y) * nx + x)
                for c in range(2)
                for y in range(ny)
                for x in range(nx)
            }
        else:
            parts = {
                (c, y, x): cut((y * 2 + c) * nx + x)
                for c in range(2)
                for y in range(ny)
                for x in range(nx)
            }
        bits = [(0, me_c)]
        if square:
            bits += [(1, lax.axis_index("y")), (2, lax.axis_index("ctx"))]
        for pos, bit in bits:
            flip = lambda k: tuple(1 - e if i == pos else e for i, e in enumerate(k))
            parts = {k: jnp.where(bit == 0, parts[k], parts[flip(k)]) for k in parts}
        if back:
            out = [
                parts[(c, y, x)]
                for y in range(ny)
                for c in range(2)
                for x in range(nx)
            ]
        else:
            out = [
                parts[(c, y, x)]
                for c in range(2)
                for y in range(ny)
                for x in range(nx)
            ]
        return jnp.concatenate(out, axis=1)

    def gather(w):
        if square:
            h = w.shape[0] // 2
            wx, wy = to_ctx(w), to_y(w)
            d1, d2 = to_y(wx[:h]), to_ctx(wy[h:])
            mine = jnp.concatenate([w, wx, wy, d1, d2], axis=0)
        else:
            mine = lax.all_gather(w, ("y", "ctx"), axis=0, tiled=True)
        return mine, to_core(mine)

    def scatter(mine, other):
        s = wide(mine) + wide(to_core(other))
        if not square:
            return lax.psum_scatter(
                s.astype(LOW), ("y", "ctx"), scatter_dimension=0, tiled=True
            ).astype(F32)
        b = s.shape[0] // 4
        h = b // 2
        s0, s1, s2, s3 = [s[i * b : (i + 1) * b] for i in range(4)]
        s3 = s3.astype(LOW)
        gx, gy = to_ctx(s3[:h]), to_y(s3[h:])
        t1 = jnp.concatenate([s1[:h], s1[h:] + wide(gy)], axis=0).astype(LOW)
        t2 = jnp.concatenate([s2[:h] + wide(gx), s2[h:]], axis=0).astype(LOW)
        return s0 + wide(to_ctx(t1)) + wide(to_y(t2))

    def local(
        layer_input,
        query_weight,
        key_weight,
        value_weight,
        output_weight,
        gate_weight,
        up_weight,
        down_weight,
        attn_in_gain,
        attn_out_gain,
        ffn_in_gain,
        ffn_out_gain,
        out_cotangent,
        segment_ids,
        live_mask,
    ):
        rows, toks, width = layer_input.shape
        blk = query_weight.shape[0]
        qw, kw = query_weight.shape[1], key_weight.shape[1]
        qkv_w = qw + 2 * kw
        half = toks // 2
        halves = [slice(0, half), slice(half, toks)]
        scale = 1.0 / math.sqrt(HD)

        gains = jnp.stack([attn_in_gain, attn_out_gain, ffn_in_gain, ffn_out_gain])
        gains = jnp.pad(gains, ((0, 12), (0, qkv_w - blk)))
        qkv_own = jnp.concatenate([query_weight, key_weight, value_weight], axis=1)
        packet = jnp.concatenate([qkv_own, gains], axis=0)

        def gather_packet():
            if square:
                px, py = to_ctx(packet), to_y(packet)
                h = packet.shape[0] // 2
                d1, d2 = to_y(px[:h]), to_ctx(py[h:])
                four = [packet, px, py, jnp.concatenate([d1, d2], axis=0)]
            else:
                full = lax.all_gather(packet, ("y", "ctx"), axis=0, tiled=True)
                four = [
                    full[i * packet.shape[0] : (i + 1) * packet.shape[0]]
                    for i in range(ny * nx)
                ]
            both = jnp.concatenate(four, axis=0)
            sib = to_core(both)
            n = packet.shape[0]
            pick = lambda a: (
                jnp.concatenate([a[i * n : i * n + blk] for i in range(ny * nx)], 0),
                jnp.concatenate(
                    [a[i * n + blk : i * n + blk + 4, :blk] for i in range(ny * nx)], 1
                ),
            )
            (m, gm), (s, gs) = pick(both), pick(sib)
            return m, s, wide(jnp.concatenate([gm, gs], axis=1))

        qkv_m, qkv_s, gain = gather_packet()
        g1, g2, g3, g4 = [gain[i : i + 1] for i in range(4)]
        out_m, out_s = gather(output_weight)
        gate_m, gate_s = gather(gate_weight)
        up_m, up_s = gather(up_weight)
        down_m, down_s = gather(down_weight)
        mid = width // 2

        def times(h, wm, ws):
            return dot(h[:, :mid], wm) + dot(h[:, mid:], ws)

        def times_t(u, wm, ws):
            return jnp.concatenate([dot_t(u, wm), dot_t(u, ws)], axis=1)

        index = lax.axis_index("ctx") * toks + jnp.arange(toks, dtype=jnp.int32)
        own_info = jnp.concatenate([segment_ids, live_mask, index[None]], axis=0)
        if square:
            info = jnp.concatenate([own_info, to_ctx(own_info)], axis=1)
        else:
            info = lax.all_gather(own_info, "ctx", axis=1, tiled=True)
        seg_all, live_all, index_all = info[0:1], info[1:2], info[2:3]
        seg_col, index_col = segment_ids.reshape(toks, 1), index.reshape(toks, 1)
        start = jnp.sum((seg_all < seg_col).astype(jnp.int32), axis=1)
        pos = index - start
        allowed = (
            (index_all <= index_col)
            & (seg_all == seg_col)
            & ((live_all == 1) | (index_all == index_col))
        )
        freq = jnp.exp(
            jnp.arange(HD // 2, dtype=F32) * (-2.0 * math.log(10000.0) / HD)
        )
        angle = wide(pos)[:, None] * freq
        cos, sin = jnp.cos(angle), jnp.sin(angle)
        cos, sin = cos[:, None, :], sin[:, None, :]

        x = wide(order(layer_input.reshape(toks, width)))
        dy = wide(order(out_cotangent.reshape(toks, width)))
        h1 = (x * norm_factor(x) * (1.0 + g1)).astype(LOW)

        qkv = times(h1, qkv_m, qkv_s)
        heads, groups = qw // HD, kw // HD
        per = heads // groups
        q = (rotate(qkv[:, :qw].reshape(toks, heads, HD), cos, sin) * scale).astype(LOW)
        k = rotate(qkv[:, qw : qw + kw].reshape(toks, groups, HD), cos, sin).astype(LOW)
        kv = jnp.concatenate([k.reshape(toks, kw), qkv[:, qw + kw :].astype(LOW)], 1)
        if square:
            kv_all = jnp.concatenate([kv, to_ctx(kv)], axis=0)
        else:
            kv_all = lax.all_gather(kv, "ctx", axis=0, tiled=True)
        length = kv_all.shape[0]
        k_all = kv_all[:, :kw].reshape(length, groups, HD)
        v_all = kv_all[:, kw:].reshape(length, groups, HD)
        q = q.reshape(toks, groups, per, HD)

        def scores(sl):
            raw = jnp.einsum(
                "tkgd,lkd->kgtl", q[sl], k_all, preferred_element_type=F32
            )
            bounded = jnp.tanh(raw / SOFT_CAP)
            return jnp.where(allowed[sl], SOFT_CAP * bounded, MASKED_SCORE), bounded

        xs = [x[sl] for sl in halves]
        dys = [dy[sl] for sl in halves]
        outs_low, logs, attn = [], [], []
        for sl in halves:
            capped, _ = scores(sl)
            peak = jnp.max(capped, axis=-1, keepdims=True)
            e = jnp.exp(capped - peak)
            total = jnp.sum(e, axis=-1, keepdims=True)
            logs.append(peak + jnp.log(total))
            p = (e / total).astype(LOW)
            o = jnp.einsum("kgtl,lkd->tkgd", p, v_all, preferred_element_type=F32)
            o = o.reshape(half, qw).astype(LOW)
            outs_low.append(o)
            attn.append(lax.psum(times_t(o, out_m, out_s).astype(LOW), "tensor"))
        mids, h3s, gates, ups, hids, fs = [], [], [], [], [], []
        for i, sl in enumerate(halves):
            a = wide(attn[i])
            x2 = xs[i] + a * norm_factor(a) * (1.0 + g2)
            h3 = (x2 * norm_factor(x2) * (1.0 + g3)).astype(LOW)
            mids.append(x2)
            h3s.append(h3)
            gates.append(times(h3, gate_m, gate_s))
            ups.append(times(h3, up_m, up_s))
            hids.append((gelu_parts(gates[i])[0] * ups[i]).astype(LOW))
            f = times_t(hids[i], down_m, down_s)
            fs.append(lax.psum(f.astype(LOW), "tensor"))
        ys, dfs, dgs, dus, dh3s = [], [], [], [], []
        dg4 = 0.0
        for i in range(2):
            f = wide(fs[i])
            ys.append((mids[i] + f * norm_factor(f) * (1.0 + g4)).astype(LOW))
            df, dg = norm_back(f, g4, dys[i])
            dg4 = dg4 + dg
            df = df.astype(LOW)
            dfs.append(df)
            dhid = times(df, down_m, down_s)
            gl, dgl = gelu_parts(gates[i])
            dgs.append((dhid * ups[i] * dgl).astype(LOW))
            dus.append((dhid * gl).astype(LOW))
            part = times_t(dgs[i], gate_m, gate_s) + times_t(dus[i], up_m, up_s)
            dh3s.append(lax.psum(part.astype(LOW), "tensor"))
        cat = lambda a: jnp.concatenate(a, axis=0)
        h3, dgl, dul, dfl, hid = map(cat, (h3s, dgs, dus, dfs, hids))

        def weight_grad(a, b):
            other = outer(a[:, mid:], b).astype(LOW)
            return scatter(outer(a[:, :mid], b), other)

        down_grad = weight_grad(dfl, hid)
        gate_grad = weight_grad(h3, dgl)
        up_grad = weight_grad(h3, dul)

        dx2s, dabs, dqs = [], [], []
        dg3 = dg2 = 0.0
        dk_all = dv_all = 0.0
        for i, sl in enumerate(halves):
            dv3, dg = norm_back(mids[i], g3, wide(dh3s[i]))
            dg3 = dg3 + dg
            dx2 = dys[i] + dv3
            dx2s.append(dx2)
            da, dg = norm_back(wide(attn[i]), g2, dx2)
            dg2 = dg2 + dg
            dab = da.astype(LOW)
            dabs.append(dab)
            do = times(dab, out_m, out_s).astype(LOW).reshape(half, groups, per, HD)
            capped, bounded = scores(sl)
            p = jnp.exp(capped - logs[i])
            dp = jnp.einsum("tkgd,lkd->kgtl", do, v_all, preferred_element_type=F32)
            dc = p * (dp - jnp.sum(p * dp, axis=-1, keepdims=True))
            ds = (dc * (1.0 - bounded * bounded)).astype(LOW)
            dq = jnp.einsum("kgtl,lkd->tkgd", ds, k_all, preferred_element_type=F32)
            dqs.append(dq.reshape(half, heads, HD))
            dk_all = dk_all + jnp.einsum(
                "kgtl,tkgd->lkd", ds, q[sl], preferred_element_type=F32
            )
            dv_all = dv_all + jnp.einsum(
                "kgtl,tkgd->lkd", p.astype(LOW), do, preferred_element_type=F32
            )
        dkv = jnp.concatenate(
            [dk_all.reshape(length, kw), dv_all.reshape(length, kw)], axis=1
        )
        if square:
            dkv = dkv[:toks] + wide(to_ctx(dkv[toks:].astype(LOW)))
        else:
            dkv = wide(
                lax.psum_scatter(
                    dkv.astype(LOW), "ctx", scatter_dimension=0, tiled=True
                )
            )
        dqr = (rotate_back(cat(dqs), cos, sin) * scale).astype(LOW).reshape(toks, qw)
        dkr = rotate_back(dkv[:, :kw].reshape(toks, groups, HD), cos, sin).astype(LOW)
        dqkv = jnp.concatenate(
            [dqr, dkr.reshape(toks, kw), dkv[:, kw:].astype(LOW)], axis=1
        )
        dh1 = wide(
            lax.psum(times_t(dqkv, qkv_m, qkv_s).astype(LOW), "tensor")
        )
        dab, o = cat(dabs), cat(outs_low)
        low = jnp.concatenate(
            [outer(h1[:, mid:], dqkv), outer(dab[:, mid:], o)], axis=1
        ).astype(LOW)
        high = jnp.concatenate(
            [outer(h1[:, :mid], dqkv), outer(dab[:, :mid], o)], axis=1
        )
        attn_grad = scatter(high, low)
        dv1, dg1 = norm_back(x, g1, dh1)
        input_grad = order(cat(dx2s) + dv1, back=True)
        layer_output = order(cat(ys), back=True)

        dgain = jnp.concatenate([dg1, dg2, dg3, dg4], axis=0)
        if square:
            dgain = dgain[:, :mid] + to_core(dgain[:, mid:])
            s = dgain[:, : mid // 2] + to_y(dgain[:, mid // 2 :])
            dgain = s[:, :blk] + to_ctx(s[:, blk:])
        else:
            dgain = dgain[:, :mid] + to_core(dgain[:, mid:])
            dgain = lax.psum_scatter(
                dgain, ("y", "ctx"), scatter_dimension=1, tiled=True
            )
        return (
            layer_output.reshape(rows, toks, width),
            input_grad.reshape(rows, toks, width),
            attn_grad[:, :qw],
            attn_grad[:, qw : qw + kw],
            attn_grad[:, qw + kw : qkv_w],
            attn_grad[:, qkv_w:],
            gate_grad,
            up_grad,
            down_grad,
            dgain[0],
            dgain[1],
            dgain[2],
            dgain[3],
        )

    return local


def solution(mesh):
    dp, nx = mesh.shape["dp"], mesh.shape["ctx"]
    nz = mesh.shape["tensor"]
    fine = Mesh(
        mesh.devices.reshape(dp // 2, 2, nx, nz), ("y", "core", "ctx", "tensor")
    )
    d = ("y", "core")
    w = P(("y", "core", "ctx"), "tensor")
    g = P(("y", "core", "ctx"))
    t = P(d, "ctx", None)
    return jax.shard_map(
        make_local(dp // 2, nx),
        mesh=fine,
        in_specs=(t, w, w, w, w, w, w, w, g, g, g, g, t, P(d, "ctx"), P(d, "ctx")),
        out_specs=(t, t, w, w, w, w, w, w, w, g, g, g, g),
        check_vma=False,
    )
```

```python
import math

import jax
import jax.numpy as jnp
from jax import lax
from jax.experimental import pallas as pl
from jax.experimental.pallas import tpu as pltpu
from jax.sharding import Mesh
from jax.sharding import PartitionSpec as P

HD = 256
NORM_EPSILON = 1e-06
SOFT_CAP = 50.0
MASKED_SCORE = -1e30
SWAP = [(0, 1), (1, 0)]
LOW = jnp.bfloat16
F32 = jnp.float32
VMEM_MB = 56


def wide(a):
    return a.astype(F32)


def after(value, *deps):
    return lax.optimization_barrier((value,) + deps)[0]


class Order:
    def __init__(self):
        self.last = ()

    def __call__(self, *values):
        return after(values, *self.last) if self.last else values

    def run(self, fn, *values, **kw):
        out = fn(*self(*values), **kw)
        self.last = (out,)
        return out

    def send(self, move, value):
        (value,) = self(value)
        self.last = (value,)
        return move(value)


def to_ctx(a):
    return lax.ppermute(a, "ctx", SWAP)


def to_y(a):
    return lax.ppermute(a, "y", SWAP)


def to_core(a):
    return lax.ppermute(a, "core", SWAP)


def hop(bit):
    return lambda a: lax.ppermute(a, "tensor", [(k, k ^ bit) for k in range(4)])


def nn(a, b):
    return jnp.dot(a, b, preferred_element_type=F32)


def nt(a, b):
    return lax.dot_general(a, b, (((1,), (1,)), ((), ())), preferred_element_type=F32)


def tn(a, b):
    return lax.dot_general(a, b, (((0,), (0,)), ((), ())), preferred_element_type=F32)


def norm_factor(v):
    return lax.rsqrt(jnp.mean(v * v, axis=-1, keepdims=True) + NORM_EPSILON)


def norm_back(v, gain, grad):
    r = norm_factor(v)
    w = (1.0 + gain) * grad
    dv = r * w - v * (r * r * r) * jnp.mean(v * w, axis=-1, keepdims=True)
    dg = jnp.sum(grad * v * r, axis=0, keepdims=True)
    return dv, dg


def gelu_parts(u):
    k = math.sqrt(2.0 / math.pi)
    th = jnp.tanh(k * (u + 0.044715 * u * u * u))
    g = 0.5 * u * (1.0 + th)
    dg = 0.5 * (1.0 + th) + 0.5 * u * (1.0 - th * th) * k * (1.0 + 3 * 0.044715 * u * u)
    return g, dg


def turn(v, c, s):
    h = HD // 2
    a, b = v[:, :h], v[:, h:]
    return jnp.concatenate([a * c - b * s, b * c + a * s], axis=1)


def turn_back(v, c, s):
    h = HD // 2
    a, b = v[:, :h], v[:, h:]
    return jnp.concatenate([a * c + b * s, b * c - a * s], axis=1)


def kernel(body, grid, ins, outs, flops=0, scratch=()):
    size = lambda s, d: math.prod(s) * jnp.dtype(d).itemsize
    moved = sum(size(a.shape, a.dtype) for a, _, _ in ins)
    moved += sum(size(s, d) for s, d, _, _ in outs)
    return pl.pallas_call(
        body,
        grid=grid,
        in_specs=[pl.BlockSpec(b, m) for _, b, m in ins],
        out_specs=[pl.BlockSpec(b, m) for _, _, b, m in outs],
        out_shape=[jax.ShapeDtypeStruct(s, d) for s, d, _, _ in outs],
        scratch_shapes=list(scratch),
        cost_estimate=pl.CostEstimate(
            flops=int(flops), bytes_accessed=int(moved), transcendentals=0
        ),
        compiler_params=pltpu.CompilerParams(vmem_limit_bytes=VMEM_MB * 2**20),
    )(*[a for a, _, _ in ins])


def all_of(shape):
    return tuple(shape), lambda *i: (0,) * len(shape)


def qkv_kernel(x, gain, wm, ws, cos, sin, qw):
    toks, width = x.shape
    mid, cols = wm.shape
    kw = (cols - qw) // 2
    scale = 1.0 / math.sqrt(HD)

    def body(x_r, g_r, wm_r, ws_r, c_r, s_r, h_r, q_r, kv_r):
        xv = wide(x_r[...])
        h = (xv * norm_factor(xv) * (1.0 + g_r[...])).astype(LOW)
        h_r[...] = h
        raw = nn(h[:, :mid], wm_r[...]) + nn(h[:, mid:], ws_r[...])
        c, s = c_r[...], s_r[...]
        for j in range(qw // HD):
            cut = slice(j * HD, (j + 1) * HD)
            q_r[:, cut] = (turn(raw[:, cut], c, s) * scale).astype(LOW)
        for j in range(kw // HD):
            cut = slice(j * HD, (j + 1) * HD)
            kv_r[:, cut] = turn(raw[:, qw + j * HD : qw + (j + 1) * HD], c, s).astype(
                LOW
            )
        kv_r[:, kw:] = raw[:, qw + kw :].astype(LOW)

    ins = [(a, *all_of(a.shape)) for a in (x, gain, wm, ws, cos, sin)]
    outs = [
        ((toks, n), LOW, *all_of((toks, n))) for n in (width, qw, 2 * kw)
    ]
    return kernel(body, (1,), ins, outs, 2 * toks * width * cols)


def query_block(rows, length):
    return min(rows, 256 if length <= 2048 else 128)


def attn_kernel(q, kv, allowed, wm, ws):
    rows, qw = q.shape
    length = kv.shape[0]
    mid = wm.shape[0]
    qb = query_block(rows, length)
    heads = qw // HD

    def body(q_r, kv_r, m_r, wm_r, ws_r, o_r, t_r, a_r):
        ok = m_r[...] > 0
        k, v = kv_r[:, :HD], kv_r[:, HD:]
        logs = []
        for j in range(heads):
            cut = slice(j * HD, (j + 1) * HD)
            b = jnp.tanh(nt(q_r[:, cut], k) * (1.0 / SOFT_CAP))
            c = jnp.where(ok, SOFT_CAP * b, MASKED_SCORE)
            peak = jnp.max(c, axis=-1, keepdims=True)
            e = jnp.exp(c - peak)
            total = jnp.sum(e, axis=-1, keepdims=True)
            p = (e / total).astype(LOW)
            o_r[:, cut] = nn(p, v).astype(LOW)
            logs.append(jnp.broadcast_to(peak + jnp.log(total), (qb, 128)))
        t_r[...] = jnp.concatenate(logs, axis=1)
        o = o_r[...]
        a_r[:, :mid] = nt(o, wm_r[...]).astype(LOW)
        a_r[:, mid:] = nt(o, ws_r[...]).astype(LOW)

    row = lambda n: ((qb, n), lambda i: (i, 0))
    ins = [(q, *row(qw)), (kv, *all_of(kv.shape)), (allowed, *row(length))]
    ins += [(w, *all_of(w.shape)) for w in (wm, ws)]
    outs = [
        ((rows, qw), LOW, *row(qw)),
        ((rows, 128 * heads), F32, *row(128 * heads)),
        ((rows, 2 * mid), LOW, *row(2 * mid)),
    ]
    flops = 4 * rows * length * qw + 4 * rows * mid * qw
    return kernel(body, (rows // qb,), ins, outs, flops)


def attn_back_kernel(
    dh3, x2, dy, a, g3, g2, wm, ws, q, kv, allowed, logs, cos, sin, before
):
    rows, width = x2.shape
    qw = q.shape[1]
    length = kv.shape[0]
    mid = wm.shape[0]
    qb = query_block(rows, length)
    heads = qw // HD
    scale = 1.0 / math.sqrt(HD)
    first = before is None

    def body(*refs):
        refs = list(refs)
        d_r, x_r, dy_r, a_r, g3_r, g2_r, wm_r, ws_r = refs[:8]
        q_r, kv_r, m_r, t_r, c_r, s_r = refs[8:14]
        dx_r, da_r, dq_r, dkv_r, dg_r = refs[-5:]
        step = pl.program_id(0)

        @pl.when(step == 0)
        def _():
            dkv_r[...] = jnp.zeros_like(dkv_r) if first else refs[14][...]
            dg_r[...] = jnp.zeros_like(dg_r) if first else refs[15][...]

        dv3, dg3 = norm_back(x_r[...], g3_r[...], wide(d_r[...]))
        dx2 = wide(dy_r[...]) + dv3
        dx_r[...] = dx2
        da, dg2 = norm_back(wide(a_r[...]), g2_r[...], dx2)
        dg_r[0:1] += dg2
        dg_r[1:2] += dg3
        da = da.astype(LOW)
        da_r[...] = da
        do = (nn(da[:, :mid], wm_r[...]) + nn(da[:, mid:], ws_r[...])).astype(LOW)
        ok = m_r[...] > 0
        k, v = kv_r[:, :HD], kv_r[:, HD:]
        c, s = c_r[...], s_r[...]
        dk = dv = 0.0
        for j in range(heads):
            cut = slice(j * HD, (j + 1) * HD)
            qj, doj = q_r[:, cut], do[:, cut]
            b = jnp.tanh(nt(qj, k) * (1.0 / SOFT_CAP))
            logit = jnp.where(ok, SOFT_CAP * b, MASKED_SCORE)
            p = jnp.exp(logit - t_r[:, j * 128 : j * 128 + 1])
            dp = nt(doj, v)
            dc = p * (dp - jnp.sum(p * dp, axis=-1, keepdims=True))
            ds = (dc * (1.0 - b * b)).astype(LOW)
            dq_r[:, cut] = (turn_back(nn(ds, k), c, s) * scale).astype(LOW)
            dk = dk + tn(ds, qj)
            dv = dv + tn(p.astype(LOW), doj)
        dkv_r[:, :HD] += dk
        dkv_r[:, HD:] += dv

    row = lambda n: ((qb, n), lambda i: (i, 0))
    ins = [(v, *row(width)) for v in (dh3, x2, dy, a)]
    ins += [(v, *all_of(v.shape)) for v in (g3, g2, wm, ws)]
    ins += [(q, *row(qw)), (kv, *all_of(kv.shape)), (allowed, *row(length))]
    ins += [(logs, *row(128 * heads)), (cos, *row(HD // 2)), (sin, *row(HD // 2))]
    if not first:
        ins += [(v, *all_of(v.shape)) for v in before]
    outs = [
        ((rows, width), F32, *row(width)),
        ((rows, width), LOW, *row(width)),
        ((rows, qw), LOW, *row(qw)),
        ((length, 2 * HD), F32, *all_of((length, 2 * HD))),
        ((8, width), F32, *all_of((8, width))),
    ]
    flops = 10 * rows * length * qw + 4 * rows * mid * qw
    return kernel(body, (rows // qb,), ins, outs, flops)


def ffn_in_kernel(a, x, g2, g3, gm, gs, um, us):
    rows, width = x.shape
    mid, units = gm.shape
    bn = math.gcd(units, 768)

    def body(a_r, x_r, g2_r, g3_r, gm_r, gs_r, um_r, us_r, x2_r, h_r, g_r, u_r, hid_r):
        @pl.when(pl.program_id(0) == 0)
        def _():
            av = wide(a_r[...])
            x2 = wide(x_r[...]) + av * norm_factor(av) * (1.0 + g2_r[...])
            x2_r[...] = x2
            h_r[...] = (x2 * norm_factor(x2) * (1.0 + g3_r[...])).astype(LOW)

        hm, hs = h_r[:, :mid], h_r[:, mid:]
        gate = nn(hm, gm_r[...]) + nn(hs, gs_r[...])
        up = nn(hm, um_r[...]) + nn(hs, us_r[...])
        g_r[...] = gate
        u_r[...] = up
        hid_r[...] = (gelu_parts(gate)[0] * up).astype(LOW)

    w = ((mid, bn), lambda j: (0, j))
    t = ((rows, bn), lambda j: (0, j))
    ins = [(v, *all_of(v.shape)) for v in (a, x, g2, g3)]
    ins += [(v, *w) for v in (gm, gs, um, us)]
    outs = [
        ((rows, width), F32, *all_of((rows, width))),
        ((rows, width), LOW, *all_of((rows, width))),
        ((rows, units), F32, *t),
        ((rows, units), F32, *t),
        ((rows, units), LOW, *t),
    ]
    return kernel(body, (units // bn,), ins, outs, 4 * rows * width * units)


def project_kernel(u, wm, ws):
    rows, cols = u.shape
    mid = wm.shape[0]
    bd = math.gcd(mid, 384)
    n = mid // bd

    def body(u_r, m_r, s_r, o_r):
        j = pl.program_id(0)

        @pl.when(j < n)
        def _():
            o_r[...] = nt(u_r[...], m_r[...]).astype(LOW)

        @pl.when(j >= n)
        def _():
            o_r[...] = nt(u_r[...], s_r[...]).astype(LOW)

    ins = [
        (u, *all_of(u.shape)),
        (wm, (bd, cols), lambda j: (jnp.minimum(j, n - 1), 0)),
        (ws, (bd, cols), lambda j: (jnp.maximum(j - n, 0), 0)),
    ]
    outs = [((rows, 2 * mid), LOW, (rows, bd), lambda j: (0, j))]
    return kernel(body, (2 * n,), ins, outs, 4 * rows * mid * cols)[0]


def ffn_back_kernel(f, x2, dy, g4, gate, up, dm, ds, gm, gs, um, us):
    rows, width = x2.shape
    mid, units = dm.shape
    bn, bd = math.gcd(units, 768), math.gcd(mid, 384)
    n1, n2 = units // bn, mid // bd

    def body(
        f_r, x2_r, dy_r, g4_r, gate_r, up_r, dm_r, ds_r, gm_r, gs_r, um_r, us_r,
        y_r, df_r, dg_r, du_r, g_r, o_r,
    ):
        j = pl.program_id(0)

        @pl.when(j == 0)
        def _():
            fv, g4v = wide(f_r[...]), g4_r[...]
            y_r[...] = (x2_r[...] + fv * norm_factor(fv) * (1.0 + g4v)).astype(LOW)
            df, dg = norm_back(fv, g4v, wide(dy_r[...]))
            df_r[...] = df.astype(LOW)
            g_r[...] = dg

        for k in range(n1):

            @pl.when(j == k)
            def _():
                dh = nn(df_r[:, :mid], dm_r[...]) + nn(df_r[:, mid:], ds_r[...])
                gl, dgl = gelu_parts(gate_r[...])
                cut = slice(k * bn, (k + 1) * bn)
                dg_r[:, cut] = (dh * up_r[...] * dgl).astype(LOW)
                du_r[:, cut] = (dh * gl).astype(LOW)

        @pl.when((j >= n1) & (j < n1 + n2))
        def _():
            o_r[...] = (nt(dg_r[...], gm_r[...]) + nt(du_r[...], um_r[...])).astype(LOW)

        @pl.when(j >= n1 + n2)
        def _():
            o_r[...] = (nt(dg_r[...], gs_r[...]) + nt(du_r[...], us_r[...])).astype(LOW)

    w = ((mid, bn), lambda j: (0, jnp.minimum(j, n1 - 1)))
    t = ((rows, bn), lambda j: (0, jnp.minimum(j, n1 - 1)))
    lo = ((bd, units), lambda j: (jnp.clip(j - n1, 0, n2 - 1), 0))
    hi = ((bd, units), lambda j: (jnp.clip(j - n1 - n2, 0, n2 - 1), 0))
    ins = [(v, *all_of(v.shape)) for v in (f, x2, dy, g4)]
    ins += [(gate, *t), (up, *t), (dm, *w), (ds, *w)]
    ins += [(gm, *lo), (gs, *hi), (um, *lo), (us, *hi)]
    whole = lambda n, d: ((rows, n), d, *all_of((rows, n)))
    outs = [
        whole(width, LOW),
        whole(width, LOW),
        whole(units, LOW),
        whole(units, LOW),
        ((1, width), F32, *all_of((1, width))),
        ((rows, width), LOW, (rows, bd), lambda j: (0, jnp.maximum(j - n1, 0))),
    ]
    return kernel(body, (n1 + 2 * n2,), ins, outs, 6 * rows * width * units)


def outer_kernel(a, b, start, count, add=None):
    rows, cols = b.shape
    bm = math.gcd(count, 384)
    skip = start // bm

    def body(a_r, b_r, *rest):
        v = tn(a_r[...], b_r[...])
        if add is not None:
            v = v + wide(rest[0][...])
        rest[-1][...] = v.astype(LOW)

    ins = [(a, (rows, bm), lambda j: (0, j + skip)), (b, *all_of(b.shape))]
    tile = ((bm, cols), lambda j: (j, 0))
    if add is not None:
        ins.append((add, *tile))
    return kernel(
        body, (count // bm,), ins, [((count, cols), LOW, *tile)], 2 * rows * count * cols
    )[0]


def last_kernel(x, gain, dh1, dx2):
    rows, width = x.shape
    br = min(rows, 128)

    def body(x_r, g_r, d_r, dx_r, o_r, dg_r):
        dv, dg = norm_back(wide(x_r[...]), g_r[...], wide(d_r[...]))
        o_r[...] = dx_r[...] + dv

        @pl.when(pl.program_id(0) == 0)
        def _():
            dg_r[...] = dg

        @pl.when(pl.program_id(0) > 0)
        def _():
            dg_r[...] += dg

    row = ((br, width), lambda i: (i, 0))
    ins = [(x, *row), (gain, *all_of(gain.shape)), (dh1, *row), (dx2, *row)]
    outs = [((rows, width), F32, *row), ((1, width), F32, *all_of((1, width)))]
    return kernel(body, (rows // br,), ins, outs)


def keys_back_kernel(own, got, cos, sin):
    def body(a_r, b_r, c_r, s_r, o_r):
        v = a_r[...] + wide(b_r[...])
        o_r[:, :HD] = turn_back(v[:, :HD], c_r[...], s_r[...]).astype(LOW)
        o_r[:, HD:] = v[:, HD:].astype(LOW)

    ins = [(v, *all_of(v.shape)) for v in (own, got, cos, sin)]
    return kernel(body, (1,), ins, [(own.shape, LOW, *all_of(own.shape))])[0]


def make_local(ny, nx, nz):
    square = ny == 2 and nx == 2
    plane = ny * nx

    def order(v, back=False):
        blk = v.shape[1] // (2 * plane)
        here = lambda c, y, x: (c * ny + y) * nx + x
        there = lambda c, y, x: (y * 2 + c) * nx + x
        place = here if back else there
        keys = [(c, y, x) for c in range(2) for y in range(ny) for x in range(nx)]
        cut = lambda j: lax.slice_in_dim(v, j * blk, (j + 1) * blk, axis=1)
        parts = {k: cut(place(*k)) for k in keys}
        bits = [(0, lax.axis_index("core"))]
        if square:
            bits += [(1, lax.axis_index("y")), (2, lax.axis_index("ctx"))]
        for pos, bit in bits:
            flip = lambda k: tuple(1 - e if i == pos else e for i, e in enumerate(k))
            parts = {k: jnp.where(bit == 0, parts[k], parts[flip(k)]) for k in keys}
        if back:
            keys = [(c, y, x) for y in range(ny) for c in range(2) for x in range(nx)]
        return jnp.concatenate([parts[k] for k in keys], axis=1)

    def row_order(wm, ws):
        blk = wm.shape[0] // plane
        c = lax.axis_index("core")
        out = jnp.zeros((2 * wm.shape[0], wm.shape[1]), wm.dtype)
        for half, w in ((0, wm), (1, ws)):
            for y in range(ny):
                for x in range(nx):
                    i = y * nx + x
                    gy, gx = y, x
                    if square:
                        gy, gx = y ^ lax.axis_index("y"), x ^ lax.axis_index("ctx")
                    at = ((gy * 2 + (c ^ half)) * nx + gx) * blk
                    piece = lax.slice_in_dim(w, i * blk, (i + 1) * blk, axis=0)
                    out = lax.dynamic_update_slice_in_dim(out, piece, at, 0)
        return out

    def local(
        layer_input,
        query_weight,
        key_weight,
        value_weight,
        output_weight,
        gate_weight,
        up_weight,
        down_weight,
        attn_in_gain,
        attn_out_gain,
        ffn_in_gain,
        ffn_out_gain,
        out_cotangent,
        segment_ids,
        live_mask,
    ):
        rows, toks, width = layer_input.shape
        blk, qw = query_weight.shape
        kw = key_weight.shape[1]
        qkv_w = qw + 2 * kw
        mid = width // 2
        half = toks // 2
        ab = (slice(0, half), slice(half, toks))
        seq = Order()

        b0, b1 = lax.axis_index("tensor") & 1, (lax.axis_index("tensor") >> 1) & 1

        def take(a, k, n):
            return lax.dynamic_slice_in_dim(a, k * n, n, 0)

        def join(a, b, bit):
            return jnp.where(
                bit == 0, jnp.concatenate([a, b], 0), jnp.concatenate([b, a], 0)
            )

        class Exchange:
            def __init__(self, part):
                self.part = part
                if nz != 4:
                    self.out = lax.psum(part, "tensor")
                    return
                n = part.shape[0] // 2
                self.keep = take(part, b0, n)
                self.got = seq.send(hop(1), take(part, 1 - b0, n))

            def two(self):
                if nz != 4:
                    return
                keep, got = seq(self.keep, self.got)
                s = wide(keep) + wide(got)
                n = s.shape[0] // 2
                self.keep = take(s, b1, n)
                self.got = seq.send(hop(2), take(s, 1 - b1, n).astype(LOW))

            def three(self):
                if nz != 4:
                    return
                keep, got = seq(self.keep, self.got)
                self.keep = (keep + wide(got)).astype(LOW)
                self.got = seq.send(hop(2), self.keep)

            def four(self):
                if nz != 4:
                    return
                keep, got = seq(self.keep, self.got)
                self.keep = join(keep, got, b1)
                self.got = seq.send(hop(1), self.keep)

            def end(self):
                if nz == 4:
                    self.out = join(self.keep, self.got, b0)
                return self.out

        gains = jnp.stack([attn_in_gain, attn_out_gain, ffn_in_gain, ffn_out_gain])
        gains = jnp.pad(gains, ((0, 12), (0, qkv_w - blk)))
        qkv_own = jnp.concatenate([query_weight, key_weight, value_weight], axis=1)
        packet = jnp.concatenate([qkv_own, gains], axis=0)
        index = lax.axis_index("ctx") * toks + jnp.arange(toks, dtype=jnp.int32)
        own_info = jnp.concatenate([segment_ids, live_mask, index[None]], axis=0)

        def near(w):
            return seq.send(to_ctx, w), seq.send(to_y, w)

        def far(got):
            h = got[0].shape[0] // 2
            wx, wy = seq(got[0], got[1])
            return seq.send(to_y, wx[:h]), seq.send(to_ctx, wy[h:])

        def whole(w):
            return lax.all_gather(w, ("y", "ctx"), axis=0, tiled=True)

        def stack(*a):
            return seq.run(lambda *v: jnp.concatenate(v, axis=0), *a)

        def positions(info):
            seg_all, live_all, index_all = info[0:1], info[1:2], info[2:3]
            seg_col, index_col = segment_ids.reshape(toks, 1), index.reshape(toks, 1)
            start = jnp.sum((seg_all < seg_col).astype(jnp.int32), axis=1)
            allowed = (
                (index_all <= index_col)
                & (seg_all == seg_col)
                & ((live_all == 1) | (index_all == index_col))
            ).astype(LOW)
            freq = jnp.exp(
                jnp.arange(HD // 2, dtype=F32) * (-2.0 * math.log(10000.0) / HD)
            )
            angle = wide(index - start)[:, None] * freq
            return allowed, jnp.cos(angle), jnp.sin(angle)

        x_raw = layer_input.reshape(toks, width)
        dy_raw = out_cotangent.reshape(toks, width)
        if square:
            n_pk = near(packet)
            n_out = near(output_weight)
            info = jnp.concatenate([own_info, seq.send(to_ctx, own_info)], axis=1)
            x = seq.run(order, x_raw)
            f_pk = far(n_pk)
            f_out = far(n_out)
            half_w = gate_weight.shape[1] // 2
            n_ga = near(gate_weight[:, :half_w])
            allowed, cos, sin = seq.run(positions, info)
            packet4 = stack(packet, *n_pk, *f_pk)
            packet_s = seq.send(to_core, packet4)
            out_m = stack(output_weight, *n_out, *f_out)
            out_s = seq.send(to_core, out_m)
        else:
            info = lax.all_gather(own_info, "ctx", axis=1, tiled=True)
            x = order(x_raw)
            allowed, cos, sin = positions(info)
            packet4, out_m = whole(packet), whole(output_weight)
            packet_s, out_s = to_core(packet4), to_core(out_m)

        def pick(a):
            n = packet.shape[0]
            return (
                jnp.concatenate([a[i * n : i * n + blk] for i in range(plane)], 0),
                jnp.concatenate(
                    [a[i * n + blk : i * n + blk + 4, :blk] for i in range(plane)], 1
                ),
            )

        (qkv_m, gm), (qkv_s, gs) = pick(packet4), pick(packet_s)
        gain = wide(jnp.concatenate([gm, gs], axis=1))
        g1, g2, g3, g4 = [gain[i : i + 1] for i in range(4)]
        h1, q, kv = seq.run(qkv_kernel, x, g1, qkv_m, qkv_s, cos, sin, qw=qw)
        if square:
            kv_got = seq.send(to_ctx, kv)
            n_gb = near(gate_weight[:, half_w:])
            n_up = near(up_weight)
            kv_all = stack(kv, kv_got)
        else:
            kv_all = lax.all_gather(kv, "ctx", axis=0, tiled=True)
        length = kv_all.shape[0]

        def attend(sl):
            return seq.run(attn_kernel, q[sl], kv_all, allowed[sl], out_m, out_s)

        o_a, log_a, part_a = attend(ab[0])
        a_a = lax.psum(part_a, "tensor")
        o_b, log_b, part_b = attend(ab[1])
        ex = Exchange(part_b)
        if square:
            n_gate = [jnp.concatenate(p, 1) for p in zip(n_ga, n_gb)]
            n_gate = seq.run(lambda *v: v, *n_gate)
            f_gate = far(n_gate)
        ex.two()
        if square:
            f_up = far(n_up)
            n_down = near(down_weight)
            gate_m = stack(gate_weight, *n_gate, *f_gate)
        else:
            gate_m = whole(gate_weight)
        gate_s = seq.send(to_core, gate_m)
        ex.three()
        up_m = stack(up_weight, *n_up, *f_up) if square else whole(up_weight)
        up_s = seq.send(to_core, up_m)
        ex.four()
        dy = seq.run(order, dy_raw)
        fw = (g2, g3, gate_m, gate_s, up_m, up_s)
        x2_a, h3_a, gate_a, up_a, hid_a = seq.run(ffn_in_kernel, a_a, x[ab[0]], *fw)
        a_b = ex.end()
        if square:
            f_down = far(n_down)
        x2_b, h3_b, gate_b, up_b, hid_b = seq.run(ffn_in_kernel, a_b, x[ab[1]], *fw)
        down_m = stack(down_weight, *n_down, *f_down) if square else whole(down_weight)
        down_s = seq.send(to_core, down_m)
        fp_a = seq.run(project_kernel, hid_a, down_m, down_s)
        f_a = lax.psum(fp_a, "tensor")
        fp_b = seq.run(project_kernel, hid_b, down_m, down_s)
        ex = Exchange(fp_b)
        qkv_g = row_order(qkv_m, qkv_s)
        g1_g = order(jnp.concatenate([g1, g1], 0), back=True)[:1]
        both = lambda a, b: jnp.concatenate([a, b], 0)
        h3, hid, o = both(h3_a, h3_b), both(hid_a, hid_b), both(o_a, o_b)
        h3, hid, o = seq.run(lambda *v: v, h3, hid, o)
        ex.two()
        ex.three()
        ex.four()
        f_b = ex.end()

        bw = (down_m, down_s, gate_m, gate_s, up_m, up_s)
        y_a, df_a, dg_a, du_a, dg4_a, part_a = seq.run(
            ffn_back_kernel, f_a, x2_a, dy[ab[0]], g4, gate_a, up_a, *bw
        )
        dh3_a = lax.psum(part_a, "tensor")
        y_b, df_b, dg_b, du_b, dg4_b, part_b = seq.run(
            ffn_back_kernel, f_b, x2_b, dy[ab[1]], g4, gate_b, up_b, *bw
        )
        ex = Exchange(part_b)
        df, dgate, dup = both(df_a, df_b), both(dg_a, dg_b), both(du_a, du_b)
        df, dgate, dup = seq.run(lambda *v: v, df, dgate, dup)

        class Scatter:
            def __init__(self, a, b):
                self.ab = a, b
                low = seq.run(outer_kernel, a, b, start=mid, count=mid)
                self.got = seq.send(to_core, low)

            def first(self):
                s = seq.run(
                    outer_kernel, *self.ab, start=0, count=mid, add=self.got
                )
                self.s = s
                if square:
                    h = blk // 2
                    self.gx = seq.send(to_ctx, s[3 * blk : 3 * blk + h])
                    self.gy = seq.send(to_y, s[3 * blk + h :])

            def second(self):
                if not square:
                    self.rest = lax.psum_scatter(
                        self.s, ("y", "ctx"), scatter_dimension=0, tiled=True
                    )
                    return
                h = blk // 2

                def sums(s, gx, gy):
                    t1 = [s[blk : blk + h], wide(s[blk + h : 2 * blk]) + wide(gy)]
                    t2 = [wide(s[2 * blk : 2 * blk + h]) + wide(gx), s[2 * blk + h : 3 * blk]]
                    return [jnp.concatenate([v.astype(LOW) for v in t], 0) for t in (t1, t2)]

                t1, t2 = seq.run(sums, self.s, self.gx, self.gy)
                self.rest = seq.send(to_ctx, t1), seq.send(to_y, t2)

            def end(self):
                if not square:
                    return wide(self.rest)
                rx, ry = self.rest
                return wide(self.s[:blk]) + wide(rx) + wide(ry)

        sd = Scatter(df, hid)
        sg = Scatter(h3, dgate)
        ex.two()
        sd.first()
        su = Scatter(h3, dup)
        ex.three()
        sg.first()
        sd.second()
        ex.four()
        su.first()
        sg.second()
        layer_output = order(both(y_a, y_b), back=True)
        dh3_b = ex.end()

        def back(dh3, x2, sl, a, logs, before):
            return seq.run(
                attn_back_kernel, dh3, x2, dy[sl], a, g3, g2, out_m, out_s,
                q[sl], kv_all, allowed[sl], logs, cos[sl], sin[sl], before=before,
            )

        dx_a, da_a, dq_a, dkv, dg23 = back(dh3_a, x2_a, ab[0], a_a, log_a, None)
        dx_b, da_b, dq_b, dkv, dg23 = back(dh3_b, x2_b, ab[1], a_b, log_b, (dkv, dg23))
        if square:
            got = seq.send(to_ctx, dkv[toks:].astype(LOW))
            own = dkv[:toks]
        else:
            got = lax.psum_scatter(
                dkv.astype(LOW), "ctx", scatter_dimension=0, tiled=True
            )
            own = jnp.zeros((toks, 2 * kw), F32)
        da, dq = both(da_a, da_b), both(dq_a, dq_b)
        da, dq = seq.run(lambda *v: v, da, dq)
        so = Scatter(da, o)
        so.first()
        dkv_low = seq.run(keys_back_kernel, own, got, cos, sin)
        dqkv = jnp.concatenate([dq, dkv_low], axis=1)
        part = seq.run(project_kernel, dqkv, qkv_g[:mid], qkv_g[mid:])
        dh1 = lax.psum(part, "tensor")
        su.second()
        sq = Scatter(h1, dqkv)
        so.second()
        sq.first()
        dx2 = seq.run(lambda v: order(v, back=True), both(dx_a, dx_b))
        sq.second()
        down_grad, gate_grad, up_grad = sd.end(), sg.end(), su.end()
        out_grad, qkv_grad = so.end(), sq.end()
        input_grad, dg1 = last_kernel(x_raw, g1_g, dh1, dx2)
        dg1 = order(jnp.concatenate([dg1, dg1], 0))[:1]
        dgain = jnp.concatenate([dg1, dg23[:2], dg4_a + dg4_b], axis=0)
        dgain = dgain[:, :mid] + to_core(dgain[:, mid:])
        if square:
            s = dgain[:, : mid // 2] + to_y(dgain[:, mid // 2 :])
            dgain = s[:, :blk] + to_ctx(s[:, blk:])
        else:
            dgain = lax.psum_scatter(
                dgain, ("y", "ctx"), scatter_dimension=1, tiled=True
            )
        return (
            layer_output.reshape(rows, toks, width),
            input_grad.reshape(rows, toks, width),
            qkv_grad[:, :qw],
            qkv_grad[:, qw : qw + kw],
            qkv_grad[:, qw + kw :],
            out_grad,
            gate_grad,
            up_grad,
            down_grad,
            dgain[0],
            dgain[1],
            dgain[2],
            dgain[3],
        )

    return local


def solution(mesh):
    dp, nx, nz = (mesh.shape[a] for a in ("dp", "ctx", "tensor"))
    fine = Mesh(
        mesh.devices.reshape(dp // 2, 2, nx, nz), ("y", "core", "ctx", "tensor")
    )
    d = ("y", "core")
    w = P(("y", "core", "ctx"), "tensor")
    g = P(("y", "core", "ctx"))
    t = P(d, "ctx", None)
    return jax.shard_map(
        make_local(dp // 2, nx, nz),
        mesh=fine,
        in_specs=(t, w, w, w, w, w, w, w, g, g, g, g, t, P(d, "ctx"), P(d, "ctx")),
        out_specs=(t, t, w, w, w, w, w, w, w, g, g, g, g),
        check_vma=False,
    )
```

```python
import math

import jax
import jax.numpy as jnp
from jax import lax
from jax.experimental import pallas as pl
from jax.experimental.pallas import tpu as pltpu
from jax.sharding import Mesh
from jax.sharding import PartitionSpec as P

HD = 256
NORM_EPSILON = 1e-06
SOFT_CAP = 50.0
MASKED_SCORE = -1e30
SWAP = [(0, 1), (1, 0)]
LOW = jnp.bfloat16
F32 = jnp.float32
VMEM_MB = 56
NO_COST = pl.CostEstimate(flops=0, bytes_accessed=0, transcendentals=0)
LONG = pl.CostEstimate(flops=10**12, bytes_accessed=0, transcendentals=0)


def wide(a):
    return a.astype(F32)


def after(value, *deps):
    return lax.optimization_barrier((value,) + deps)[0]


class Order:
    def __init__(self):
        self.last = ()

    def __call__(self, *values):
        return after(values, *self.last) if self.last else values

    def run(self, fn, *values, **kw):
        out = fn(*self(*values), **kw)
        self.last = (out,)
        return out

    def send(self, move, value):
        (value,) = self(value)
        self.last = (value,)
        return move(value)


def to_ctx(a):
    return lax.ppermute(a, "ctx", SWAP)


def to_y(a):
    return lax.ppermute(a, "y", SWAP)


def to_core(a):
    return lax.ppermute(a, "core", SWAP)


def nn(a, b):
    return jnp.dot(a, b, preferred_element_type=F32)


def nt(a, b):
    return lax.dot_general(a, b, (((1,), (1,)), ((), ())), preferred_element_type=F32)


def tn(a, b):
    return lax.dot_general(a, b, (((0,), (0,)), ((), ())), preferred_element_type=F32)


def norm_factor(v):
    return lax.rsqrt(jnp.mean(v * v, axis=-1, keepdims=True) + NORM_EPSILON)


def over_rows(rows, step, carry=None, block=64):
    block = math.gcd(rows, block)
    at = lambda i: pl.ds(pl.multiple_of(i * block, block), block)
    return lax.fori_loop(0, rows // block, lambda i, c: step(at(i), c), carry)


def fold(v):
    return sum(v[i : i + 8] for i in range(0, v.shape[0], 8))


def norm_back_rows(v, gain, grad):
    r = norm_factor(v)
    w = (1.0 + gain) * grad
    vr = v * r
    dv = r * (w - vr * jnp.mean(vr * w, axis=-1, keepdims=True))
    return dv, fold(grad * vr)


def gelu_parts(u):
    k = math.sqrt(2.0 / math.pi)
    th = jnp.tanh(k * (u + 0.044715 * u * u * u))
    g = 0.5 * u * (1.0 + th)
    dg = 0.5 * (1.0 + th) + 0.5 * u * (1.0 - th * th) * k * (1.0 + 3 * 0.044715 * u * u)
    return g, dg


def turn(v, c, s):
    h = HD // 2
    a, b = v[:, :h], v[:, h:]
    return jnp.concatenate([a * c - b * s, b * c + a * s], axis=1)


def turn_back(v, c, s):
    h = HD // 2
    a, b = v[:, :h], v[:, h:]
    return jnp.concatenate([a * c + b * s, b * c - a * s], axis=1)


def spec(block, index, mode=None):
    return pl.BlockSpec(block, index, pipeline_mode=mode)


def kernel(body, grid, ins, outs, scratch=(), cost=NO_COST):
    return pl.pallas_call(
        body,
        grid=grid,
        in_specs=[spec(*e[1:]) for e in ins],
        out_specs=[spec(*e[2:]) for e in outs],
        out_shape=[jax.ShapeDtypeStruct(*e[:2]) for e in outs],
        scratch_shapes=list(scratch),
        cost_estimate=cost,
        compiler_params=pltpu.CompilerParams(vmem_limit_bytes=VMEM_MB * 2**20),
    )(*[e[0] for e in ins])


def all_of(shape):
    return tuple(shape), lambda *i: (0,) * len(shape), pl.Buffered(1)


def stack_kernel(*pieces, outs, plan, cost=NO_COST):
    sets, n = len(plan), len(pieces)
    widths = [pieces[p[0][0]].shape[1] for p in plan]
    bc = math.gcd(*widths, 768)
    first = [sum(widths[:i]) // bc for i in range(sets + 1)]

    def body(*refs):
        for i, copies in enumerate(plan):

            @pl.when((pl.program_id(0) >= first[i]) & (pl.program_id(0) < first[i + 1]))
            def _(copies=copies):
                for p, o, r0, r, at in copies:
                    refs[n + o][at : at + r, :] = refs[p][r0 : r0 + r, :]

    ins = []
    for i, copies in enumerate(plan):
        lo, count = first[i], first[i + 1] - first[i]
        for p in sorted({e[0] for e in copies}):
            tile = (pieces[p].shape[0], bc)
            ins.append((p, tile, lambda j, lo=lo, c=count: (0, jnp.clip(j - lo, 0, c - 1))))
    ins = [(pieces[p], t, m) for p, t, m in sorted(ins, key=lambda e: e[0])]
    tile = lambda r: ((r, bc), lambda j: (0, j))
    outs = [((r, sum(widths)), LOW, *tile(r)) for r in outs]
    return kernel(body, (first[-1],), ins, outs, cost=cost)


def first_kernel(x, r, cos, sin, *pieces, plan, blk, qw, kw):
    toks, width = x.shape
    wide_w = pieces[0].shape[1]
    cols = qw + 2 * kw
    devices = width // blk
    lanes = -(-blk // 128) * 128
    scale = 1.0 / math.sqrt(HD)
    n = len(pieces)

    def body(x_r, r_r, c_r, s_r, *refs):
        piece_h = refs[:n]
        h_h, q_r, kv_r, g_r, w_h, o_h = refs[n : n + 6]
        h_r, w_r, raw_g_r, sems = refs[n + 6 :]
        c = Copies(sems)
        for k, (p, r0, rows, at, gain_at) in enumerate(plan):
            if at is None:
                src = piece_h[p].at[pl.ds(r0, rows), pl.ds(0, lanes)]
                c.start(("g", k), src, raw_g_r.at[pl.ds(gain_at, rows)])
        for k, (p, r0, rows, at, gain_at) in enumerate(plan):
            if at is not None:
                c.start(("w", k), piece_h[p].at[pl.ds(r0, rows)], w_r.at[pl.ds(at, rows)])
        c.wait(*[k for k in c.known if k[0] == "g"])
        rows16 = raw_g_r[...]
        gains = [rows16[d * 16 : d * 16 + 8, :blk] for d in range(devices)]
        gains = wide(jnp.concatenate(gains, axis=1))
        g_r[...] = gains
        g1 = 1.0 + gains[0:1]

        def normed(at, _):
            h_r[at, :] = (wide(x_r[at, :]) * r_r[at, 0:1] * g1).astype(LOW)

        over_rows(toks, normed)
        c.start("h", h_r, h_h)
        c.wait(*[k for k in c.known if k[0] == "w"])
        c.start("qkv", w_r.at[:, pl.ds(0, cols)], w_h)
        c.start("out", w_r.at[:, pl.ds(cols, wide_w - cols)], o_h)
        raw = nn(h_r[...], w_r[:, :cols])
        co, si = c_r[...], s_r[...]
        for j in range(qw // HD):
            cut = slice(j * HD, (j + 1) * HD)
            q_r[:, cut] = (turn(raw[:, cut], co, si) * scale).astype(LOW)
        for j in range(kw // HD):
            cut = slice(j * HD, (j + 1) * HD)
            k = turn(raw[:, qw + j * HD : qw + (j + 1) * HD], co, si)
            kv_r[:, cut] = k.astype(LOW)
        kv_r[:, kw:] = raw[:, qw + kw :].astype(LOW)
        c.wait("h", "qkv", "out")

    ins = [(v, "vmem") for v in (x, r, cos, sin)] + [(p, "hbm") for p in pieces]
    outs = [
        ((toks, width), LOW, "hbm"),
        ((toks, qw), LOW, "vmem"),
        ((toks, 2 * kw), LOW, "vmem"),
        ((8, width), F32, "vmem"),
        ((width, cols), LOW, "hbm"),
        ((width, wide_w - cols), LOW, "hbm"),
    ]
    scratch = [((toks, width), LOW), ((width, wide_w), LOW), ((16 * devices, lanes), LOW)]
    return streaming(body, ins, outs, scratch, len(plan) + 3, LONG)


def query_block(rows, length):
    return min(rows, 256 if length <= 2048 else 128)


def attn_kernel(q, kv, allowed, w):
    rows, qw = q.shape
    length = kv.shape[0]
    width = w.shape[0]
    qb = query_block(rows, length)
    heads = qw // HD

    def body(q_r, kv_r, m_r, w_r, o_r, t_r, a_r):
        ok = m_r[...] > 0
        k, v = kv_r[:, :HD], kv_r[:, HD:]
        logs = []
        for j in range(heads):
            cut = slice(j * HD, (j + 1) * HD)
            b = jnp.tanh(nt(q_r[:, cut], k) * (1.0 / SOFT_CAP))
            c = jnp.where(ok, SOFT_CAP * b, MASKED_SCORE)
            peak = jnp.max(c, axis=-1, keepdims=True)
            e = jnp.exp(c - peak)
            total = jnp.sum(e, axis=-1, keepdims=True)
            p = (e / total).astype(LOW)
            o_r[:, cut] = nn(p, v).astype(LOW)
            logs.append(jnp.broadcast_to(peak + jnp.log(total), (qb, 128)))
        t_r[...] = jnp.concatenate(logs, axis=1)
        a_r[...] = nt(o_r[...], w_r[...]).astype(LOW)

    row = lambda n: ((qb, n), lambda i: (i, 0))
    ins = [(q, *row(qw)), (kv, *all_of(kv.shape)), (allowed, *row(length))]
    ins += [(w, *all_of(w.shape))]
    outs = [
        ((rows, qw), LOW, *row(qw)),
        ((rows, 128 * heads), F32, *row(128 * heads)),
        ((rows, width), LOW, *row(width)),
    ]
    return kernel(body, (rows // qb,), ins, outs)


def attn_back_kernel(
    dh3, x2, dy, a, g3, g2, w, q, kv, allowed, logs, cos, sin
):
    rows, width = x2.shape
    qw = q.shape[1]
    length = kv.shape[0]
    qb = query_block(rows, length)
    heads = qw // HD
    scale = 1.0 / math.sqrt(HD)

    def body(
        d_r, x_r, dy_r, a_r, g3_r, g2_r, w_r, q_r, kv_r, m_r, t_r, c_r, s_r,
        dx_r, da_r, dq_r, dkv_r, dg_r,
    ):
        @pl.when(pl.program_id(0) == 0)
        def _():
            dkv_r[...] = jnp.zeros_like(dkv_r)
            dg_r[...] = jnp.zeros_like(dg_r)

        def step(at, total):
            dv3, dg3 = norm_back_rows(x_r[at, :], g3_r[...], wide(d_r[at, :]))
            dx2 = wide(dy_r[at, :]) + dv3
            dx_r[at, :] = dx2
            da, dg2 = norm_back_rows(wide(a_r[at, :]), g2_r[...], dx2)
            da_r[at, :] = da.astype(LOW)
            return total[0] + dg2, total[1] + dg3

        none = jnp.zeros((8, width), F32)
        dg2, dg3 = over_rows(qb, step, (none, none))
        dg_r[0:1] += jnp.sum(dg2, axis=0, keepdims=True)
        dg_r[1:2] += jnp.sum(dg3, axis=0, keepdims=True)
        do = nn(da_r[...], w_r[...]).astype(LOW)
        ok = m_r[...] > 0
        k, v = kv_r[:, :HD], kv_r[:, HD:]
        c, s = c_r[...], s_r[...]
        dk = dv = 0.0
        for j in range(heads):
            cut = slice(j * HD, (j + 1) * HD)
            qj, doj = q_r[:, cut], do[:, cut]
            b = jnp.tanh(nt(qj, k) * (1.0 / SOFT_CAP))
            logit = jnp.where(ok, SOFT_CAP * b, MASKED_SCORE)
            p = jnp.exp(logit - t_r[:, j * 128 : j * 128 + 1])
            dp = nt(doj, v)
            dc = p * (dp - jnp.sum(p * dp, axis=-1, keepdims=True))
            ds = (dc * (1.0 - b * b)).astype(LOW)
            dq_r[:, cut] = (turn_back(nn(ds, k), c, s) * scale).astype(LOW)
            dk = dk + tn(ds, qj)
            dv = dv + tn(p.astype(LOW), doj)
        dkv_r[:, :HD] += dk
        dkv_r[:, HD:] += dv

    row = lambda n: ((qb, n), lambda i: (i, 0))
    ins = [(v, *row(width)) for v in (dh3, x2, dy, a)]
    ins += [(v, *all_of(v.shape)) for v in (g3, g2, w)]
    ins += [(q, *row(qw)), (kv, *all_of(kv.shape)), (allowed, *row(length))]
    ins += [(logs, *row(128 * heads)), (cos, *row(HD // 2)), (sin, *row(HD // 2))]
    outs = [
        ((rows, width), F32, *row(width)),
        ((rows, width), LOW, *row(width)),
        ((rows, qw), LOW, *row(qw)),
        ((length, 2 * HD), F32, *all_of((length, 2 * HD))),
        ((8, width), F32, *all_of((8, width))),
    ]
    return kernel(body, (rows // qb,), ins, outs, cost=LONG)


class Copies:
    def __init__(self, sems):
        self.sems, self.known = sems, {}

    def start(self, name, src, dst):
        self.known[name] = pltpu.make_async_copy(src, dst, self.sems.at[len(self.known)])
        self.known[name].start()

    def wait(self, *names):
        for name in names:
            self.known[name].wait()


def streaming(body, ins, outs, scratch, copies, cost=NO_COST):
    place = {"vmem": pl.BlockSpec(memory_space=pltpu.VMEM), "hbm": pl.BlockSpec(memory_space=pl.ANY)}
    return pl.pallas_call(
        body,
        in_specs=[place[p] for _, p in ins],
        out_specs=[place[p] for _, _, p in outs],
        out_shape=[jax.ShapeDtypeStruct(s, d) for s, d, _ in outs],
        scratch_shapes=[pltpu.VMEM(*v) for v in scratch]
        + [pltpu.SemaphoreType.DMA((copies,))],
        cost_estimate=cost,
        compiler_params=pltpu.CompilerParams(vmem_limit_bytes=VMEM_MB * 2**20),
    )(*[a for a, _ in ins])


def row_parts(rows, block=128):
    return [pl.ds(i, min(block, rows)) for i in range(0, rows, min(block, rows))]


def row_tiles(mid, tile=384):
    t = math.gcd(mid, tile)
    tiles = [(k, i, k * mid + i, t) for k in range(2) for i in range(0, mid, t)]
    return [tiles[i : i + 2] for i in range(0, len(tiles), 2)]


def ffn_in_kernel(a, x, g2, g3, gm, gs, um, us):
    rows, width = x.shape
    mid, units = um.shape
    bn = math.gcd(units, 768)
    parts, cols = row_parts(rows), [pl.ds(i, bn) for i in range(0, units, bn)]

    def body(
        a_h, x_h, g2_r, g3_r, gm_h, gs_h, um_h, us_h,
        x2_h, h_h, g_h, u_h, hid_h,
        a_r, x_r, x2_r, h_r, wg_r, wu_r, g_r, u_r, hid_r, sems,
    ):
        c = Copies(sems)
        for i, at in enumerate(parts):
            c.start(("a", i), a_h.at[at], a_r.at[at])
            c.start(("x", i), x_h.at[at], x_r.at[at])
        for j, at in enumerate(cols):
            for name, m, s, w in (("g", gm_h, gs_h, wg_r), ("u", um_h, us_h, wu_r)):
                c.start((name, "m", j), m.at[:, at], w.at[pl.ds(0, mid), at])
                c.start((name, "s", j), s.at[:, at], w.at[pl.ds(mid, mid), at])
        out = []

        def send(src, dst, at):
            out.append(len(out))
            c.start(("out", out[-1]), src.at[at], dst.at[at])

        for i, part in enumerate(parts):
            c.wait(("a", i), ("x", i))

            def normed(at, _, first=part.start):
                at = pl.ds(pl.multiple_of(first + at.start, 16), at.size)
                av = wide(a_r[at, :])
                x2 = wide(x_r[at, :]) + av * norm_factor(av) * (1.0 + g2_r[...])
                x2_r[at, :] = x2
                h_r[at, :] = (x2 * norm_factor(x2) * (1.0 + g3_r[...])).astype(LOW)

            over_rows(part.size, normed)
            send(x2_r, x2_h, (part,))
            send(h_r, h_h, (part,))
        for j, at in enumerate(cols):
            c.wait(("g", "m", j), ("g", "s", j), ("u", "m", j), ("u", "s", j))
            h = h_r[...]
            gate, up = nn(h, wg_r[:, at]), nn(h, wu_r[:, at])
            g_r[:, at] = gate.astype(LOW)
            u_r[:, at] = up.astype(LOW)
            hid_r[:, at] = (gelu_parts(gate)[0] * up).astype(LOW)
            for src, dst in ((g_r, g_h), (u_r, u_h), (hid_r, hid_h)):
                send(src, dst, (slice(None), at))
        c.wait(*[("out", i) for i in out])

    t, n = (rows, width), (rows, units)
    ins = [(a, "hbm"), (x, "hbm"), (g2, "vmem"), (g3, "vmem")]
    ins += [(w, "hbm") for w in (gm, gs, um, us)]
    outs = [(t, F32, "hbm"), (t, LOW, "hbm"), (n, LOW, "hbm"), (n, LOW, "hbm"), (n, LOW, "hbm")]
    w = (2 * mid, units)
    scratch = [(t, LOW), (t, LOW), (t, F32), (t, LOW), (w, LOW), (w, LOW)]
    scratch += [(n, LOW)] * 3
    return streaming(body, ins, outs, scratch, 4 * len(parts) + 7 * len(cols))


def project_kernel(u, wm, ws):
    rows, cols = u.shape
    mid = wm.shape[0]
    groups = row_tiles(mid)

    def body(u_r, m_h, s_h, o_h, w_r, o_r, sems):
        c = Copies(sems)
        for g, tiles in enumerate(groups):
            for k, i, at, n in tiles:
                src = (m_h, s_h)[k].at[pl.ds(i, n)]
                c.start((g, at), src, w_r.at[pl.ds(at, n)])
        for g, tiles in enumerate(groups):
            c.wait(*[(g, t[2]) for t in tiles])
            at = pl.ds(tiles[0][2], sum(t[3] for t in tiles))
            o_r[:, at] = nt(u_r[...], w_r[at, :]).astype(LOW)
            c.start(("out", g), o_r.at[:, at], o_h.at[:, at])
        c.wait(*[("out", g) for g in range(len(groups))])

    ins = [(u, "vmem"), (wm, "hbm"), (ws, "hbm")]
    outs = [((rows, 2 * mid), LOW, "hbm")]
    scratch = [((2 * mid, cols), LOW), ((rows, 2 * mid), LOW)]
    n = sum(map(len, groups)) + len(groups)
    return streaming(body, ins, outs, scratch, n)[0]


def ffn_back_kernel(f, x2, dy, g4, gate, up, dm, ds):
    rows, width = x2.shape
    mid, units = dm.shape
    bn = math.gcd(units, 768)
    parts, cols = row_parts(rows), [pl.ds(i, bn) for i in range(0, units, bn)]

    def body(
        f_h, x2_h, dy_h, g4_r, gate_h, up_h, dm_h, ds_h,
        y_h, df_h, dg_h, du_h, g_r,
        f_r, x2_r, dy_r, gate_r, up_r, w_r, y_r, df_r, dg_r, du_r, sems,
    ):
        c = Copies(sems)
        for i, at in enumerate(parts):
            for name, src, dst in (("f", f_h, f_r), ("x", x2_h, x2_r), ("d", dy_h, dy_r)):
                c.start((name, i), src.at[at], dst.at[at])
        for j, at in enumerate(cols):
            c.start(("m", j), dm_h.at[:, at], w_r.at[pl.ds(0, mid), at])
            c.start(("s", j), ds_h.at[:, at], w_r.at[pl.ds(mid, mid), at])
            c.start(("gate", j), gate_h.at[:, at], gate_r.at[:, at])
            c.start(("up", j), up_h.at[:, at], up_r.at[:, at])
        out = []

        def send(src, dst, at):
            out.append(len(out))
            c.start(("out", out[-1]), src.at[at], dst.at[at])

        total = jnp.zeros((8, width), F32)
        for i, part in enumerate(parts):
            c.wait(("f", i), ("x", i), ("d", i))

            def step(at, total, first=part.start):
                at = pl.ds(pl.multiple_of(first + at.start, 16), at.size)
                fv, g4v, x2v = wide(f_r[at, :]), g4_r[...], x2_r[at, :]
                y_r[at, :] = (x2v + fv * norm_factor(fv) * (1.0 + g4v)).astype(LOW)
                df, dg = norm_back_rows(fv, g4v, wide(dy_r[at, :]))
                df_r[at, :] = df.astype(LOW)
                return total + dg

            total = over_rows(part.size, step, total)
            send(y_r, y_h, (part,))
            send(df_r, df_h, (part,))
        g_r[...] = jnp.sum(total, axis=0, keepdims=True)
        for j, at in enumerate(cols):
            c.wait(("m", j), ("s", j), ("gate", j), ("up", j))
            dh = nn(df_r[...], w_r[:, at])
            gl, dgl = gelu_parts(wide(gate_r[:, at]))
            dg_r[:, at] = (dh * wide(up_r[:, at]) * dgl).astype(LOW)
            du_r[:, at] = (dh * gl).astype(LOW)
            send(dg_r, dg_h, (slice(None), at))
            send(du_r, du_h, (slice(None), at))
        c.wait(*[("out", i) for i in out])

    t, n = (rows, width), (rows, units)
    ins = [(v, "hbm") for v in (f, x2, dy)] + [(g4, "vmem")]
    ins += [(v, "hbm") for v in (gate, up, dm, ds)]
    outs = [(t, LOW, "hbm"), (t, LOW, "hbm"), (n, LOW, "hbm"), (n, LOW, "hbm")]
    outs += [((1, width), F32, "vmem")]
    scratch = [(t, LOW), (t, F32), (t, LOW), (n, LOW), (n, LOW), ((2 * mid, units), LOW)]
    scratch += [(t, LOW), (t, LOW), (n, LOW), (n, LOW)]
    return streaming(body, ins, outs, scratch, 5 * len(parts) + 6 * len(cols))


def ffn_inputs_kernel(dg, du, gm, gs, um, us):
    rows, units = dg.shape
    mid = um.shape[0]
    groups = row_tiles(mid)

    def body(dg_r, du_r, gm_h, gs_h, um_h, us_h, o_h, wg_r, wu_r, o_r, sems):
        c = Copies(sems)
        for g, tiles in enumerate(groups):
            for k, i, at, n in tiles:
                for name, src, dst in (("g", (gm_h, gs_h), wg_r), ("u", (um_h, us_h), wu_r)):
                    c.start((name, g, at), src[k].at[pl.ds(i, n)], dst.at[pl.ds(at, n)])
        for g, tiles in enumerate(groups):
            c.wait(*[(name, g, t[2]) for t in tiles for name in "gu"])
            at = pl.ds(tiles[0][2], sum(t[3] for t in tiles))
            v = nt(dg_r[...], wg_r[at, :]) + nt(du_r[...], wu_r[at, :])
            o_r[:, at] = v.astype(LOW)
            c.start(("out", g), o_r.at[:, at], o_h.at[:, at])
        c.wait(*[("out", g) for g in range(len(groups))])

    ins = [(dg, "vmem"), (du, "vmem")] + [(w, "hbm") for w in (gm, gs, um, us)]
    outs = [((rows, 2 * mid), LOW, "hbm")]
    w = ((2 * mid, units), LOW)
    n = 2 * sum(map(len, groups)) + len(groups)
    return streaming(body, ins, outs, [w, w, ((rows, 2 * mid), LOW)], n)[0]


def outer_kernel(a, b, *got, side, cuts, cost=NO_COST):
    toks, cols = b.shape
    mid = a.shape[1] // 2
    bn = math.gcd(cols, 768)
    chunks = [pl.ds(i, bn) for i in range(0, cols, bn)]
    n, m = len(got), len(cuts)
    at = [sum(cuts[:i]) for i in range(m)]
    step = mid // n if n else 0

    def body(a_h, b_h, *refs):
        got_h, out_h = refs[:n], refs[n : n + m]
        a_r, b_r, got_r, out_r, sems = refs[n + m :]
        c = Copies(sems)
        c.start("a", a_h.at[:, pl.ds(side * mid, mid)], a_r)
        for j, part in enumerate(chunks):
            c.start(("b", j), b_h.at[:, part], b_r.at[:, part])
        for i in range(n):
            c.start(("got", i), got_h[i], got_r.at[pl.ds(i * step, step)])
        c.wait("a")
        for j, part in enumerate(chunks):
            c.wait(("b", j))
            v = tn(a_r[...], b_r[:, part])
            if n:
                if j == 0:
                    c.wait(*[("got", i) for i in range(n)])
                v = v + wide(got_r[:, part])
            out_r[:, part] = v.astype(LOW)
            for i in range(m):
                c.start(
                    ("out", i, j),
                    out_r.at[pl.ds(at[i], cuts[i]), part],
                    out_h[i].at[:, part],
                )
        c.wait(*[("out", i, j) for i in range(m) for j in range(len(chunks))])

    ins = [(v, "hbm") for v in (a, b, *got)]
    outs = [((r, cols), LOW, "hbm") for r in cuts]
    full = (mid, cols)
    scratch = [((toks, mid), LOW), ((toks, cols), LOW)]
    scratch += [(full if n else (16, 128), LOW), (full, LOW)]
    copies = 1 + len(chunks) * (1 + m) + n
    return streaming(body, ins, outs, scratch, copies, cost)


def sum_kernel(s, ra, rb, qa, qb):
    rows, cols = s.shape
    h = ra.shape[0]
    bc = math.gcd(cols, 768)

    def body(s_r, ra_r, rb_r, qa_r, qb_r, o_r):
        o_r[:h] = wide(s_r[:h]) + wide(ra_r[...]) + wide(qa_r[...])
        o_r[h:] = wide(s_r[h:]) + wide(rb_r[...]) + wide(qb_r[...])

    tile = lambda r: ((r, bc), lambda j: (0, j))
    ins = [(v, *tile(v.shape[0])) for v in (s, ra, rb, qa, qb)]
    return kernel(body, (cols // bc,), ins, [((rows, cols), F32, *tile(rows))])[0]


def add_kernel(a, b):
    rows, cols = a.shape
    bc = math.gcd(cols, 1152)

    def body(a_r, b_r, o_r):
        o_r[...] = (wide(a_r[...]) + wide(b_r[...])).astype(LOW)

    tile = ((rows, bc), lambda j: (0, j))
    return kernel(body, (cols // bc,), [(a, *tile), (b, *tile)], [(a.shape, LOW, *tile)])[0]


def last_kernel(x, gain, dh1, dx2):
    rows, width = x.shape
    br = min(rows, 128)

    def body(x_r, g_r, d_r, dx_r, o_r, dg_r):
        def step(at, total):
            dv, dg = norm_back_rows(wide(x_r[at, :]), g_r[...], wide(d_r[at, :]))
            o_r[at, :] = dx_r[at, :] + dv
            return total + dg

        @pl.when(pl.program_id(0) == 0)
        def _():
            dg_r[...] = jnp.zeros_like(dg_r)

        total = over_rows(br, step, jnp.zeros((8, width), F32))
        dg_r[...] += jnp.sum(total, axis=0, keepdims=True)

    row = ((br, width), lambda i: (i, 0))
    ins = [(x, *row), (gain, *all_of(gain.shape)), (dh1, *row), (dx2, *row)]
    outs = [((rows, width), F32, *row), ((1, width), F32, *all_of((1, width)))]
    return kernel(body, (rows // br,), ins, outs)


def order_kernel(v, bits, back, ny, nx, factors=False):
    rows, width = v.shape
    blk = width // (2 * ny * nx)
    br = min(rows, 128)
    here = lambda c, y, x: (c * ny + y) * nx + x
    there = lambda c, y, x: (y * 2 + c) * nx + x
    keys = [(c, y, x) for c in range(2) for y in range(ny) for x in range(nx)]
    src, dst = (here, there) if back else (there, here)
    flips = 3 if ny == 2 and nx == 2 else 1

    def body(b_r, v_r, o_r, *f_r):
        def step(at, _):
            rows_ = v_r[at, :]
            if factors:
                f = norm_factor(wide(rows_))
                f_r[0][at, :] = jnp.broadcast_to(f, (f.shape[0], 128))
            cut = lambda j: rows_[:, j * blk : (j + 1) * blk]
            parts = {k: cut(src(*k)) for k in keys}
            for pos in range(flips):
                on = b_r[pos] == 0
                flip = lambda k: tuple(1 - e if i == pos else e for i, e in enumerate(k))
                parts = {k: jnp.where(on, parts[k], parts[flip(k)]) for k in keys}
            o_r[at, :] = jnp.concatenate([parts[k] for k in sorted(keys, key=lambda k: dst(*k))], axis=1)

        over_rows(br, step)

    tile = pl.BlockSpec((br, width), lambda i: (i, 0))
    return pl.pallas_call(
        body,
        grid=(rows // br,),
        in_specs=[pl.BlockSpec(memory_space=pltpu.SMEM), tile],
        out_specs=[tile, pl.BlockSpec((br, 128), lambda i: (i, 0))][: 1 + factors],
        out_shape=[
            jax.ShapeDtypeStruct(v.shape, v.dtype),
            jax.ShapeDtypeStruct((rows, 128), F32),
        ][: 1 + factors],
        cost_estimate=NO_COST,
    )(bits, v)


def keys_back_kernel(own, got, cos, sin):
    def body(a_r, b_r, c_r, s_r, o_r):
        v = a_r[...] + wide(b_r[...])
        o_r[:, :HD] = turn_back(v[:, :HD], c_r[...], s_r[...]).astype(LOW)
        o_r[:, HD:] = v[:, HD:].astype(LOW)

    ins = [(v, *all_of(v.shape)) for v in (own, got, cos, sin)]
    return kernel(body, (1,), ins, [(own.shape, LOW, *all_of(own.shape))])[0]


def make_local(ny, nx, nz):
    square = ny == 2 and nx == 2
    plane = ny * nx

    def order(v, back=False, factors=False):
        bits = jnp.stack([lax.axis_index(a) for a in ("core", "y", "ctx")])
        out = order_kernel(v, bits.astype(jnp.int32), back, ny, nx, factors)
        return out if factors else out[0]

    def row_order(w):
        blk = w.shape[0] // (2 * plane)
        c = lax.axis_index("core")
        out = jnp.zeros_like(w)
        for half in range(2):
            for y in range(ny):
                for x in range(nx):
                    i = (half * ny + y) * nx + x
                    gy, gx = y, x
                    if square:
                        gy, gx = y ^ lax.axis_index("y"), x ^ lax.axis_index("ctx")
                    at = ((gy * 2 + (c ^ half)) * nx + gx) * blk
                    piece = lax.slice_in_dim(w, i * blk, (i + 1) * blk, axis=0)
                    out = lax.dynamic_update_slice_in_dim(out, piece, at, 0)
        return out

    def local(
        layer_input,
        query_weight,
        key_weight,
        value_weight,
        output_weight,
        gate_weight,
        up_weight,
        down_weight,
        attn_in_gain,
        attn_out_gain,
        ffn_in_gain,
        ffn_out_gain,
        out_cotangent,
        segment_ids,
        live_mask,
    ):
        rows, toks, width = layer_input.shape
        blk, qw = query_weight.shape
        kw = key_weight.shape[1]
        qkv_w = qw + 2 * kw
        mid = width // 2
        seq = Order()

        class ZSum:
            def __init__(self, part):
                self.own = lax.psum_scatter(
                    part, "tensor", scatter_dimension=0, tiled=True
                )

            def middle(self):
                (own,) = seq(self.own)
                seq.last = (own,)
                self.out = lax.all_gather(own, "tensor", axis=0, tiled=True)

        class Weight:
            def __init__(self, w):
                self.w = w
                if not square:
                    m = lax.all_gather(w, ("y", "ctx"), axis=0, tiled=True)
                    self.mine, self.other = [m], [to_core(m)]

            def near(self):
                if square:
                    w = self.w
                    self.mine = [w, seq.send(to_ctx, w), seq.send(to_y, w)]
                    self.other = [seq.send(to_core, w)]

            def far(self):
                if square:
                    h = blk // 2
                    wx, wy = seq(*self.mine[1:])
                    self.mine += [seq.send(to_y, wx[:h]), seq.send(to_ctx, wy[h:])]
                    self.other += [seq.send(to_core, wx), seq.send(to_core, wy)]

            def core(self):
                if square:
                    self.mine[3:] = seq(*self.mine[3:])
                    self.other += [seq.send(to_core, d) for d in self.mine[3:]]

        def stack(*weights, cost=NO_COST):
            pieces, plans = [], []
            for weight in weights:
                plan = []
                for o, side in enumerate((weight.mine, weight.other)):
                    at = 0
                    for p in side:
                        plan.append((len(pieces), o, 0, p.shape[0], at))
                        at += p.shape[0]
                        pieces.append(p)
                plans.append(plan)
            return seq.run(
                stack_kernel, *pieces, outs=[plane * blk] * 2, plan=plans, cost=cost
            )

        def packet_plan():
            pieces, plan, full, device = [], [], packet.w.shape[0], 0
            for side in (packet.mine, packet.other):
                at = 0
                for p in side:
                    i, r = 0, p.shape[0]
                    while i < r:
                        d, inside = divmod(at + i, full)
                        d += device
                        if inside < blk:
                            k = min(r - i, blk - inside)
                            plan.append((len(pieces), i, k, d * blk + inside, None))
                        else:
                            k = min(r - i, full - inside)
                            plan.append((len(pieces), i, k, None, d * 16))
                        i += k
                    at += r
                    pieces.append(p)
                device += plane
            return pieces, plan

        gains = jnp.stack([attn_in_gain, attn_out_gain, ffn_in_gain, ffn_out_gain])
        own = [query_weight, key_weight, value_weight, output_weight]
        own = jnp.concatenate(own, axis=1)
        gains = jnp.pad(gains, ((0, 12), (0, own.shape[1] - blk)))
        packet = Weight(jnp.concatenate([own, gains], axis=0))
        index = lax.axis_index("ctx") * toks + jnp.arange(toks, dtype=jnp.int32)
        own_info = jnp.concatenate([segment_ids, live_mask, index[None]], axis=0)

        def positions(info):
            seg_all, live_all, index_all = info[0:1], info[1:2], info[2:3]
            seg_col, index_col = segment_ids.reshape(toks, 1), index.reshape(toks, 1)
            start = jnp.sum((seg_all < seg_col).astype(jnp.int32), axis=1)
            allowed = (
                (index_all <= index_col)
                & (seg_all == seg_col)
                & ((live_all == 1) | (index_all == index_col))
            ).astype(LOW)
            freq = jnp.exp(
                jnp.arange(HD // 2, dtype=F32) * (-2.0 * math.log(10000.0) / HD)
            )
            angle = wide(index - start)[:, None] * freq
            return allowed, jnp.cos(angle), jnp.sin(angle)

        x_raw = layer_input.reshape(toks, width)
        dy_raw = out_cotangent.reshape(toks, width)
        half_w = gate_weight.shape[1] * 4 // 9 // 128 * 128
        wga, wgb = Weight(gate_weight[:, :half_w]), Weight(gate_weight[:, half_w:])
        wu, wd = Weight(up_weight), Weight(down_weight)

        packet.near()
        if square:
            info = jnp.concatenate([own_info, seq.send(to_ctx, own_info)], axis=1)
        else:
            info = lax.all_gather(own_info, "ctx", axis=1, tiled=True)
        x, factors = seq.run(order, x_raw, factors=True)
        packet.far()
        allowed, cos, sin = seq.run(positions, info)
        packet.core()
        wga.near()
        pieces, plan = packet_plan()
        h1, q, kv, gain, w_qkv, w_out = seq.run(
            first_kernel, x, factors, cos, sin, *pieces, plan=plan, blk=blk, qw=qw, kw=kw
        )
        g1, g2, g3, g4 = [gain[i : i + 1] for i in range(4)]
        if square:
            kv_got = seq.send(to_ctx, kv)
            wga.far()
            wgb.near()
            kv_all = seq.run(lambda a, b: jnp.concatenate([a, b], 0), kv, kv_got)
        else:
            kv_all = lax.all_gather(kv, "ctx", axis=0, tiled=True)
        length = kv_all.shape[0]

        o, logs, part = seq.run(attn_kernel, q, kv_all, allowed, w_out)
        za = ZSum(part)
        wgb.far()
        wu.near()
        wga.core()
        wgb.core()
        gate_w = stack(wga, wgb)
        wd.near()
        wu.far()
        za.middle()
        wu.core()
        up_m, up_s = stack(wu)
        dy = seq.run(order, dy_raw)
        wd.far()
        x2, h3, gate, up, hid = seq.run(
            ffn_in_kernel, za.out, x, g2, g3, *gate_w, up_m, up_s
        )
        wd.core()
        down_m, down_s = stack(wd)
        part = seq.run(project_kernel, hid, down_m, down_s)
        zf = ZSum(part)
        zf.middle()
        qkv_g = seq.run(row_order, w_qkv)
        g1_g = seq.run(order, jnp.broadcast_to(g1, (16, width)), back=True)[:1]

        y, df, dgate, dup, dg4 = seq.run(
            ffn_back_kernel, zf.out, x2, dy, g4, gate, up, down_m, down_s
        )
        part = seq.run(ffn_inputs_kernel, dgate, dup, *gate_w, up_m, up_s)
        zd = ZSum(part)

        class Scatter:
            def __init__(self, a, b):
                self.ab = a, b

            def low(self, cost=NO_COST):
                cuts = [blk] * 4 if square else [mid]
                low = seq.run(outer_kernel, *self.ab, side=1, cuts=cuts, cost=cost)
                self.got = [seq.send(to_core, v) for v in low]

            def first(self, cost=NO_COST):
                h = blk // 2
                cuts = [blk] + [h] * 6 if square else [mid]
                self.s = seq.run(
                    outer_kernel, *self.ab, *self.got, side=0, cuts=cuts, cost=cost
                )
                if square:
                    self.gx = seq.send(to_ctx, self.s[5])
                    self.gy = seq.send(to_y, self.s[6])

            def plain(self):
                if square:
                    self.xa = seq.send(to_ctx, self.s[1])
                    self.yb = seq.send(to_y, self.s[4])

            def wait(self):
                if square:
                    self.xa, self.yb = seq(self.xa, self.yb)
                    seq.last = (self.xa, self.yb)

            def second(self):
                if not square:
                    self.rest = lax.psum_scatter(
                        self.s[0], ("y", "ctx"), scatter_dimension=0, tiled=True
                    )
                    return
                t1 = seq.run(add_kernel, self.s[2], self.gy)
                self.xb = seq.send(to_ctx, t1)
                t2 = seq.run(add_kernel, self.s[3], self.gx)
                self.ya = seq.send(to_y, t2)

            def end(self):
                if not square:
                    return wide(self.rest)
                return seq.run(
                    sum_kernel, self.s[0], self.xa, self.xb, self.ya, self.yb
                )

        sd, sg, su = Scatter(df, hid), Scatter(h3, dgate), Scatter(h3, dup)
        sd.low()
        sg.low()
        sd.first()
        sd.plain()
        su.low(cost=LONG)
        sg.first()
        sg.plain()
        sd.second()
        sd.wait()
        zd.middle()
        su.first(cost=LONG)
        sg.second()
        sg.wait()
        down_grad = sd.end()
        layer_output = seq.run(order, y, back=True)

        dx2, da, dq, dkv, dg23 = seq.run(
            attn_back_kernel, zd.out, x2, dy, za.out, g3, g2, w_out,
            q, kv_all, allowed, logs, cos, sin,
        )
        if square:
            got = seq.send(to_ctx, dkv[toks:].astype(LOW))
            own = dkv[:toks]
        else:
            got = lax.psum_scatter(
                dkv.astype(LOW), "ctx", scatter_dimension=0, tiled=True
            )
            own = jnp.zeros((toks, 2 * kw), F32)
        su.plain()
        so = Scatter(da, o)
        so.low(cost=LONG)
        su.second()
        dkv_low = seq.run(keys_back_kernel, own, got, cos, sin)
        dqkv = seq.run(lambda a, b: jnp.concatenate([a, b], 1), dq, dkv_low)
        part = seq.run(project_kernel, dqkv, qkv_g[:mid], qkv_g[mid:])
        z1 = ZSum(part)
        sq = Scatter(h1, dqkv)
        sq.low()
        so.first()
        so.plain()
        sq.first(cost=LONG)
        su.wait()
        sq.plain()
        gate_grad = sg.end()
        dx2 = seq.run(order, dx2, back=True)
        so.second()
        up_grad = su.end()
        z1.middle()
        so.wait()
        sq.second()
        out_grad = so.end()
        sq.wait()
        qkv_grad = sq.end()
        input_grad, dg1 = seq.run(last_kernel, x_raw, g1_g, z1.out, dx2)
        dg1 = order(jnp.broadcast_to(dg1, (16, width)))[:1]
        dgain = jnp.concatenate([dg1, dg23[:2], dg4], axis=0)
        dgain = dgain[:, :mid] + to_core(dgain[:, mid:])
        if square:
            s = dgain[:, : mid // 2] + to_y(dgain[:, mid // 2 :])
            dgain = s[:, :blk] + to_ctx(s[:, blk:])
        else:
            dgain = lax.psum_scatter(
                dgain, ("y", "ctx"), scatter_dimension=1, tiled=True
            )
        return (
            layer_output.reshape(rows, toks, width),
            input_grad.reshape(rows, toks, width),
            qkv_grad[:, :qw],
            qkv_grad[:, qw : qw + kw],
            qkv_grad[:, qw + kw :],
            out_grad,
            gate_grad,
            up_grad,
            down_grad,
            dgain[0],
            dgain[1],
            dgain[2],
            dgain[3],
        )

    return local


def solution(mesh):
    dp, nx, nz = (mesh.shape[a] for a in ("dp", "ctx", "tensor"))
    fine = Mesh(
        mesh.devices.reshape(dp // 2, 2, nx, nz), ("y", "core", "ctx", "tensor")
    )
    d = ("y", "core")
    w = P(("y", "core", "ctx"), "tensor")
    g = P(("y", "core", "ctx"))
    t = P(d, "ctx", None)
    return jax.shard_map(
        make_local(dp // 2, nx, nz),
        mesh=fine,
        in_specs=(t, w, w, w, w, w, w, w, g, g, g, g, t, P(d, "ctx"), P(d, "ctx")),
        out_specs=(t, t, w, w, w, w, w, w, w, g, g, g, g),
        check_vma=False,
    )
```

```python
import math

import jax
import jax.numpy as jnp
from jax import lax
from jax.experimental import pallas as pl
from jax.experimental.pallas import tpu as pltpu
from jax.sharding import Mesh
from jax.sharding import PartitionSpec as P

HD = 256
NORM_EPSILON = 1e-06
SOFT_CAP = 50.0
MASKED_SCORE = -1e30
SWAP = [(0, 1), (1, 0)]
LOW = jnp.bfloat16
F32 = jnp.float32
VMEM_MB = 56
NO_COST = pl.CostEstimate(flops=0, bytes_accessed=0, transcendentals=0)
LONG = pl.CostEstimate(flops=10**12, bytes_accessed=0, transcendentals=0)


def wide(a):
    return a.astype(F32)


def after(value, *deps):
    return lax.optimization_barrier((value,) + deps)[0]


class Order:
    def __init__(self):
        self.last = ()

    def __call__(self, *values):
        return after(values, *self.last) if self.last else values

    def run(self, fn, *values, **kw):
        out = fn(*self(*values), **kw)
        self.last = (out,)
        return out

    def send(self, move, value):
        (value,) = self(value)
        self.last = (value,)
        return move(value)


def to_ctx(a):
    return lax.ppermute(a, "ctx", SWAP)


def to_y(a):
    return lax.ppermute(a, "y", SWAP)


def to_core(a):
    return lax.ppermute(a, "core", SWAP)


def nn(a, b):
    return jnp.dot(a, b, preferred_element_type=F32)


def nt(a, b):
    return lax.dot_general(a, b, (((1,), (1,)), ((), ())), preferred_element_type=F32)


def tn(a, b):
    return lax.dot_general(a, b, (((0,), (0,)), ((), ())), preferred_element_type=F32)


def norm_factor(v):
    return lax.rsqrt(jnp.mean(v * v, axis=-1, keepdims=True) + NORM_EPSILON)


def over_rows(rows, step, carry=None, block=64):
    block = math.gcd(rows, block)
    at = lambda i: pl.ds(pl.multiple_of(i * block, block), block)
    return lax.fori_loop(0, rows // block, lambda i, c: step(at(i), c), carry)


def fold(v):
    return sum(v[i : i + 8] for i in range(0, v.shape[0], 8))


def norm_back_rows(v, gain, grad):
    r = norm_factor(v)
    w = (1.0 + gain) * grad
    vr = v * r
    dv = r * (w - vr * jnp.mean(vr * w, axis=-1, keepdims=True))
    return dv, fold(grad * vr)


def gelu_parts(u):
    k = math.sqrt(2.0 / math.pi)
    th = jnp.tanh(k * (u + 0.044715 * u * u * u))
    g = 0.5 * u * (1.0 + th)
    dg = 0.5 * (1.0 + th) + 0.5 * u * (1.0 - th * th) * k * (1.0 + 3 * 0.044715 * u * u)
    return g, dg


def turn(v, c, s):
    h = HD // 2
    a, b = v[:, :h], v[:, h:]
    return jnp.concatenate([a * c - b * s, b * c + a * s], axis=1)


def turn_back(v, c, s):
    h = HD // 2
    a, b = v[:, :h], v[:, h:]
    return jnp.concatenate([a * c + b * s, b * c - a * s], axis=1)


def spec(block, index, mode=None):
    return pl.BlockSpec(block, index, pipeline_mode=mode)


def kernel(body, grid, ins, outs, scratch=(), cost=NO_COST):
    return pl.pallas_call(
        body,
        grid=grid,
        in_specs=[spec(*e[1:]) for e in ins],
        out_specs=[spec(*e[2:]) for e in outs],
        out_shape=[jax.ShapeDtypeStruct(*e[:2]) for e in outs],
        scratch_shapes=list(scratch),
        cost_estimate=cost,
        name=body.__qualname__.split(".")[0],
        compiler_params=pltpu.CompilerParams(vmem_limit_bytes=VMEM_MB * 2**20),
    )(*[e[0] for e in ins])


def all_of(shape):
    return tuple(shape), lambda *i: (0,) * len(shape), pl.Buffered(1)


def first_kernel(x, r, cos, sin, *pieces, plan, blk, qw, kw):
    toks, width = x.shape
    wide_w = pieces[0].shape[1]
    cols = qw + 2 * kw
    devices = width // blk
    lanes = -(-blk // 128) * 128
    scale = 1.0 / math.sqrt(HD)
    n = len(pieces)

    def body(x_r, r_r, c_r, s_r, *refs):
        piece_h = refs[:n]
        h_h, q_r, kv_r, g_r, w_h, o_h = refs[n : n + 6]
        h_r, w_r, raw_g_r, sems = refs[n + 6 :]
        c = Copies(sems)
        for k, (p, r0, rows, at, gain_at) in enumerate(plan):
            if at is None:
                src = piece_h[p].at[pl.ds(r0, rows), pl.ds(0, lanes)]
                c.start(("g", k), src, raw_g_r.at[pl.ds(gain_at, rows)])
        for k, (p, r0, rows, at, gain_at) in enumerate(plan):
            if at is not None:
                c.start(("w", k), piece_h[p].at[pl.ds(r0, rows)], w_r.at[pl.ds(at, rows)])
        c.wait(*[k for k in c.known if k[0] == "g"])
        rows16 = raw_g_r[...]
        gains = [rows16[d * 16 : d * 16 + 8, :blk] for d in range(devices)]
        gains = wide(jnp.concatenate(gains, axis=1))
        g_r[...] = gains
        g1 = 1.0 + gains[0:1]

        def normed(at, _):
            h_r[at, :] = (wide(x_r[at, :]) * r_r[at, 0:1] * g1).astype(LOW)

        over_rows(toks, normed)
        c.start("h", h_r, h_h)
        c.wait(*[k for k in c.known if k[0] == "w"])
        c.start("qkv", w_r.at[:, pl.ds(0, cols)], w_h)
        c.start("out", w_r.at[:, pl.ds(cols, wide_w - cols)], o_h)
        raw = nn(h_r[...], w_r[:, :cols])
        co, si = c_r[...], s_r[...]
        for j in range(qw // HD):
            cut = slice(j * HD, (j + 1) * HD)
            q_r[:, cut] = (turn(raw[:, cut], co, si) * scale).astype(LOW)
        for j in range(kw // HD):
            cut = slice(j * HD, (j + 1) * HD)
            k = turn(raw[:, qw + j * HD : qw + (j + 1) * HD], co, si)
            kv_r[:, cut] = k.astype(LOW)
        kv_r[:, kw:] = raw[:, qw + kw :].astype(LOW)
        c.wait("h", "qkv", "out")

    ins = [(v, "vmem") for v in (x, r, cos, sin)] + [(p, "hbm") for p in pieces]
    outs = [
        ((toks, width), LOW, "hbm"),
        ((toks, qw), LOW, "vmem"),
        ((toks, 2 * kw), LOW, "vmem"),
        ((8, width), F32, "vmem"),
        ((width, cols), LOW, "hbm"),
        ((width, wide_w - cols), LOW, "hbm"),
    ]
    scratch = [((toks, width), LOW), ((width, wide_w), LOW), ((16 * devices, lanes), LOW)]
    return streaming(body, ins, outs, scratch, len(plan) + 3, LONG)


def query_block(rows, length):
    return min(rows, 256 if length <= 2048 else 128)


def attn_kernel(q, kv, allowed, w):
    rows, qw = q.shape
    length = kv.shape[0]
    width = w.shape[0]
    qb = query_block(rows, length)
    heads = qw // HD

    def body(q_r, kv_r, m_r, w_r, o_r, t_r, a_r):
        ok = m_r[...] > 0
        k, v = kv_r[:, :HD], kv_r[:, HD:]
        logs = []
        for j in range(heads):
            cut = slice(j * HD, (j + 1) * HD)
            b = jnp.tanh(nt(q_r[:, cut], k) * (1.0 / SOFT_CAP))
            c = jnp.where(ok, SOFT_CAP * b, MASKED_SCORE)
            peak = jnp.max(c, axis=-1, keepdims=True)
            e = jnp.exp(c - peak)
            total = jnp.sum(e, axis=-1, keepdims=True)
            p = (e / total).astype(LOW)
            o_r[:, cut] = nn(p, v).astype(LOW)
            logs.append(jnp.broadcast_to(peak + jnp.log(total), (qb, 128)))
        t_r[...] = jnp.concatenate(logs, axis=1)
        a_r[...] = nt(o_r[...], w_r[...]).astype(LOW)

    row = lambda n: ((qb, n), lambda i: (i, 0))
    ins = [(q, *row(qw)), (kv, *all_of(kv.shape)), (allowed, *row(length))]
    ins += [(w, *all_of(w.shape))]
    outs = [
        ((rows, qw), LOW, *row(qw)),
        ((rows, 128 * heads), F32, *row(128 * heads)),
        ((rows, width), LOW, *row(width)),
    ]
    return kernel(body, (rows // qb,), ins, outs, cost=LONG)


def attn_back_kernel(
    dh3, x2, dy, a, g3, g2, w, q, kv, allowed, logs, cos, sin
):
    rows, width = x2.shape
    qw = q.shape[1]
    length = kv.shape[0]
    qb = query_block(rows, length)
    heads = qw // HD
    scale = 1.0 / math.sqrt(HD)

    def body(
        d_r, x_r, dy_r, a_r, g3_r, g2_r, w_r, q_r, kv_r, m_r, t_r, c_r, s_r,
        dx_r, da_r, dq_r, dkv_r, dg_r,
    ):
        @pl.when(pl.program_id(0) == 0)
        def _():
            dkv_r[...] = jnp.zeros_like(dkv_r)
            dg_r[...] = jnp.zeros_like(dg_r)

        def step(at, total):
            dv3, dg3 = norm_back_rows(x_r[at, :], g3_r[...], wide(d_r[at, :]))
            dx2 = wide(dy_r[at, :]) + dv3
            dx_r[at, :] = dx2
            da, dg2 = norm_back_rows(wide(a_r[at, :]), g2_r[...], dx2)
            da_r[at, :] = da.astype(LOW)
            return total[0] + dg2, total[1] + dg3

        none = jnp.zeros((8, width), F32)
        dg2, dg3 = over_rows(qb, step, (none, none))
        dg_r[0:1] += jnp.sum(dg2, axis=0, keepdims=True)
        dg_r[1:2] += jnp.sum(dg3, axis=0, keepdims=True)
        do = nn(da_r[...], w_r[...]).astype(LOW)
        ok = m_r[...] > 0
        k, v = kv_r[:, :HD], kv_r[:, HD:]
        c, s = c_r[...], s_r[...]
        dk = dv = 0.0
        for j in range(heads):
            cut = slice(j * HD, (j + 1) * HD)
            qj, doj = q_r[:, cut], do[:, cut]
            b = jnp.tanh(nt(qj, k) * (1.0 / SOFT_CAP))
            logit = jnp.where(ok, SOFT_CAP * b, MASKED_SCORE)
            p = jnp.exp(logit - t_r[:, j * 128 : j * 128 + 1])
            dp = nt(doj, v)
            dc = p * (dp - jnp.sum(p * dp, axis=-1, keepdims=True))
            ds = (dc * (1.0 - b * b)).astype(LOW)
            dq_r[:, cut] = (turn_back(nn(ds, k), c, s) * scale).astype(LOW)
            dk = dk + tn(ds, qj)
            dv = dv + tn(p.astype(LOW), doj)
        dkv_r[:, :HD] += dk
        dkv_r[:, HD:] += dv

    row = lambda n: ((qb, n), lambda i: (i, 0))
    ins = [(v, *row(width)) for v in (dh3, x2, dy, a)]
    ins += [(v, *all_of(v.shape)) for v in (g3, g2, w)]
    ins += [(q, *row(qw)), (kv, *all_of(kv.shape)), (allowed, *row(length))]
    ins += [(logs, *row(128 * heads)), (cos, *row(HD // 2)), (sin, *row(HD // 2))]
    outs = [
        ((rows, width), F32, *row(width)),
        ((rows, width), LOW, *row(width)),
        ((rows, qw), LOW, *row(qw)),
        ((length, 2 * HD), F32, *all_of((length, 2 * HD))),
        ((8, width), F32, *all_of((8, width))),
    ]
    return kernel(body, (rows // qb,), ins, outs, cost=LONG)


class Copies:
    def __init__(self, sems):
        self.sems, self.known = sems, {}

    def start(self, name, src, dst):
        self.known[name] = pltpu.make_async_copy(src, dst, self.sems.at[len(self.known)])
        self.known[name].start()

    def wait(self, *names):
        for name in names:
            self.known[name].wait()


def streaming(body, ins, outs, scratch, copies, cost=NO_COST):
    place = {"vmem": pl.BlockSpec(memory_space=pltpu.VMEM), "hbm": pl.BlockSpec(memory_space=pltpu.HBM)}
    return pl.pallas_call(
        body,
        in_specs=[place[p] for _, p in ins],
        out_specs=[place[p] for _, _, p in outs],
        out_shape=[jax.ShapeDtypeStruct(s, d) for s, d, _ in outs],
        scratch_shapes=[pltpu.VMEM(*v) for v in scratch]
        + [pltpu.SemaphoreType.DMA((copies,))],
        cost_estimate=cost,
        name=body.__qualname__.split(".")[0],
        compiler_params=pltpu.CompilerParams(vmem_limit_bytes=VMEM_MB * 2**20),
    )(*[a for a, _ in ins])


def row_parts(rows, block=128):
    return [pl.ds(i, min(block, rows)) for i in range(0, rows, min(block, rows))]


def col_chunks(where, total, most=768):
    starts = sorted({c for _, c in where}) + [total]
    chunks = []
    for lo, hi in zip(starts, starts[1:]):
        while lo < hi:
            n = hi - lo if hi - lo <= most else min(most, -(-(hi - lo) // 2 // 128) * 128)
            chunks.append((lo, n))
            lo += n
    return chunks


def start_cols(c, name, j, chunk, pieces, shapes, where, dst):
    names, (lo, n) = [], chunk
    for i, (p, s, (row, col)) in enumerate(zip(pieces, shapes, where)):
        if col <= lo < col + s[1]:
            src = p.at[:, pl.ds(lo - col, n)]
            c.start((name, j, i), src, dst.at[pl.ds(row, s[0]), pl.ds(lo, n)])
            names.append((name, j, i))
    return names


def start_rows(c, name, pieces, shapes, where, dst):
    names = []
    for i in sorted(range(len(pieces)), key=lambda i: where[i]):
        (row, col), s = where[i], shapes[i]
        c.start((name, i), pieces[i], dst.at[pl.ds(row, s[0]), pl.ds(col, s[1])])
        names.append((row, row + s[0], (name, i)))
    return names


def wait_rows(c, names, lo, hi, seen):
    for first, last, name in names:
        if first < hi and last > lo and name not in seen:
            seen.add(name)
            c.wait(name)


def row_groups(rows, most=768):
    return [(i, min(most, rows - i)) for i in range(0, rows, most)]


def ffn_in_kernel(a, x, g2, g3, *weights, gate_at, up_at):
    rows, width = x.shape
    ng = len(gate_at)
    shapes = [w.shape for w in weights]
    units = shapes[-1][1]
    parts = row_parts(rows)
    chunks = col_chunks(gate_at, units)

    def body(a_h, x_h, g2_r, g3_r, *refs):
        w_h, refs = refs[: len(shapes)], refs[len(shapes) :]
        x2_h, h_h, g_h, u_h, hid_h = refs[:5]
        a_r, x_r, x2_r, h_r, wg_r, wu_r, g_r, u_r, hid_r, sems = refs[5:]
        c = Copies(sems)
        for i, at in enumerate(parts):
            c.start(("a", i), a_h.at[at], a_r.at[at])
            c.start(("x", i), x_h.at[at], x_r.at[at])
        need = []
        for j, chunk in enumerate(chunks):
            names = start_cols(c, "g", j, chunk, w_h[:ng], shapes[:ng], gate_at, wg_r)
            names += start_cols(c, "u", j, chunk, w_h[ng:], shapes[ng:], up_at, wu_r)
            need.append(names)
        out = []

        def send(src, dst, at):
            out.append(("out", len(out)))
            c.start(out[-1], src.at[at], dst.at[at])

        for i, part in enumerate(parts):
            c.wait(("a", i), ("x", i))

            def normed(at, _, first=part.start):
                at = pl.ds(pl.multiple_of(first + at.start, 16), at.size)
                av = wide(a_r[at, :])
                x2 = wide(x_r[at, :]) + av * norm_factor(av) * (1.0 + g2_r[...])
                x2_r[at, :] = x2
                h_r[at, :] = (x2 * norm_factor(x2) * (1.0 + g3_r[...])).astype(LOW)

            over_rows(part.size, normed)
            send(x2_r, x2_h, (part,))
            send(h_r, h_h, (part,))
        for names, (lo, n) in zip(need, chunks):
            c.wait(*names)
            at = pl.ds(lo, n)
            h = h_r[...]
            gate, up = nn(h, wg_r[:, at]), nn(h, wu_r[:, at])
            g_r[:, at] = gate.astype(LOW)
            u_r[:, at] = up.astype(LOW)
            hid_r[:, at] = (gelu_parts(gate)[0] * up).astype(LOW)
            for src, dst in ((g_r, g_h), (u_r, u_h), (hid_r, hid_h)):
                send(src, dst, (slice(None), at))
        c.wait(*out)

    t, n = (rows, width), (rows, units)
    ins = [(a, "hbm"), (x, "hbm"), (g2, "vmem"), (g3, "vmem")]
    ins += [(w, "hbm") for w in weights]
    outs = [(t, F32, "hbm"), (t, LOW, "hbm")] + [(n, LOW, "hbm")] * 3
    w = (width, units)
    scratch = [(t, LOW), (t, LOW), (t, F32), (t, LOW), (w, LOW), (w, LOW)]
    scratch += [(n, LOW)] * 3
    copies = 4 * len(parts) + (3 + len(weights)) * len(chunks)
    return streaming(body, ins, outs, scratch, copies)


def project_kernel(u, *weights, at):
    rows, cols = u.shape
    shapes = [w.shape for w in weights]
    width = sum(s[0] for s in shapes)
    groups = row_groups(width)

    def body(u_r, *refs):
        w_h, (o_h, w_r, o_r, sems) = refs[: len(shapes)], refs[len(shapes) :]
        c = Copies(sems)
        names, seen = start_rows(c, "w", w_h, shapes, at, w_r), set()
        for g, (lo, n) in enumerate(groups):
            wait_rows(c, names, lo, lo + n, seen)
            cut = pl.ds(lo, n)
            o_r[:, cut] = nt(u_r[...], w_r[cut, :]).astype(LOW)
            c.start(("out", g), o_r.at[:, cut], o_h.at[:, cut])
        c.wait(*[("out", g) for g in range(len(groups))])

    ins = [(u, "vmem")] + [(w, "hbm") for w in weights]
    outs = [((rows, width), LOW, "hbm")]
    scratch = [((width, cols), LOW), ((rows, width), LOW)]
    return streaming(body, ins, outs, scratch, len(weights) + len(groups))[0]


def ffn_back_kernel(f, x2, dy, g4, gate, up, *weights, at):
    rows, width = x2.shape
    units = gate.shape[1]
    shapes = [w.shape for w in weights]
    parts = row_parts(rows)
    chunks = col_chunks(at, units)

    def body(f_h, x2_h, dy_h, g4_r, gate_h, up_h, *refs):
        w_h, refs = refs[: len(shapes)], refs[len(shapes) :]
        y_h, df_h, dg_h, du_h, g_r = refs[:5]
        f_r, x2_r, dy_r, gate_r, up_r, w_r, y_r, df_r, dg_r, du_r, sems = refs[5:]
        c = Copies(sems)
        for i, part in enumerate(parts):
            for name, src, dst in (("f", f_h, f_r), ("x", x2_h, x2_r), ("d", dy_h, dy_r)):
                c.start((name, i), src.at[part], dst.at[part])
        need = []
        for j, (lo, n) in enumerate(chunks):
            names = start_cols(c, "w", j, (lo, n), w_h, shapes, at, w_r)
            cut = pl.ds(lo, n)
            c.start(("gate", j), gate_h.at[:, cut], gate_r.at[:, cut])
            c.start(("up", j), up_h.at[:, cut], up_r.at[:, cut])
            need.append(names + [("gate", j), ("up", j)])
        out = []

        def send(src, dst, cut):
            out.append(("out", len(out)))
            c.start(out[-1], src.at[cut], dst.at[cut])

        total = jnp.zeros((8, width), F32)
        for i, part in enumerate(parts):
            c.wait(("f", i), ("x", i), ("d", i))

            def step(cut, total, first=part.start):
                cut = pl.ds(pl.multiple_of(first + cut.start, 16), cut.size)
                fv, g4v, x2v = wide(f_r[cut, :]), g4_r[...], x2_r[cut, :]
                y_r[cut, :] = (x2v + fv * norm_factor(fv) * (1.0 + g4v)).astype(LOW)
                df, dg = norm_back_rows(fv, g4v, wide(dy_r[cut, :]))
                df_r[cut, :] = df.astype(LOW)
                return total + dg

            total = over_rows(part.size, step, total)
            send(y_r, y_h, (part,))
            send(df_r, df_h, (part,))
        g_r[...] = jnp.sum(total, axis=0, keepdims=True)
        for names, (lo, n) in zip(need, chunks):
            c.wait(*names)
            cut = pl.ds(lo, n)
            dh = nn(df_r[...], w_r[:, cut])
            gl, dgl = gelu_parts(wide(gate_r[:, cut]))
            dg_r[:, cut] = (dh * wide(up_r[:, cut]) * dgl).astype(LOW)
            du_r[:, cut] = (dh * gl).astype(LOW)
            send(dg_r, dg_h, (slice(None), cut))
            send(du_r, du_h, (slice(None), cut))
        c.wait(*out)

    t, n = (rows, width), (rows, units)
    ins = [(v, "hbm") for v in (f, x2, dy)] + [(g4, "vmem")]
    ins += [(v, "hbm") for v in (gate, up, *weights)]
    outs = [(t, LOW, "hbm"), (t, LOW, "hbm"), (n, LOW, "hbm"), (n, LOW, "hbm")]
    outs += [((1, width), F32, "vmem")]
    scratch = [(t, LOW), (t, F32), (t, LOW), (n, LOW), (n, LOW), ((width, units), LOW)]
    scratch += [(t, LOW), (t, LOW), (n, LOW), (n, LOW)]
    copies = 5 * len(parts) + (4 + len(weights)) * len(chunks)
    return streaming(body, ins, outs, scratch, copies)


def ffn_inputs_kernel(dg, du, *weights, gate_at, up_at):
    rows, units = dg.shape
    ng = len(gate_at)
    shapes = [w.shape for w in weights]
    width = sum(s[0] for s in shapes[ng:])
    groups = row_groups(width)

    def body(dg_r, du_r, *refs):
        w_h, (o_h, wg_r, wu_r, o_r, sems) = refs[: len(shapes)], refs[len(shapes) :]
        c = Copies(sems)
        order = sorted(range(len(shapes)), key=lambda i: (gate_at + up_at)[i][0])
        names, seen = [], set()
        for i in order:
            (row, col), s = (gate_at + up_at)[i], shapes[i]
            dst = (wg_r if i < ng else wu_r).at[pl.ds(row, s[0]), pl.ds(col, s[1])]
            c.start(("w", i), w_h[i], dst)
            names.append((row, row + s[0], ("w", i)))
        for g, (lo, n) in enumerate(groups):
            wait_rows(c, names, lo, lo + n, seen)
            cut = pl.ds(lo, n)
            v = nt(dg_r[...], wg_r[cut, :]) + nt(du_r[...], wu_r[cut, :])
            o_r[:, cut] = v.astype(LOW)
            c.start(("out", g), o_r.at[:, cut], o_h.at[:, cut])
        c.wait(*[("out", g) for g in range(len(groups))])

    ins = [(dg, "vmem"), (du, "vmem")] + [(w, "hbm") for w in weights]
    outs = [((rows, width), LOW, "hbm")]
    w = ((width, units), LOW)
    scratch = [w, w, ((rows, width), LOW)]
    return streaming(body, ins, outs, scratch, len(weights) + len(groups))[0]


def outer_kernel(a, b, *got, side, cuts, cost=NO_COST):
    toks, cols = b.shape
    mid = a.shape[1] // 2
    bn = math.gcd(cols, 768)
    chunks = [pl.ds(i, bn) for i in range(0, cols, bn)]
    n, m = len(got), len(cuts)
    at = [sum(cuts[:i]) for i in range(m)]
    step = mid // n if n else 0

    def body(a_h, b_h, *refs):
        got_h, out_h = refs[:n], refs[n : n + m]
        a_r, b_r, got_r, out_r, sems = refs[n + m :]
        c = Copies(sems)
        c.start("a", a_h.at[:, pl.ds(side * mid, mid)], a_r)
        for j, part in enumerate(chunks):
            c.start(("b", j), b_h.at[:, part], b_r.at[:, part])
        for i in range(n):
            c.start(("got", i), got_h[i], got_r.at[pl.ds(i * step, step)])
        c.wait("a")
        for j, part in enumerate(chunks):
            c.wait(("b", j))
            v = tn(a_r[...], b_r[:, part])
            if n:
                if j == 0:
                    c.wait(*[("got", i) for i in range(n)])
                v = v + wide(got_r[:, part])
            out_r[:, part] = v.astype(LOW)
            for i in range(m):
                c.start(
                    ("out", i, j),
                    out_r.at[pl.ds(at[i], cuts[i]), part],
                    out_h[i].at[:, part],
                )
        c.wait(*[("out", i, j) for i in range(m) for j in range(len(chunks))])

    ins = [(v, "hbm") for v in (a, b, *got)]
    outs = [((r, cols), LOW, "hbm") for r in cuts]
    full = (mid, cols)
    scratch = [((toks, mid), LOW), ((toks, cols), LOW)]
    scratch += [(full if n else (16, 128), LOW), (full, LOW)]
    copies = 1 + len(chunks) * (1 + m) + n
    return streaming(body, ins, outs, scratch, copies, cost)


def sum_kernel(s, rx, ry):
    rows, cols = s.shape
    bc = math.gcd(cols, 768)

    def body(s_r, x_r, y_r, o_r):
        o_r[...] = wide(s_r[...]) + wide(x_r[...]) + wide(y_r[...])

    tile = ((rows, bc), lambda j: (0, j))
    ins = [(v, *tile) for v in (s, rx, ry)]
    return kernel(body, (cols // bc,), ins, [((rows, cols), F32, *tile)])[0]


def pass_kernel(s1, s2, gx, gy):
    rows, cols = s1.shape
    h = rows // 2
    bc = math.gcd(cols, 768)

    def body(s1_r, s2_r, gx_r, gy_r, t1_r, t2_r):
        t1_r[:h] = s1_r[:h]
        t1_r[h:] = (wide(s1_r[h:]) + wide(gy_r[...])).astype(LOW)
        t2_r[:h] = (wide(s2_r[:h]) + wide(gx_r[...])).astype(LOW)
        t2_r[h:] = s2_r[h:]

    full, part = ((rows, bc), lambda j: (0, j)), ((h, bc), lambda j: (0, j))
    ins = [(s1, *full), (s2, *full), (gx, *part), (gy, *part)]
    return kernel(body, (cols // bc,), ins, [(s1.shape, LOW, *full)] * 2)


def last_kernel(x, gain, dh1, dx2):
    rows, width = x.shape
    br = min(rows, 128)

    def body(x_r, g_r, d_r, dx_r, o_r, dg_r):
        def step(at, total):
            dv, dg = norm_back_rows(wide(x_r[at, :]), g_r[...], wide(d_r[at, :]))
            o_r[at, :] = dx_r[at, :] + dv
            return total + dg

        @pl.when(pl.program_id(0) == 0)
        def _():
            dg_r[...] = jnp.zeros_like(dg_r)

        total = over_rows(br, step, jnp.zeros((8, width), F32))
        dg_r[...] += jnp.sum(total, axis=0, keepdims=True)

    row = ((br, width), lambda i: (i, 0))
    ins = [(x, *row), (gain, *all_of(gain.shape)), (dh1, *row), (dx2, *row)]
    outs = [((rows, width), F32, *row), ((1, width), F32, *all_of((1, width)))]
    return kernel(body, (rows // br,), ins, outs)


def order_kernel(v, bits, back, ny, nx, factors=False):
    rows, width = v.shape
    blk = width // (2 * ny * nx)
    br = min(rows, 128)
    here = lambda c, y, x: (c * ny + y) * nx + x
    there = lambda c, y, x: (y * 2 + c) * nx + x
    keys = [(c, y, x) for c in range(2) for y in range(ny) for x in range(nx)]
    src, dst = (here, there) if back else (there, here)
    flips = 3 if ny == 2 and nx == 2 else 1

    def body(b_r, v_r, o_r, *f_r):
        def step(at, _):
            rows_ = v_r[at, :]
            if factors:
                f = norm_factor(wide(rows_))
                f_r[0][at, :] = jnp.broadcast_to(f, (f.shape[0], 128))
            cut = lambda j: rows_[:, j * blk : (j + 1) * blk]
            parts = {k: cut(src(*k)) for k in keys}
            for pos in range(flips):
                on = b_r[pos] == 0
                flip = lambda k: tuple(1 - e if i == pos else e for i, e in enumerate(k))
                parts = {k: jnp.where(on, parts[k], parts[flip(k)]) for k in keys}
            o_r[at, :] = jnp.concatenate([parts[k] for k in sorted(keys, key=lambda k: dst(*k))], axis=1)

        over_rows(br, step)

    tile = pl.BlockSpec((br, width), lambda i: (i, 0))
    return pl.pallas_call(
        body,
        grid=(rows // br,),
        in_specs=[pl.BlockSpec(memory_space=pltpu.SMEM), tile],
        out_specs=[tile, pl.BlockSpec((br, 128), lambda i: (i, 0))][: 1 + factors],
        out_shape=[
            jax.ShapeDtypeStruct(v.shape, v.dtype),
            jax.ShapeDtypeStruct((rows, 128), F32),
        ][: 1 + factors],
        cost_estimate=NO_COST,
    )(bits, v)


def keys_back_kernel(own, got, cos, sin):
    def body(a_r, b_r, c_r, s_r, o_r):
        v = a_r[...] + wide(b_r[...])
        o_r[:, :HD] = turn_back(v[:, :HD], c_r[...], s_r[...]).astype(LOW)
        o_r[:, HD:] = v[:, HD:].astype(LOW)

    ins = [(v, *all_of(v.shape)) for v in (own, got, cos, sin)]
    return kernel(body, (1,), ins, [(own.shape, LOW, *all_of(own.shape))])[0]


def make_local(ny, nx, nz):
    square = ny == 2 and nx == 2
    plane = ny * nx

    def order(v, back=False, factors=False):
        bits = jnp.stack([lax.axis_index(a) for a in ("core", "y", "ctx")])
        out = order_kernel(v, bits.astype(jnp.int32), back, ny, nx, factors)
        return out if factors else out[0]

    def row_order(w):
        blk = w.shape[0] // (2 * plane)
        c = lax.axis_index("core")
        out = jnp.zeros_like(w)
        for half in range(2):
            for y in range(ny):
                for x in range(nx):
                    i = (half * ny + y) * nx + x
                    gy, gx = y, x
                    if square:
                        gy, gx = y ^ lax.axis_index("y"), x ^ lax.axis_index("ctx")
                    at = ((gy * 2 + (c ^ half)) * nx + gx) * blk
                    piece = lax.slice_in_dim(w, i * blk, (i + 1) * blk, axis=0)
                    out = lax.dynamic_update_slice_in_dim(out, piece, at, 0)
        return out

    def local(
        layer_input,
        query_weight,
        key_weight,
        value_weight,
        output_weight,
        gate_weight,
        up_weight,
        down_weight,
        attn_in_gain,
        attn_out_gain,
        ffn_in_gain,
        ffn_out_gain,
        out_cotangent,
        segment_ids,
        live_mask,
    ):
        rows, toks, width = layer_input.shape
        blk, qw = query_weight.shape
        kw = key_weight.shape[1]
        qkv_w = qw + 2 * kw
        mid = width // 2
        seq = Order()

        class ZSum:
            def __init__(self, part):
                self.own = lax.psum_scatter(
                    part, "tensor", scatter_dimension=0, tiled=True
                )

            def middle(self):
                (own,) = seq(self.own)
                seq.last = (own,)
                self.out = lax.all_gather(own, "tensor", axis=0, tiled=True)

        class Weight:
            def __init__(self, w):
                self.w = w
                if not square:
                    m = lax.all_gather(w, ("y", "ctx"), axis=0, tiled=True)
                    self.mine, self.other = [m], [to_core(m)]

            def near(self):
                if square:
                    w = self.w
                    self.mine = [w, seq.send(to_ctx, w), seq.send(to_y, w)]
                    self.other = [seq.send(to_core, w)]

            def far(self):
                if square:
                    h = blk // 2
                    wx, wy = seq(*self.mine[1:])
                    self.mine += [seq.send(to_y, wx[:h]), seq.send(to_ctx, wy[h:])]
                    self.other += [seq.send(to_core, wx), seq.send(to_core, wy)]

            def core(self):
                if square:
                    self.mine[3:] = seq(*self.mine[3:])
                    self.other += [seq.send(to_core, d) for d in self.mine[3:]]

        def settle(*values):
            values = seq(*values)
            seq.last = tuple(values)
            return list(values)

        def placed(*weights):
            pieces, where, col = [], [], 0
            for w in weights:
                at = 0
                for p in w.mine + w.other:
                    pieces.append(p)
                    where.append((at, col))
                    at += p.shape[0]
                col += w.w.shape[1]
            return pieces, where

        def packet_plan():
            pieces, plan, full, device = [], [], packet.w.shape[0], 0
            for side in (packet.mine, packet.other):
                at = 0
                for p in side:
                    i, r = 0, p.shape[0]
                    while i < r:
                        d, inside = divmod(at + i, full)
                        d += device
                        if inside < blk:
                            k = min(r - i, blk - inside)
                            plan.append((len(pieces), i, k, d * blk + inside, None))
                        else:
                            k = min(r - i, full - inside)
                            plan.append((len(pieces), i, k, None, d * 16))
                        i += k
                    at += r
                    pieces.append(p)
                device += plane
            return pieces, plan

        gains = jnp.stack([attn_in_gain, attn_out_gain, ffn_in_gain, ffn_out_gain])
        own = [query_weight, key_weight, value_weight, output_weight]
        own = jnp.concatenate(own, axis=1)
        gains = jnp.pad(gains, ((0, 12), (0, own.shape[1] - blk)))
        packet = Weight(jnp.concatenate([own, gains], axis=0))
        index = lax.axis_index("ctx") * toks + jnp.arange(toks, dtype=jnp.int32)
        own_info = jnp.concatenate([segment_ids, live_mask, index[None]], axis=0)

        def positions(info):
            seg_all, live_all, index_all = info[0:1], info[1:2], info[2:3]
            seg_col, index_col = segment_ids.reshape(toks, 1), index.reshape(toks, 1)
            start = jnp.sum((seg_all < seg_col).astype(jnp.int32), axis=1)
            allowed = (
                (index_all <= index_col)
                & (seg_all == seg_col)
                & ((live_all == 1) | (index_all == index_col))
            ).astype(LOW)
            freq = jnp.exp(
                jnp.arange(HD // 2, dtype=F32) * (-2.0 * math.log(10000.0) / HD)
            )
            angle = wide(index - start)[:, None] * freq
            return allowed, jnp.cos(angle), jnp.sin(angle)

        x_raw = layer_input.reshape(toks, width)
        dy_raw = out_cotangent.reshape(toks, width)
        wg, wu, wd = Weight(gate_weight), Weight(up_weight), Weight(down_weight)

        packet.near()
        if square:
            info = jnp.concatenate([own_info, seq.send(to_ctx, own_info)], axis=1)
        else:
            info = lax.all_gather(own_info, "ctx", axis=1, tiled=True)
        x, factors = seq.run(order, x_raw, factors=True)
        packet.far()
        allowed, cos, sin = seq.run(positions, info)
        packet.core()
        wg.near()
        pieces, plan = packet_plan()
        h1, q, kv, gain, w_qkv, w_out = seq.run(
            first_kernel, x, factors, cos, sin, *pieces, plan=plan, blk=blk, qw=qw, kw=kw
        )
        g1, g2, g3, g4 = [gain[i : i + 1] for i in range(4)]
        if square:
            kv_got = seq.send(to_ctx, kv)
            wg.far()
            kv_all = seq.run(lambda a, b: jnp.concatenate([a, b], 0), kv, kv_got)
        else:
            kv_all = lax.all_gather(kv, "ctx", axis=0, tiled=True)
        length = kv_all.shape[0]

        o, logs, part = seq.run(attn_kernel, q, kv_all, allowed, w_out)
        za = ZSum(part)
        if square:
            wg.mine[3:] = settle(*wg.mine[3:])
        wu.near()
        wg.core()
        wu.far()
        za.middle()
        dy = seq.run(order, dy_raw)
        if square:
            wu.mine[3:] = settle(*wu.mine[3:])
        wd.near()
        wu.core()
        wd.far()
        gate_p, gate_at = placed(wg)
        up_p, up_at = placed(wu)
        x2, h3, gate, up, hid = seq.run(
            ffn_in_kernel, za.out, x, g2, g3, *gate_p, *up_p, gate_at=gate_at, up_at=up_at
        )
        wd.core()
        down_p, down_at = placed(wd)
        part = seq.run(project_kernel, hid, *down_p, at=down_at)
        zf = ZSum(part)
        zf.middle()
        qkv_g = seq.run(row_order, w_qkv)
        g1_g = seq.run(order, jnp.broadcast_to(g1, (16, width)), back=True)[:1]

        y, df, dgate, dup, dg4 = seq.run(
            ffn_back_kernel, zf.out, x2, dy, g4, gate, up, *down_p, at=down_at
        )
        part = seq.run(
            ffn_inputs_kernel, dgate, dup, *gate_p, *up_p, gate_at=gate_at, up_at=up_at
        )
        zd = ZSum(part)

        class Scatter:
            def __init__(self, a, b):
                self.ab = a, b

            def low(self):
                low = seq.run(outer_kernel, *self.ab, side=1, cuts=[mid // 2] * 2)
                self.got = [seq.send(to_core, v) for v in low]

            def first(self):
                h = blk // 2
                cuts = [blk] * 3 + [h, h] if square else [mid]
                self.s = seq.run(outer_kernel, *self.ab, *self.got, side=0, cuts=cuts)
                if square:
                    self.gx = seq.send(to_ctx, self.s[3])
                    self.gy = seq.send(to_y, self.s[4])

            def second(self):
                if not square:
                    self.rest = lax.psum_scatter(
                        self.s[0], ("y", "ctx"), scatter_dimension=0, tiled=True
                    )
                    return
                s1, s2 = seq.run(pass_kernel, *self.s[1:3], self.gx, self.gy)
                self.rest = seq.send(to_ctx, s1), seq.send(to_y, s2)

            def end(self):
                if not square:
                    return wide(self.rest)
                return seq.run(sum_kernel, self.s[0], *self.rest)

        sd, sg, su = Scatter(df, hid), Scatter(h3, dgate), Scatter(h3, dup)
        sd.low()
        sg.low()
        sd.first()
        su.low()
        zd.middle()
        sg.first()
        sd.second()
        su.got = settle(*su.got)

        dx2, da, dq, dkv, dg23 = seq.run(
            attn_back_kernel, zd.out, x2, dy, za.out, g3, g2, w_out,
            q, kv_all, allowed, logs, cos, sin,
        )
        if square:
            got = seq.send(to_ctx, dkv[toks:].astype(LOW))
            own = dkv[:toks]
        else:
            got = lax.psum_scatter(
                dkv.astype(LOW), "ctx", scatter_dimension=0, tiled=True
            )
            own = jnp.zeros((toks, 2 * kw), F32)
        sg.second()
        down_grad = sd.end()
        dkv_low = seq.run(keys_back_kernel, own, got, cos, sin)
        dqkv = seq.run(lambda a, b: jnp.concatenate([a, b], 1), dq, dkv_low)
        part = seq.run(project_kernel, dqkv, qkv_g, at=[(0, 0)])
        z1 = ZSum(part)
        so, sq = Scatter(da, o), Scatter(h1, dqkv)
        su.first()
        so.low()
        sq.low()
        dx2 = seq.run(order, dx2, back=True)
        gate_grad = sg.end()
        su.second()
        z1.middle()
        so.first()
        sq.first()
        so.second()
        up_grad = su.end()
        sq.second()
        input_grad, dg1 = seq.run(last_kernel, x_raw, g1_g, z1.out, dx2)
        layer_output = seq.run(order, y, back=True)
        out_grad = so.end()
        qkv_grad = sq.end()
        dg1 = order(jnp.broadcast_to(dg1, (16, width)))[:1]
        dgain = jnp.concatenate([dg1, dg23[:2], dg4], axis=0)
        dgain = dgain[:, :mid] + to_core(dgain[:, mid:])
        if square:
            s = dgain[:, : mid // 2] + to_y(dgain[:, mid // 2 :])
            dgain = s[:, :blk] + to_ctx(s[:, blk:])
        else:
            dgain = lax.psum_scatter(
                dgain, ("y", "ctx"), scatter_dimension=1, tiled=True
            )
        return (
            layer_output.reshape(rows, toks, width),
            input_grad.reshape(rows, toks, width),
            qkv_grad[:, :qw],
            qkv_grad[:, qw : qw + kw],
            qkv_grad[:, qw + kw :],
            out_grad,
            gate_grad,
            up_grad,
            down_grad,
            dgain[0],
            dgain[1],
            dgain[2],
            dgain[3],
        )

    return local


def solution(mesh):
    dp, nx, nz = (mesh.shape[a] for a in ("dp", "ctx", "tensor"))
    fine = Mesh(
        mesh.devices.reshape(dp // 2, 2, nx, nz), ("y", "core", "ctx", "tensor")
    )
    d = ("y", "core")
    w = P(("y", "core", "ctx"), "tensor")
    g = P(("y", "core", "ctx"))
    t = P(d, "ctx", None)
    return jax.shard_map(
        make_local(dp // 2, nx, nz),
        mesh=fine,
        in_specs=(t, w, w, w, w, w, w, w, g, g, g, g, t, P(d, "ctx"), P(d, "ctx")),
        out_specs=(t, t, w, w, w, w, w, w, w, g, g, g, g),
        check_vma=False,
    )
```

```python
import math

import jax
import jax.numpy as jnp
from jax import lax
from jax.experimental import pallas as pl
from jax.experimental.pallas import tpu as pltpu
from jax.sharding import Mesh
from jax.sharding import PartitionSpec as P

HD = 256
NORM_EPSILON = 1e-06
SOFT_CAP = 50.0
MASKED_SCORE = -1e30
SWAP = [(0, 1), (1, 0)]
LOW = jnp.bfloat16
F32 = jnp.float32
VMEM_MB = 56
NO_COST = pl.CostEstimate(flops=0, bytes_accessed=0, transcendentals=0)
LONG = pl.CostEstimate(flops=10**12, bytes_accessed=0, transcendentals=0)


def wide(a):
    return a.astype(F32)


def after(value, *deps):
    return lax.optimization_barrier((value,) + deps)[0]


class Order:
    def __init__(self):
        self.last = ()

    def __call__(self, *values):
        return after(values, *self.last) if self.last else values

    def run(self, fn, *values, **kw):
        out = fn(*self(*values), **kw)
        self.last = (out,)
        return out

    def send(self, move, value):
        (value,) = self(value)
        self.last = (value,)
        return move(value)


def to_ctx(a):
    return lax.ppermute(a, "ctx", SWAP)


def to_y(a):
    return lax.ppermute(a, "y", SWAP)


def to_core(a):
    return lax.ppermute(a, "core", SWAP)


def nn(a, b):
    return jnp.dot(a, b, preferred_element_type=F32)


def nt(a, b):
    return lax.dot_general(a, b, (((1,), (1,)), ((), ())), preferred_element_type=F32)


def tn(a, b):
    return lax.dot_general(a, b, (((0,), (0,)), ((), ())), preferred_element_type=F32)


def norm_factor(v):
    return lax.rsqrt(jnp.mean(v * v, axis=-1, keepdims=True) + NORM_EPSILON)


def over_rows(rows, step, carry=None, block=64):
    block = math.gcd(rows, block)
    at = lambda i: pl.ds(pl.multiple_of(i * block, block), block)
    return lax.fori_loop(0, rows // block, lambda i, c: step(at(i), c), carry)


def fold(v):
    return sum(v[i : i + 8] for i in range(0, v.shape[0], 8))


def norm_back_rows(v, gain, grad):
    r = norm_factor(v)
    w = (1.0 + gain) * grad
    vr = v * r
    dv = r * (w - vr * jnp.mean(vr * w, axis=-1, keepdims=True))
    return dv, fold(grad * vr)


def gelu_parts(u):
    k = math.sqrt(2.0 / math.pi)
    th = jnp.tanh(k * (u + 0.044715 * u * u * u))
    g = 0.5 * u * (1.0 + th)
    dg = 0.5 * (1.0 + th) + 0.5 * u * (1.0 - th * th) * k * (1.0 + 3 * 0.044715 * u * u)
    return g, dg


def turn(v, c, s):
    h = HD // 2
    a, b = v[:, :h], v[:, h:]
    return jnp.concatenate([a * c - b * s, b * c + a * s], axis=1)


def turn_back(v, c, s):
    h = HD // 2
    a, b = v[:, :h], v[:, h:]
    return jnp.concatenate([a * c + b * s, b * c - a * s], axis=1)


def spec(block, index, mode=None):
    return pl.BlockSpec(block, index, pipeline_mode=mode)


def kernel(body, grid, ins, outs, scratch=(), cost=NO_COST):
    return pl.pallas_call(
        body,
        grid=grid,
        in_specs=[spec(*e[1:]) for e in ins],
        out_specs=[spec(*e[2:]) for e in outs],
        out_shape=[jax.ShapeDtypeStruct(*e[:2]) for e in outs],
        scratch_shapes=list(scratch),
        cost_estimate=cost,
        name=body.__qualname__.split(".")[0],
        compiler_params=pltpu.CompilerParams(vmem_limit_bytes=VMEM_MB * 2**20),
    )(*[e[0] for e in ins])


def all_of(shape):
    return tuple(shape), lambda *i: (0,) * len(shape), pl.Buffered(1)


def first_kernel(x, r, cos, sin, *pieces, plan, blk, qw, kw):
    toks, width = x.shape
    wide_w = pieces[0].shape[1]
    cols = qw + 2 * kw
    devices = width // blk
    lanes = -(-blk // 128) * 128
    scale = 1.0 / math.sqrt(HD)
    n = len(pieces)

    def body(x_r, r_r, c_r, s_r, *refs):
        piece_h = refs[:n]
        h_h, q_r, kv_r, g_r, w_h, o_h = refs[n : n + 6]
        h_r, w_r, raw_g_r, sems = refs[n + 6 :]
        c = Copies(sems)
        for k, (p, r0, rows, at, gain_at) in enumerate(plan):
            if at is None:
                src = piece_h[p].at[pl.ds(r0, rows), pl.ds(0, lanes)]
                c.start(("g", k), src, raw_g_r.at[pl.ds(gain_at, rows)])
        for k, (p, r0, rows, at, gain_at) in enumerate(plan):
            if at is not None:
                c.start(("w", k), piece_h[p].at[pl.ds(r0, rows)], w_r.at[pl.ds(at, rows)])
        c.wait(*[k for k in c.known if k[0] == "g"])
        rows16 = raw_g_r[...]
        gains = [rows16[d * 16 : d * 16 + 8, :blk] for d in range(devices)]
        gains = wide(jnp.concatenate(gains, axis=1))
        g_r[...] = gains
        g1 = 1.0 + gains[0:1]

        def normed(at, _):
            h_r[at, :] = (wide(x_r[at, :]) * r_r[at, 0:1] * g1).astype(LOW)

        over_rows(toks, normed)
        c.start("h", h_r, h_h)
        c.wait(*[k for k in c.known if k[0] == "w"])
        c.start("qkv", w_r.at[:, pl.ds(0, cols)], w_h)
        c.start("out", w_r.at[:, pl.ds(cols, wide_w - cols)], o_h)
        raw = nn(h_r[...], w_r[:, :cols])
        co, si = c_r[...], s_r[...]
        for j in range(qw // HD):
            cut = slice(j * HD, (j + 1) * HD)
            q_r[:, cut] = (turn(raw[:, cut], co, si) * scale).astype(LOW)
        for j in range(kw // HD):
            cut = slice(j * HD, (j + 1) * HD)
            k = turn(raw[:, qw + j * HD : qw + (j + 1) * HD], co, si)
            kv_r[:, cut] = k.astype(LOW)
        kv_r[:, kw:] = raw[:, qw + kw :].astype(LOW)
        c.wait("h", "qkv", "out")

    ins = [(v, "vmem") for v in (x, r, cos, sin)] + [(p, "hbm") for p in pieces]
    outs = [
        ((toks, width), LOW, "hbm"),
        ((toks, qw), LOW, "vmem"),
        ((toks, 2 * kw), LOW, "vmem"),
        ((8, width), F32, "vmem"),
        ((width, cols), LOW, "hbm"),
        ((width, wide_w - cols), LOW, "hbm"),
    ]
    scratch = [((toks, width), LOW), ((width, wide_w), LOW), ((16 * devices, lanes), LOW)]
    return streaming(body, ins, outs, scratch, len(plan) + 3, LONG)


def query_block(rows, length):
    return min(rows, 256 if length <= 2048 else 128)


def attn_kernel(q, kv, allowed, w):
    rows, qw = q.shape
    length = kv.shape[0]
    width = w.shape[0]
    qb = query_block(rows, length)
    heads = qw // HD

    def body(q_r, kv_r, m_r, w_r, o_r, t_r, a_r):
        ok = m_r[...] > 0
        k, v = kv_r[:, :HD], kv_r[:, HD:]
        logs = []
        for j in range(heads):
            cut = slice(j * HD, (j + 1) * HD)
            b = jnp.tanh(nt(q_r[:, cut], k) * (1.0 / SOFT_CAP))
            c = jnp.where(ok, SOFT_CAP * b, MASKED_SCORE)
            peak = jnp.max(c, axis=-1, keepdims=True)
            e = jnp.exp(c - peak)
            total = jnp.sum(e, axis=-1, keepdims=True)
            p = (e / total).astype(LOW)
            o_r[:, cut] = nn(p, v).astype(LOW)
            logs.append(jnp.broadcast_to(peak + jnp.log(total), (qb, 128)))
        t_r[...] = jnp.concatenate(logs, axis=1)
        a_r[...] = nt(o_r[...], w_r[...]).astype(LOW)

    row = lambda n: ((qb, n), lambda i: (i, 0))
    ins = [(q, *row(qw)), (kv, *all_of(kv.shape)), (allowed, *row(length))]
    ins += [(w, *all_of(w.shape))]
    outs = [
        ((rows, qw), LOW, *row(qw)),
        ((rows, 128 * heads), F32, *row(128 * heads)),
        ((rows, width), LOW, *row(width)),
    ]
    return kernel(body, (rows // qb,), ins, outs, cost=LONG)


def attn_back_kernel(
    dh3, x2, dy, a, g3, g2, w, q, kv, allowed, logs, cos, sin, toks
):
    rows, width = x2.shape
    qw = q.shape[1]
    length = kv.shape[0]
    qb = query_block(rows, length)
    heads = qw // HD
    other = toks if length == 2 * toks else length
    scale = 1.0 / math.sqrt(HD)

    def body(
        d_r, x_r, dy_r, a_r, g3_r, g2_r, w_r, q_r, kv_r, m_r, t_r, c_r, s_r,
        dx_r, da_r, dq_r, own_r, other_r, dg_r, dkv_r,
    ):
        @pl.when(pl.program_id(0) == 0)
        def _():
            dkv_r[...] = jnp.zeros_like(dkv_r)
            dg_r[...] = jnp.zeros_like(dg_r)

        def step(at, total):
            dv3, dg3 = norm_back_rows(x_r[at, :], g3_r[...], wide(d_r[at, :]))
            dx2 = wide(dy_r[at, :]) + dv3
            dx_r[at, :] = dx2
            da, dg2 = norm_back_rows(wide(a_r[at, :]), g2_r[...], dx2)
            da_r[at, :] = da.astype(LOW)
            return total[0] + dg2, total[1] + dg3

        none = jnp.zeros((8, width), F32)
        dg2, dg3 = over_rows(qb, step, (none, none))
        dg_r[0:1] += jnp.sum(dg2, axis=0, keepdims=True)
        dg_r[1:2] += jnp.sum(dg3, axis=0, keepdims=True)
        do = nn(da_r[...], w_r[...]).astype(LOW)
        ok = m_r[...] > 0
        k, v = kv_r[:, :HD], kv_r[:, HD:]
        c, s = c_r[...], s_r[...]
        dk = dv = 0.0
        for j in range(heads):
            cut = slice(j * HD, (j + 1) * HD)
            qj, doj = q_r[:, cut], do[:, cut]
            b = jnp.tanh(nt(qj, k) * (1.0 / SOFT_CAP))
            logit = jnp.where(ok, SOFT_CAP * b, MASKED_SCORE)
            p = jnp.exp(logit - t_r[:, j * 128 : j * 128 + 1])
            dp = nt(doj, v)
            dc = p * (dp - jnp.sum(p * dp, axis=-1, keepdims=True))
            ds = (dc * (1.0 - b * b)).astype(LOW)
            dq_r[:, cut] = (turn_back(nn(ds, k), c, s) * scale).astype(LOW)
            dk = dk + tn(ds, qj)
            dv = dv + tn(p.astype(LOW), doj)
        dkv_r[:, :HD] += dk
        dkv_r[:, HD:] += dv

        @pl.when(pl.program_id(0) == rows // qb - 1)
        def _():
            own_r[...] = dkv_r[:toks]
            other_r[...] = dkv_r[length - other :].astype(LOW)

    row = lambda n: ((qb, n), lambda i: (i, 0))
    ins = [(v, *row(width)) for v in (dh3, x2, dy, a)]
    ins += [(v, *all_of(v.shape)) for v in (g3, g2, w)]
    ins += [(q, *row(qw)), (kv, *all_of(kv.shape)), (allowed, *row(length))]
    ins += [(logs, *row(128 * heads)), (cos, *row(HD // 2)), (sin, *row(HD // 2))]
    outs = [
        ((rows, width), F32, *row(width)),
        ((rows, width), LOW, *row(width)),
        ((rows, qw), LOW, *row(qw)),
        ((toks, 2 * HD), F32, *all_of((toks, 2 * HD))),
        ((other, 2 * HD), LOW, *all_of((other, 2 * HD))),
        ((8, width), F32, *all_of((8, width))),
    ]
    scratch = [pltpu.VMEM((length, 2 * HD), F32)]
    return kernel(body, (rows // qb,), ins, outs, scratch, LONG)


class Copies:
    def __init__(self, sems):
        self.sems, self.known = sems, {}

    def start(self, name, src, dst):
        self.known[name] = pltpu.make_async_copy(src, dst, self.sems.at[len(self.known)])
        self.known[name].start()

    def wait(self, *names):
        for name in names:
            self.known[name].wait()


def streaming(body, ins, outs, scratch, copies, cost=NO_COST):
    place = {"vmem": pl.BlockSpec(memory_space=pltpu.VMEM), "hbm": pl.BlockSpec(memory_space=pltpu.HBM)}
    return pl.pallas_call(
        body,
        in_specs=[place[p] for _, p in ins],
        out_specs=[place[p] for _, _, p in outs],
        out_shape=[jax.ShapeDtypeStruct(s, d) for s, d, _ in outs],
        scratch_shapes=[pltpu.VMEM(*v) for v in scratch]
        + [pltpu.SemaphoreType.DMA((copies,))],
        cost_estimate=cost,
        name=body.__qualname__.split(".")[0],
        compiler_params=pltpu.CompilerParams(vmem_limit_bytes=VMEM_MB * 2**20),
    )(*[a for a, _ in ins])


def row_parts(rows, block=128):
    return [pl.ds(i, min(block, rows)) for i in range(0, rows, min(block, rows))]


def col_chunks(where, total, most=768):
    starts = sorted({c for _, c in where}) + [total]
    chunks = []
    for lo, hi in zip(starts, starts[1:]):
        while lo < hi:
            n = hi - lo if hi - lo <= most else min(most, -(-(hi - lo) // 2 // 128) * 128)
            chunks.append((lo, n))
            lo += n
    return chunks


def start_cols(c, name, j, chunk, pieces, shapes, where, dst):
    names, (lo, n) = [], chunk
    for i, (p, s, (row, col)) in enumerate(zip(pieces, shapes, where)):
        if col <= lo < col + s[1]:
            src = p.at[:, pl.ds(lo - col, n)]
            c.start((name, j, i), src, dst.at[pl.ds(row, s[0]), pl.ds(lo, n)])
            names.append((name, j, i))
    return names


def start_rows(c, name, pieces, shapes, where, dst):
    names = []
    for i in sorted(range(len(pieces)), key=lambda i: where[i]):
        (row, col), s = where[i], shapes[i]
        c.start((name, i), pieces[i], dst.at[pl.ds(row, s[0]), pl.ds(col, s[1])])
        names.append((row, row + s[0], (name, i)))
    return names


def wait_rows(c, names, lo, hi, seen):
    for first, last, name in names:
        if first < hi and last > lo and name not in seen:
            seen.add(name)
            c.wait(name)


def row_groups(rows, most=768):
    return [(i, min(most, rows - i)) for i in range(0, rows, most)]


def ffn_in_kernel(a, x, g2, g3, *weights, gate_at, up_at):
    rows, width = x.shape
    ng = len(gate_at)
    shapes = [w.shape for w in weights]
    units = shapes[-1][1]
    parts = row_parts(rows)
    chunks = col_chunks(gate_at, units)

    def body(a_h, x_h, g2_r, g3_r, *refs):
        w_h, refs = refs[: len(shapes)], refs[len(shapes) :]
        x2_h, h_h, gu_h, hid_h = refs[:4]
        a_r, x_r, x2_r, h_r, wg_r, wu_r, gu_r, hid_r, sems = refs[4:]
        c = Copies(sems)
        for i, at in enumerate(parts):
            c.start(("a", i), a_h.at[at], a_r.at[at])
            c.start(("x", i), x_h.at[at], x_r.at[at])
        need = []
        for j, chunk in enumerate(chunks):
            names = start_cols(c, "g", j, chunk, w_h[:ng], shapes[:ng], gate_at, wg_r)
            names += start_cols(c, "u", j, chunk, w_h[ng:], shapes[ng:], up_at, wu_r)
            need.append(names)
        out = []

        def send(src, dst, at):
            out.append(("out", len(out)))
            c.start(out[-1], src.at[at], dst.at[at])

        for i, part in enumerate(parts):
            c.wait(("a", i), ("x", i))

            def normed(at, _, first=part.start):
                at = pl.ds(pl.multiple_of(first + at.start, 16), at.size)
                av = wide(a_r[at, :])
                x2 = wide(x_r[at, :]) + av * norm_factor(av) * (1.0 + g2_r[...])
                x2_r[at, :] = x2
                h_r[at, :] = (x2 * norm_factor(x2) * (1.0 + g3_r[...])).astype(LOW)

            over_rows(part.size, normed)
            send(x2_r, x2_h, (part,))
            send(h_r, h_h, (part,))
        for names, (lo, n) in zip(need, chunks):
            c.wait(*names)
            at = pl.ds(lo, n)
            h = h_r[...]
            gate, up = nn(h, wg_r[:, at]), nn(h, wu_r[:, at])
            at2 = pl.ds(units + lo, n)
            gu_r[:, at] = gate.astype(LOW)
            gu_r[:, at2] = up.astype(LOW)
            hid_r[:, at] = (gelu_parts(gate)[0] * up).astype(LOW)
            for src, dst, cut in ((gu_r, gu_h, at), (gu_r, gu_h, at2), (hid_r, hid_h, at)):
                send(src, dst, (slice(None), cut))
        c.wait(*out)

    t, n = (rows, width), (rows, units)
    ins = [(a, "hbm"), (x, "hbm"), (g2, "vmem"), (g3, "vmem")]
    ins += [(w, "hbm") for w in weights]
    gu = (rows, 2 * units)
    outs = [(t, F32, "hbm"), (t, LOW, "hbm"), (gu, LOW, "hbm"), (n, LOW, "hbm")]
    w = (width, units)
    scratch = [(t, LOW), (t, LOW), (t, F32), (t, LOW), (w, LOW), (w, LOW)]
    scratch += [(gu, LOW), (n, LOW)]
    copies = 4 * len(parts) + (3 + len(weights)) * len(chunks)
    return streaming(body, ins, outs, scratch, copies)


def project_kernel(u, *weights, at):
    rows, cols = u.shape
    shapes = [w.shape for w in weights]
    width = sum(s[0] for s in shapes)
    groups = row_groups(width)

    def body(u_r, *refs):
        w_h, (o_h, w_r, o_r, sems) = refs[: len(shapes)], refs[len(shapes) :]
        c = Copies(sems)
        names, seen = start_rows(c, "w", w_h, shapes, at, w_r), set()
        for g, (lo, n) in enumerate(groups):
            wait_rows(c, names, lo, lo + n, seen)
            cut = pl.ds(lo, n)
            o_r[:, cut] = nt(u_r[...], w_r[cut, :]).astype(LOW)
            c.start(("out", g), o_r.at[:, cut], o_h.at[:, cut])
        c.wait(*[("out", g) for g in range(len(groups))])

    ins = [(u, "vmem")] + [(w, "hbm") for w in weights]
    outs = [((rows, width), LOW, "hbm")]
    scratch = [((width, cols), LOW), ((rows, width), LOW)]
    return streaming(body, ins, outs, scratch, len(weights) + len(groups))[0]


def ffn_back_kernel(f, x2, dy, g4, gate_up, *weights, at):
    rows, width = x2.shape
    units = gate_up.shape[1] // 2
    shapes = [w.shape for w in weights]
    parts = row_parts(rows)
    chunks = col_chunks(at, units, 1152)

    def body(f_h, x2_h, dy_h, g4_r, gu_h, *refs):
        w_h, refs = refs[: len(shapes)], refs[len(shapes) :]
        y_h, df_h, dg_h, du_h, g_r = refs[:5]
        f_r, x2_r, dy_r, gate_r, up_r, w_r, y_r, df_r, dg_r, du_r, sems = refs[5:]
        c = Copies(sems)
        for i, part in enumerate(parts):
            for name, src, dst in (("f", f_h, f_r), ("x", x2_h, x2_r), ("d", dy_h, dy_r)):
                c.start((name, i), src.at[part], dst.at[part])
        need = []
        for j, (lo, n) in enumerate(chunks):
            names = start_cols(c, "w", j, (lo, n), w_h, shapes, at, w_r)
            cut = pl.ds(lo, n)
            c.start(("gate", j), gu_h.at[:, cut], gate_r.at[:, cut])
            up_at = pl.ds(units + lo, n)
            c.start(("up", j), gu_h.at[:, up_at], up_r.at[:, cut])
            need.append(names + [("gate", j), ("up", j)])
        out = []

        def send(src, dst, cut):
            out.append(("out", len(out)))
            c.start(out[-1], src.at[cut], dst.at[cut])

        total = jnp.zeros((8, width), F32)
        for i, part in enumerate(parts):
            c.wait(("f", i), ("x", i), ("d", i))

            def step(cut, total, first=part.start):
                cut = pl.ds(pl.multiple_of(first + cut.start, 16), cut.size)
                fv, g4v, x2v = wide(f_r[cut, :]), g4_r[...], x2_r[cut, :]
                y_r[cut, :] = (x2v + fv * norm_factor(fv) * (1.0 + g4v)).astype(LOW)
                df, dg = norm_back_rows(fv, g4v, wide(dy_r[cut, :]))
                df_r[cut, :] = df.astype(LOW)
                return total + dg

            total = over_rows(part.size, step, total)
            send(y_r, y_h, (part,))
            send(df_r, df_h, (part,))
        g_r[...] = jnp.sum(total, axis=0, keepdims=True)
        for names, (lo, n) in zip(need, chunks):
            c.wait(*names)
            cut = pl.ds(lo, n)
            dh = nn(df_r[...], w_r[:, cut])
            gl, dgl = gelu_parts(wide(gate_r[:, cut]))
            dg_r[:, cut] = (dh * wide(up_r[:, cut]) * dgl).astype(LOW)
            du_r[:, cut] = (dh * gl).astype(LOW)
            send(dg_r, dg_h, (slice(None), cut))
            send(du_r, du_h, (slice(None), cut))
        c.wait(*out)

    t, n = (rows, width), (rows, units)
    ins = [(v, "hbm") for v in (f, x2, dy)] + [(g4, "vmem")]
    ins += [(v, "hbm") for v in (gate_up, *weights)]
    outs = [(t, LOW, "hbm"), (t, LOW, "hbm"), (n, LOW, "hbm"), (n, LOW, "hbm")]
    outs += [((1, width), F32, "vmem")]
    scratch = [(t, LOW), (t, F32), (t, LOW), (n, LOW), (n, LOW), ((width, units), LOW)]
    scratch += [(t, LOW), (t, LOW), (n, LOW), (n, LOW)]
    copies = 5 * len(parts) + (4 + len(weights)) * len(chunks)
    return streaming(body, ins, outs, scratch, copies)


def ffn_inputs_kernel(dg, du, *weights, gate_at, up_at):
    rows, units = dg.shape
    ng = len(gate_at)
    shapes = [w.shape for w in weights]
    width = sum(s[0] for s in shapes[ng:])
    groups = row_groups(width)

    def body(dg_r, du_r, *refs):
        w_h, (o_h, wg_r, wu_r, o_r, sems) = refs[: len(shapes)], refs[len(shapes) :]
        c = Copies(sems)
        order = sorted(range(len(shapes)), key=lambda i: (gate_at + up_at)[i][0])
        names, seen = [], set()
        for i in order:
            (row, col), s = (gate_at + up_at)[i], shapes[i]
            dst = (wg_r if i < ng else wu_r).at[pl.ds(row, s[0]), pl.ds(col, s[1])]
            c.start(("w", i), w_h[i], dst)
            names.append((row, row + s[0], ("w", i)))
        for g, (lo, n) in enumerate(groups):
            wait_rows(c, names, lo, lo + n, seen)
            cut = pl.ds(lo, n)
            v = nt(dg_r[...], wg_r[cut, :]) + nt(du_r[...], wu_r[cut, :])
            o_r[:, cut] = v.astype(LOW)
            c.start(("out", g), o_r.at[:, cut], o_h.at[:, cut])
        c.wait(*[("out", g) for g in range(len(groups))])

    ins = [(dg, "vmem"), (du, "vmem")] + [(w, "hbm") for w in weights]
    outs = [((rows, width), LOW, "hbm")]
    w = ((width, units), LOW)
    scratch = [w, w, ((rows, width), LOW)]
    return streaming(body, ins, outs, scratch, len(weights) + len(groups))[0]


def outer_kernel(a, b, *got, side, cuts, cost=NO_COST):
    toks, cols = b.shape
    mid = a.shape[1] // 2
    bn = math.gcd(cols, 768)
    chunks = [pl.ds(i, bn) for i in range(0, cols, bn)]
    n, m = len(got), len(cuts)
    at = [sum(cuts[:i]) for i in range(m)]
    step = mid // n if n else 0

    def body(a_h, b_h, *refs):
        got_h, out_h = refs[:n], refs[n : n + m]
        a_r, b_r, got_r, out_r, sems = refs[n + m :]
        c = Copies(sems)
        c.start("a", a_h.at[:, pl.ds(side * mid, mid)], a_r)
        for j, part in enumerate(chunks):
            c.start(("b", j), b_h.at[:, part], b_r.at[:, part])
        for i in range(n):
            c.start(("got", i), got_h[i], got_r.at[pl.ds(i * step, step)])
        c.wait("a")
        for j, part in enumerate(chunks):
            c.wait(("b", j))
            v = tn(a_r[...], b_r[:, part])
            if n:
                if j == 0:
                    c.wait(*[("got", i) for i in range(n)])
                v = v + wide(got_r[:, part])
            out_r[:, part] = v.astype(LOW)
            for i in range(m):
                c.start(
                    ("out", i, j),
                    out_r.at[pl.ds(at[i], cuts[i]), part],
                    out_h[i].at[:, part],
                )
        c.wait(*[("out", i, j) for i in range(m) for j in range(len(chunks))])

    ins = [(v, "hbm") for v in (a, b, *got)]
    outs = [((r, cols), LOW, "hbm") for r in cuts]
    full = (mid, cols)
    scratch = [((toks, mid), LOW), ((toks, cols), LOW)]
    scratch += [(full if n else (16, 128), LOW), (full, LOW)]
    copies = 1 + len(chunks) * (1 + m) + n
    return streaming(body, ins, outs, scratch, copies, cost)


def sum_kernel(s, rx, ry):
    rows, cols = s.shape
    bc = math.gcd(cols, 768)

    def body(s_r, x_r, y_r, o_r):
        o_r[...] = wide(s_r[...]) + wide(x_r[...]) + wide(y_r[...])

    tile = ((rows, bc), lambda j: (0, j))
    ins = [(v, *tile) for v in (s, rx, ry)]
    return kernel(body, (cols // bc,), ins, [((rows, cols), F32, *tile)])[0]


def pass_kernel(s1, s2, gx, gy):
    rows, cols = s1.shape
    h = rows // 2
    bc = math.gcd(cols, 768)

    def body(s1_r, s2_r, gx_r, gy_r, t1_r, t2_r):
        t1_r[:h] = s1_r[:h]
        t1_r[h:] = (wide(s1_r[h:]) + wide(gy_r[...])).astype(LOW)
        t2_r[:h] = (wide(s2_r[:h]) + wide(gx_r[...])).astype(LOW)
        t2_r[h:] = s2_r[h:]

    full, part = ((rows, bc), lambda j: (0, j)), ((h, bc), lambda j: (0, j))
    ins = [(s1, *full), (s2, *full), (gx, *part), (gy, *part)]
    return kernel(body, (cols // bc,), ins, [(s1.shape, LOW, *full)] * 2)


def last_kernel(x, gain, dh1, dx2):
    rows, width = x.shape
    br = min(rows, 128)

    def body(x_r, g_r, d_r, dx_r, o_r, dg_r):
        def step(at, total):
            dv, dg = norm_back_rows(wide(x_r[at, :]), g_r[...], wide(d_r[at, :]))
            o_r[at, :] = dx_r[at, :] + dv
            return total + dg

        @pl.when(pl.program_id(0) == 0)
        def _():
            dg_r[...] = jnp.zeros_like(dg_r)

        total = over_rows(br, step, jnp.zeros((8, width), F32))
        dg_r[...] += jnp.sum(total, axis=0, keepdims=True)

    row = ((br, width), lambda i: (i, 0))
    ins = [(x, *row), (gain, *all_of(gain.shape)), (dh1, *row), (dx2, *row)]
    outs = [((rows, width), F32, *row), ((1, width), F32, *all_of((1, width)))]
    return kernel(body, (rows // br,), ins, outs)


def order_kernel(v, bits, back, ny, nx, factors=False):
    rows, width = v.shape
    blk = width // (2 * ny * nx)
    br = min(rows, 128)
    here = lambda c, y, x: (c * ny + y) * nx + x
    there = lambda c, y, x: (y * 2 + c) * nx + x
    keys = [(c, y, x) for c in range(2) for y in range(ny) for x in range(nx)]
    src, dst = (here, there) if back else (there, here)
    flips = 3 if ny == 2 and nx == 2 else 1

    def body(b_r, v_r, o_r, *f_r):
        def step(at, _):
            rows_ = v_r[at, :]
            if factors:
                f = norm_factor(wide(rows_))
                f_r[0][at, :] = jnp.broadcast_to(f, (f.shape[0], 128))
            cut = lambda j: rows_[:, j * blk : (j + 1) * blk]
            parts = {k: cut(src(*k)) for k in keys}
            for pos in range(flips):
                on = b_r[pos] == 0
                flip = lambda k: tuple(1 - e if i == pos else e for i, e in enumerate(k))
                parts = {k: jnp.where(on, parts[k], parts[flip(k)]) for k in keys}
            o_r[at, :] = jnp.concatenate([parts[k] for k in sorted(keys, key=lambda k: dst(*k))], axis=1)

        over_rows(br, step)

    tile = pl.BlockSpec((br, width), lambda i: (i, 0))
    return pl.pallas_call(
        body,
        grid=(rows // br,),
        in_specs=[pl.BlockSpec(memory_space=pltpu.SMEM), tile],
        out_specs=[tile, pl.BlockSpec((br, 128), lambda i: (i, 0))][: 1 + factors],
        out_shape=[
            jax.ShapeDtypeStruct(v.shape, v.dtype),
            jax.ShapeDtypeStruct((rows, 128), F32),
        ][: 1 + factors],
        cost_estimate=NO_COST,
    )(bits, v)


def keys_back_kernel(own, got, cos, sin, dq):
    qw = dq.shape[1]

    def body(a_r, b_r, c_r, s_r, q_r, o_r):
        v = a_r[...] + wide(b_r[...])
        o_r[:, :qw] = q_r[...]
        o_r[:, qw : qw + HD] = turn_back(v[:, :HD], c_r[...], s_r[...]).astype(LOW)
        o_r[:, qw + HD :] = v[:, HD:].astype(LOW)

    ins = [(v, *all_of(v.shape)) for v in (own, got, cos, sin, dq)]
    shape = (own.shape[0], qw + own.shape[1])
    return kernel(body, (1,), ins, [(shape, LOW, *all_of(shape))])[0]


def make_local(ny, nx, nz):
    square = ny == 2 and nx == 2
    plane = ny * nx

    def order(v, back=False, factors=False):
        bits = jnp.stack([lax.axis_index(a) for a in ("core", "y", "ctx")])
        out = order_kernel(v, bits.astype(jnp.int32), back, ny, nx, factors)
        return out if factors else out[0]

    def row_order(w):
        blk = w.shape[0] // (2 * plane)
        c = lax.axis_index("core")
        out = jnp.zeros_like(w)
        for half in range(2):
            for y in range(ny):
                for x in range(nx):
                    i = (half * ny + y) * nx + x
                    gy, gx = y, x
                    if square:
                        gy, gx = y ^ lax.axis_index("y"), x ^ lax.axis_index("ctx")
                    at = ((gy * 2 + (c ^ half)) * nx + gx) * blk
                    piece = lax.slice_in_dim(w, i * blk, (i + 1) * blk, axis=0)
                    out = lax.dynamic_update_slice_in_dim(out, piece, at, 0)
        return out

    def local(
        layer_input,
        query_weight,
        key_weight,
        value_weight,
        output_weight,
        gate_weight,
        up_weight,
        down_weight,
        attn_in_gain,
        attn_out_gain,
        ffn_in_gain,
        ffn_out_gain,
        out_cotangent,
        segment_ids,
        live_mask,
    ):
        rows, toks, width = layer_input.shape
        blk, qw = query_weight.shape
        kw = key_weight.shape[1]
        qkv_w = qw + 2 * kw
        mid = width // 2
        seq = Order()

        class ZSum:
            def __init__(self, part):
                self.own = lax.psum_scatter(
                    part, "tensor", scatter_dimension=0, tiled=True
                )

            def middle(self):
                (own,) = seq(self.own)
                seq.last = (own,)
                self.out = lax.all_gather(own, "tensor", axis=0, tiled=True)

        class Weight:
            def __init__(self, w):
                self.w = w
                if not square:
                    m = lax.all_gather(w, ("y", "ctx"), axis=0, tiled=True)
                    self.mine, self.other = [m], [to_core(m)]

            def near(self):
                if square:
                    w = self.w
                    self.mine = [w, seq.send(to_ctx, w), seq.send(to_y, w)]
                    self.other = [seq.send(to_core, w)]

            def far(self):
                if square:
                    h = blk // 2
                    wx, wy = seq(*self.mine[1:])
                    self.mine += [seq.send(to_y, wx[:h]), seq.send(to_ctx, wy[h:])]
                    self.other += [seq.send(to_core, wx), seq.send(to_core, wy)]

            def core(self):
                if square:
                    self.mine[3:] = seq(*self.mine[3:])
                    self.other += [seq.send(to_core, d) for d in self.mine[3:]]

        def settle(*values):
            values = seq(*values)
            seq.last = tuple(values)
            return list(values)

        def placed(*weights):
            pieces, where, col = [], [], 0
            for w in weights:
                at = 0
                for p in w.mine + w.other:
                    pieces.append(p)
                    where.append((at, col))
                    at += p.shape[0]
                col += w.w.shape[1]
            return pieces, where

        def packet_plan():
            pieces, plan, full, device = [], [], packet.w.shape[0], 0
            for side in (packet.mine, packet.other):
                at = 0
                for p in side:
                    i, r = 0, p.shape[0]
                    while i < r:
                        d, inside = divmod(at + i, full)
                        d += device
                        if inside < blk:
                            k = min(r - i, blk - inside)
                            plan.append((len(pieces), i, k, d * blk + inside, None))
                        else:
                            k = min(r - i, full - inside)
                            plan.append((len(pieces), i, k, None, d * 16))
                        i += k
                    at += r
                    pieces.append(p)
                device += plane
            return pieces, plan

        gains = jnp.stack([attn_in_gain, attn_out_gain, ffn_in_gain, ffn_out_gain])
        own = [query_weight, key_weight, value_weight, output_weight]
        own = jnp.concatenate(own, axis=1)
        gains = jnp.pad(gains, ((0, 12), (0, own.shape[1] - blk)))
        if square:
            flags = jnp.concatenate([segment_ids, live_mask], axis=0).astype(LOW)
            flags = jnp.pad(flags, ((0, 0), (0, own.shape[1] - toks)))
            gains = jnp.concatenate([gains[:4], flags, gains[6:]], axis=0)
        packet = Weight(jnp.concatenate([own, gains], axis=0))
        index = lax.axis_index("ctx") * toks + jnp.arange(toks, dtype=jnp.int32)
        own_info = jnp.concatenate([segment_ids, live_mask, index[None]], axis=0)

        def positions(info):
            seg_all, live_all, index_all = info[0:1], info[1:2], info[2:3]
            seg_col, index_col = segment_ids.reshape(toks, 1), index.reshape(toks, 1)
            start = jnp.sum((seg_all < seg_col).astype(jnp.int32), axis=1)
            allowed = (
                (index_all <= index_col)
                & (seg_all == seg_col)
                & ((live_all == 1) | (index_all == index_col))
            ).astype(LOW)
            freq = jnp.exp(
                jnp.arange(HD // 2, dtype=F32) * (-2.0 * math.log(10000.0) / HD)
            )
            angle = wide(index - start)[:, None] * freq
            return allowed, jnp.cos(angle), jnp.sin(angle)

        x_raw = layer_input.reshape(toks, width)
        dy_raw = out_cotangent.reshape(toks, width)
        wg, wu, wd = Weight(gate_weight), Weight(up_weight), Weight(down_weight)

        packet.near()
        if not square:
            info = lax.all_gather(own_info, "ctx", axis=1, tiled=True)
        x, factors = seq.run(order, x_raw, factors=True)
        packet.far()
        if square:

            def both_info(mine, wx):
                flags = wx[blk + 4 : blk + 6, :toks].astype(jnp.int32)
                there = mine[2:3] + (1 - 2 * lax.axis_index("ctx")) * toks
                return jnp.concatenate(
                    [mine, jnp.concatenate([flags, there], axis=0)], axis=1
                )

            info = seq.run(both_info, own_info, packet.mine[1])
        allowed, cos, sin = seq.run(positions, info)
        packet.core()
        wg.near()
        pieces, plan = packet_plan()
        h1, q, kv, gain, w_qkv, w_out = seq.run(
            first_kernel, x, factors, cos, sin, *pieces, plan=plan, blk=blk, qw=qw, kw=kw
        )
        g1, g2, g3, g4 = [gain[i : i + 1] for i in range(4)]
        if square:
            kv_got = seq.send(to_ctx, kv)
            wg.far()
            kv_all = seq.run(lambda a, b: jnp.concatenate([a, b], 0), kv, kv_got)
        else:
            kv_all = lax.all_gather(kv, "ctx", axis=0, tiled=True)
        length = kv_all.shape[0]

        o, logs, part = seq.run(attn_kernel, q, kv_all, allowed, w_out)
        za = ZSum(part)
        if square:
            wg.mine[3:] = settle(*wg.mine[3:])
        wu.near()
        wg.core()
        wu.far()
        za.middle()
        if square:
            wu.mine[3:] = settle(*wu.mine[3:])
        wd.near()
        wu.core()
        wd.far()
        gate_p, gate_at = placed(wg)
        up_p, up_at = placed(wu)
        x2, h3, gate_up, hid = seq.run(
            ffn_in_kernel, za.out, x, g2, g3, *gate_p, *up_p, gate_at=gate_at, up_at=up_at
        )
        wd.core()
        down_p, down_at = placed(wd)
        part = seq.run(project_kernel, hid, *down_p, at=down_at)
        zf = ZSum(part)
        zf.middle()
        dy = seq.run(order, dy_raw)
        qkv_g = seq.run(row_order, w_qkv)
        g1_g = seq.run(order, jnp.broadcast_to(g1, (16, width)), back=True)[:1]

        y, df, dgate, dup, dg4 = seq.run(
            ffn_back_kernel, zf.out, x2, dy, g4, gate_up, *down_p, at=down_at
        )
        part = seq.run(
            ffn_inputs_kernel, dgate, dup, *gate_p, *up_p, gate_at=gate_at, up_at=up_at
        )
        zd = ZSum(part)

        class Scatter:
            def __init__(self, a, b):
                self.ab = a, b

            def low(self):
                low = seq.run(outer_kernel, *self.ab, side=1, cuts=[mid // 2] * 2)
                self.got = [seq.send(to_core, v) for v in low]

            def first(self):
                h = blk // 2
                cuts = [blk] * 3 + [h, h] if square else [mid]
                self.s = seq.run(outer_kernel, *self.ab, *self.got, side=0, cuts=cuts)
                if square:
                    self.gx = seq.send(to_ctx, self.s[3])
                    self.gy = seq.send(to_y, self.s[4])

            def second(self):
                if not square:
                    self.rest = lax.psum_scatter(
                        self.s[0], ("y", "ctx"), scatter_dimension=0, tiled=True
                    )
                    return
                s1, s2 = seq.run(pass_kernel, *self.s[1:3], self.gx, self.gy)
                self.rest = seq.send(to_ctx, s1), seq.send(to_y, s2)

            def end(self):
                if not square:
                    return wide(self.rest)
                return seq.run(sum_kernel, self.s[0], *self.rest)

        sd, sg, su = Scatter(df, hid), Scatter(h3, dgate), Scatter(h3, dup)
        sd.low()
        sg.low()
        sd.first()
        su.low()
        sg.first()
        zd.middle()
        layer_output = seq.run(order, y, back=True)
        sd.second()
        su.got = settle(*su.got)

        dx2, da, dq, own, other, dg23 = seq.run(
            attn_back_kernel, zd.out, x2, dy, za.out, g3, g2, w_out,
            q, kv_all, allowed, logs, cos, sin, toks=toks,
        )
        if square:
            got = seq.send(to_ctx, other)
        else:
            got = lax.psum_scatter(other, "ctx", scatter_dimension=0, tiled=True)
            own = jnp.zeros_like(own)
        sg.second()
        down_grad = sd.end()
        dqkv = seq.run(keys_back_kernel, own, got, cos, sin, dq)
        part = seq.run(project_kernel, dqkv, qkv_g, at=[(0, 0)])
        z1 = ZSum(part)
        so, sq = Scatter(da, o), Scatter(h1, dqkv)
        su.first()
        so.low()
        sq.low()
        dx2 = seq.run(order, dx2, back=True)
        gate_grad = sg.end()
        su.second()
        z1.middle()
        so.first()
        sq.first()
        so.second()
        sq.second()
        input_grad, dg1 = seq.run(last_kernel, x_raw, g1_g, z1.out, dx2)
        dg1 = seq.run(order, jnp.broadcast_to(dg1, (16, width)))[:1]
        dgain = jnp.concatenate([dg1, dg23[:2], dg4], axis=0)
        got = seq.send(to_core, dgain[:, mid:])
        up_grad = su.end()
        dgain = seq.run(lambda a, b: a[:, :mid] + b, dgain, got)
        if square:
            got = seq.send(to_y, dgain[:, mid // 2 :])
            out_grad, qkv_grad = so.end(), sq.end()
            dgain = seq.run(lambda a, b: a[:, : mid // 2] + b, dgain, got)
            dgain = dgain[:, :blk] + to_ctx(dgain[:, blk:])
        else:
            out_grad, qkv_grad = so.end(), sq.end()
            dgain = lax.psum_scatter(
                dgain, ("y", "ctx"), scatter_dimension=1, tiled=True
            )
        return (
            layer_output.reshape(rows, toks, width),
            input_grad.reshape(rows, toks, width),
            qkv_grad[:, :qw],
            qkv_grad[:, qw : qw + kw],
            qkv_grad[:, qw + kw :],
            out_grad,
            gate_grad,
            up_grad,
            down_grad,
            dgain[0],
            dgain[1],
            dgain[2],
            dgain[3],
        )

    return local


def solution(mesh):
    dp, nx, nz = (mesh.shape[a] for a in ("dp", "ctx", "tensor"))
    fine = Mesh(
        mesh.devices.reshape(dp // 2, 2, nx, nz), ("y", "core", "ctx", "tensor")
    )
    d = ("y", "core")
    w = P(("y", "core", "ctx"), "tensor")
    g = P(("y", "core", "ctx"))
    t = P(d, "ctx", None)
    return jax.shard_map(
        make_local(dp // 2, nx, nz),
        mesh=fine,
        in_specs=(t, w, w, w, w, w, w, w, g, g, g, g, t, P(d, "ctx"), P(d, "ctx")),
        out_specs=(t, t, w, w, w, w, w, w, w, g, g, g, g),
        check_vma=False,
    )
```

```python
import math

import jax
import jax.numpy as jnp
from jax import lax
from jax.experimental import pallas as pl
from jax.experimental.pallas import tpu as pltpu
from jax.sharding import Mesh
from jax.sharding import PartitionSpec as P

HD = 256
NORM_EPSILON = 1e-06
SOFT_CAP = 50.0
MASKED_SCORE = -1e30
SWAP = [(0, 1), (1, 0)]
LOW = jnp.bfloat16
F32 = jnp.float32
VMEM_MB = 56
NO_COST = pl.CostEstimate(flops=0, bytes_accessed=0, transcendentals=0)
LONG = pl.CostEstimate(flops=10**12, bytes_accessed=0, transcendentals=0)


def wide(a):
    return a.astype(F32)


def after(value, *deps):
    return lax.optimization_barrier((value,) + deps)[0]


class Order:
    def __init__(self):
        self.last = ()

    def __call__(self, *values):
        return after(values, *self.last) if self.last else values

    def run(self, fn, *values, **kw):
        out = fn(*self(*values), **kw)
        self.last = (out,)
        return out

    def send(self, move, value):
        (value,) = self(value)
        self.last = (value,)
        return move(value)


def to_ctx(a):
    return lax.ppermute(a, "ctx", SWAP)


def to_y(a):
    return lax.ppermute(a, "y", SWAP)


def to_core(a):
    return lax.ppermute(a, "core", SWAP)


def nn(a, b):
    return jnp.dot(a, b, preferred_element_type=F32)


def nt(a, b):
    return lax.dot_general(a, b, (((1,), (1,)), ((), ())), preferred_element_type=F32)


def tn(a, b):
    return lax.dot_general(a, b, (((0,), (0,)), ((), ())), preferred_element_type=F32)


def norm_factor(v):
    return lax.rsqrt(jnp.mean(v * v, axis=-1, keepdims=True) + NORM_EPSILON)


def over_rows(rows, step, carry=None, block=64):
    block = math.gcd(rows, block)
    at = lambda i: pl.ds(pl.multiple_of(i * block, block), block)
    return lax.fori_loop(0, rows // block, lambda i, c: step(at(i), c), carry)


def fold(v):
    return sum(v[i : i + 8] for i in range(0, v.shape[0], 8))


def norm_back_rows(v, gain, grad):
    r = norm_factor(v)
    w = (1.0 + gain) * grad
    vr = v * r
    dv = r * (w - vr * jnp.mean(vr * w, axis=-1, keepdims=True))
    return dv, fold(grad * vr)


def gelu_parts(u):
    k = math.sqrt(2.0 / math.pi)
    th = jnp.tanh(k * (u + 0.044715 * u * u * u))
    g = 0.5 * u * (1.0 + th)
    dg = 0.5 * (1.0 + th) + 0.5 * u * (1.0 - th * th) * k * (1.0 + 3 * 0.044715 * u * u)
    return g, dg


def turn(v, c, s):
    h = HD // 2
    a, b = v[:, :h], v[:, h:]
    return jnp.concatenate([a * c - b * s, b * c + a * s], axis=1)


def turn_back(v, c, s):
    h = HD // 2
    a, b = v[:, :h], v[:, h:]
    return jnp.concatenate([a * c + b * s, b * c - a * s], axis=1)


def spec(block, index, mode=None):
    return pl.BlockSpec(block, index, pipeline_mode=mode)


def kernel(body, grid, ins, outs, scratch=(), cost=NO_COST):
    return pl.pallas_call(
        body,
        grid=grid,
        in_specs=[spec(*e[1:]) for e in ins],
        out_specs=[spec(*e[2:]) for e in outs],
        out_shape=[jax.ShapeDtypeStruct(*e[:2]) for e in outs],
        scratch_shapes=list(scratch),
        cost_estimate=cost,
        name=body.__qualname__.split(".")[0],
        compiler_params=pltpu.CompilerParams(vmem_limit_bytes=VMEM_MB * 2**20),
    )(*[e[0] for e in ins])


def all_of(shape):
    return tuple(shape), lambda *i: (0,) * len(shape), pl.Buffered(1)


def first_kernel(x, r, cos, sin, *pieces, plan, blk, qw, kw):
    toks, width = x.shape
    wide_w = pieces[0].shape[1]
    cols = qw + 2 * kw
    devices = width // blk
    lanes = -(-blk // 128) * 128
    scale = 1.0 / math.sqrt(HD)
    n = len(pieces)

    def body(x_r, r_r, c_r, s_r, *refs):
        piece_h = refs[:n]
        h_h, q_r, kv_r, g_r, w_h, o_h = refs[n : n + 6]
        h_r, w_r, raw_g_r, sems = refs[n + 6 :]
        c = Copies(sems)
        for k, (p, r0, rows, at, gain_at) in enumerate(plan):
            if at is None:
                src = piece_h[p].at[pl.ds(r0, rows), pl.ds(0, lanes)]
                c.start(("g", k), src, raw_g_r.at[pl.ds(gain_at, rows)])
        for k, (p, r0, rows, at, gain_at) in enumerate(plan):
            if at is not None:
                c.start(("w", k), piece_h[p].at[pl.ds(r0, rows)], w_r.at[pl.ds(at, rows)])
        c.wait(*[k for k in c.known if k[0] == "g"])
        rows16 = raw_g_r[...]
        gains = [rows16[d * 16 : d * 16 + 8, :blk] for d in range(devices)]
        gains = wide(jnp.concatenate(gains, axis=1))
        g_r[...] = gains
        g1 = 1.0 + gains[0:1]

        def normed(at, _):
            h_r[at, :] = (wide(x_r[at, :]) * r_r[at, 0:1] * g1).astype(LOW)

        over_rows(toks, normed)
        c.start("h", h_r, h_h)
        c.wait(*[k for k in c.known if k[0] == "w"])
        c.start("qkv", w_r.at[:, pl.ds(0, cols)], w_h)
        c.start("out", w_r.at[:, pl.ds(cols, wide_w - cols)], o_h)
        raw = nn(h_r[...], w_r[:, :cols])
        co, si = c_r[...], s_r[...]
        for j in range(qw // HD):
            cut = slice(j * HD, (j + 1) * HD)
            q_r[:, cut] = (turn(raw[:, cut], co, si) * scale).astype(LOW)
        for j in range(kw // HD):
            cut = slice(j * HD, (j + 1) * HD)
            k = turn(raw[:, qw + j * HD : qw + (j + 1) * HD], co, si)
            kv_r[:, cut] = k.astype(LOW)
        kv_r[:, kw:] = raw[:, qw + kw :].astype(LOW)
        c.wait("h", "qkv", "out")

    ins = [(v, "vmem") for v in (x, r, cos, sin)] + [(p, "hbm") for p in pieces]
    outs = [
        ((toks, width), LOW, "hbm"),
        ((toks, qw), LOW, "vmem"),
        ((toks, 2 * kw), LOW, "vmem"),
        ((8, width), F32, "vmem"),
        ((width, cols), LOW, "hbm"),
        ((width, wide_w - cols), LOW, "hbm"),
    ]
    scratch = [((toks, width), LOW), ((width, wide_w), LOW), ((16 * devices, lanes), LOW)]
    return streaming(body, ins, outs, scratch, len(plan) + 3, LONG)


def query_block(rows, length):
    return min(rows, 256 if length <= 2048 else 128)


def attn_kernel(q, kv, allowed, w):
    rows, qw = q.shape
    length = kv.shape[0]
    width = w.shape[0]
    qb = query_block(rows, length)
    heads = qw // HD

    def body(q_r, kv_r, m_r, w_r, o_r, t_r, a_r):
        ok = m_r[...] > 0
        k, v = kv_r[:, :HD], kv_r[:, HD:]
        logs = []
        for j in range(heads):
            cut = slice(j * HD, (j + 1) * HD)
            b = jnp.tanh(nt(q_r[:, cut], k) * (1.0 / SOFT_CAP))
            c = jnp.where(ok, SOFT_CAP * b, MASKED_SCORE)
            peak = jnp.max(c, axis=-1, keepdims=True)
            e = jnp.exp(c - peak)
            total = jnp.sum(e, axis=-1, keepdims=True)
            p = (e / total).astype(LOW)
            o_r[:, cut] = nn(p, v).astype(LOW)
            logs.append(jnp.broadcast_to(peak + jnp.log(total), (qb, 128)))
        t_r[...] = jnp.concatenate(logs, axis=1)
        a_r[...] = nt(o_r[...], w_r[...]).astype(LOW)

    row = lambda n: ((qb, n), lambda i: (i, 0))
    ins = [(q, *row(qw)), (kv, *all_of(kv.shape)), (allowed, *row(length))]
    ins += [(w, *all_of(w.shape))]
    outs = [
        ((rows, qw), LOW, *row(qw)),
        ((rows, 128 * heads), F32, *row(128 * heads)),
        ((rows, width), LOW, *row(width)),
    ]
    return kernel(body, (rows // qb,), ins, outs, cost=LONG)


def probs_kernel(q, kv, allowed, logs):
    rows, qw = q.shape
    length = kv.shape[0]
    qb = query_block(rows, length)
    heads = qw // HD

    def body(q_r, kv_r, m_r, t_r, p_r, s_r):
        ok = m_r[...] > 0
        for j in range(heads):
            b = jnp.tanh(nt(q_r[:, j * HD : (j + 1) * HD], kv_r[:, :HD]) * (1.0 / SOFT_CAP))
            logit = jnp.where(ok, SOFT_CAP * b, MASKED_SCORE)
            p = jnp.exp(logit - t_r[:, j * 128 : j * 128 + 1])
            keys = slice(j * length, (j + 1) * length)
            p_r[:, keys] = p.astype(LOW)
            s_r[:, keys] = (p * (1.0 - b * b)).astype(LOW)

    row = lambda n: ((qb, n), lambda i: (i, 0))
    ins = [(q, *row(qw)), (kv, *all_of(kv.shape)), (allowed, *row(length))]
    ins += [(logs, *row(128 * heads))]
    outs = [((rows, heads * length), LOW, *row(heads * length))] * 2
    return kernel(body, (rows // qb,), ins, outs)


def attn_back_kernel(
    dh3, x2, dy, a, g3, g2, w, q, kv, p, slope, cos, sin, toks
):
    rows, width = x2.shape
    qw = q.shape[1]
    length = kv.shape[0]
    qb = query_block(rows, length)
    heads = qw // HD
    other = toks if length == 2 * toks else length
    scale = 1.0 / math.sqrt(HD)

    def body(
        d_r, x_r, dy_r, a_r, g3_r, g2_r, w_r, q_r, kv_r, p_r, t_r, c_r, s_r,
        dx_r, da_r, dq_r, own_r, other_r, dg_r, dkv_r,
    ):
        @pl.when(pl.program_id(0) == 0)
        def _():
            dkv_r[...] = jnp.zeros_like(dkv_r)
            dg_r[...] = jnp.zeros_like(dg_r)

        def step(at, total):
            dv3, dg3 = norm_back_rows(x_r[at, :], g3_r[...], wide(d_r[at, :]))
            dx2 = wide(dy_r[at, :]) + dv3
            dx_r[at, :] = dx2
            da, dg2 = norm_back_rows(wide(a_r[at, :]), g2_r[...], dx2)
            da_r[at, :] = da.astype(LOW)
            return total[0] + dg2, total[1] + dg3

        none = jnp.zeros((8, width), F32)
        dg2, dg3 = over_rows(qb, step, (none, none))
        dg_r[0:1] += jnp.sum(dg2, axis=0, keepdims=True)
        dg_r[1:2] += jnp.sum(dg3, axis=0, keepdims=True)
        do = nn(da_r[...], w_r[...]).astype(LOW)
        k, v = kv_r[:, :HD], kv_r[:, HD:]
        c, s = c_r[...], s_r[...]
        dk = dv = 0.0
        for j in range(heads):
            cut = slice(j * HD, (j + 1) * HD)
            qj, doj = q_r[:, cut], do[:, cut]
            keys = slice(j * length, (j + 1) * length)
            p = p_r[:, keys]
            dp = nt(doj, v)
            dp = dp - jnp.sum(wide(p) * dp, axis=-1, keepdims=True)
            ds = (wide(t_r[:, keys]) * dp).astype(LOW)
            dq_r[:, cut] = (turn_back(nn(ds, k), c, s) * scale).astype(LOW)
            dk = dk + tn(ds, qj)
            dv = dv + tn(p, doj)
        dkv_r[:, :HD] += dk
        dkv_r[:, HD:] += dv

        @pl.when(pl.program_id(0) == rows // qb - 1)
        def _():
            own_r[...] = dkv_r[:toks]
            other_r[...] = dkv_r[length - other :].astype(LOW)

    row = lambda n: ((qb, n), lambda i: (i, 0))
    ins = [(v, *row(width)) for v in (dh3, x2, dy, a)]
    ins += [(v, *all_of(v.shape)) for v in (g3, g2, w)]
    ins += [(q, *row(qw)), (kv, *all_of(kv.shape)), (p, *row(p.shape[1]))]
    ins += [(slope, *row(p.shape[1])), (cos, *row(HD // 2)), (sin, *row(HD // 2))]
    outs = [
        ((rows, width), F32, *row(width)),
        ((rows, width), LOW, *row(width)),
        ((rows, qw), LOW, *row(qw)),
        ((toks, 2 * HD), F32, *all_of((toks, 2 * HD))),
        ((other, 2 * HD), LOW, *all_of((other, 2 * HD))),
        ((8, width), F32, *all_of((8, width))),
    ]
    scratch = [pltpu.VMEM((length, 2 * HD), F32)]
    return kernel(body, (rows // qb,), ins, outs, scratch, LONG)


class Copies:
    def __init__(self, sems):
        self.sems, self.known = sems, {}

    def start(self, name, src, dst):
        self.known[name] = pltpu.make_async_copy(src, dst, self.sems.at[len(self.known)])
        self.known[name].start()

    def wait(self, *names):
        for name in names:
            self.known[name].wait()


def streaming(body, ins, outs, scratch, copies, cost=NO_COST):
    place = {"vmem": pl.BlockSpec(memory_space=pltpu.VMEM), "hbm": pl.BlockSpec(memory_space=pltpu.HBM)}
    return pl.pallas_call(
        body,
        in_specs=[place[p] for _, p in ins],
        out_specs=[place[p] for _, _, p in outs],
        out_shape=[jax.ShapeDtypeStruct(s, d) for s, d, _ in outs],
        scratch_shapes=[pltpu.VMEM(*v) for v in scratch]
        + [pltpu.SemaphoreType.DMA((copies,))],
        cost_estimate=cost,
        name=body.__qualname__.split(".")[0],
        compiler_params=pltpu.CompilerParams(vmem_limit_bytes=VMEM_MB * 2**20),
    )(*[a for a, _ in ins])


def row_parts(rows, block=128):
    return [pl.ds(i, min(block, rows)) for i in range(0, rows, min(block, rows))]


def col_chunks(where, total, most=768):
    starts = sorted({c for _, c in where}) + [total]
    chunks = []
    for lo, hi in zip(starts, starts[1:]):
        while lo < hi:
            n = hi - lo if hi - lo <= most else min(most, -(-(hi - lo) // 2 // 128) * 128)
            chunks.append((lo, n))
            lo += n
    return chunks


def start_cols(c, name, j, chunk, pieces, shapes, where, dst):
    names, (lo, n) = [], chunk
    for i, (p, s, (row, col)) in enumerate(zip(pieces, shapes, where)):
        if col <= lo < col + s[1]:
            src = p.at[:, pl.ds(lo - col, n)]
            c.start((name, j, i), src, dst.at[pl.ds(row, s[0]), pl.ds(lo, n)])
            names.append((name, j, i))
    return names


def start_rows(c, name, pieces, shapes, where, dst):
    names = []
    for i in sorted(range(len(pieces)), key=lambda i: where[i]):
        (row, col), s = where[i], shapes[i]
        c.start((name, i), pieces[i], dst.at[pl.ds(row, s[0]), pl.ds(col, s[1])])
        names.append((row, row + s[0], (name, i)))
    return names


def wait_rows(c, names, lo, hi, seen):
    for first, last, name in names:
        if first < hi and last > lo and name not in seen:
            seen.add(name)
            c.wait(name)


def row_groups(rows, most=768):
    return [(i, min(most, rows - i)) for i in range(0, rows, most)]


def ffn_in_kernel(a, x, g2, g3, *weights, gate_at, up_at):
    rows, width = x.shape
    ng = len(gate_at)
    shapes = [w.shape for w in weights]
    units = shapes[-1][1]
    parts = row_parts(rows)
    chunks = col_chunks(gate_at, units)

    def body(a_h, x_h, g2_r, g3_r, *refs):
        w_h, refs = refs[: len(shapes)], refs[len(shapes) :]
        x2_h, h_h, gu_h, hid_h = refs[:4]
        a_r, x_r, x2_r, h_r, wg_r, wu_r, gu_r, hid_r, sems = refs[4:]
        c = Copies(sems)
        for i, at in enumerate(parts):
            c.start(("a", i), a_h.at[at], a_r.at[at])
            c.start(("x", i), x_h.at[at], x_r.at[at])
        need = []
        for j, chunk in enumerate(chunks):
            names = start_cols(c, "g", j, chunk, w_h[:ng], shapes[:ng], gate_at, wg_r)
            names += start_cols(c, "u", j, chunk, w_h[ng:], shapes[ng:], up_at, wu_r)
            need.append(names)
        out = []

        def send(src, dst, at):
            out.append(("out", len(out)))
            c.start(out[-1], src.at[at], dst.at[at])

        for i, part in enumerate(parts):
            c.wait(("a", i), ("x", i))

            def normed(at, _, first=part.start):
                at = pl.ds(pl.multiple_of(first + at.start, 16), at.size)
                av = wide(a_r[at, :])
                x2 = wide(x_r[at, :]) + av * norm_factor(av) * (1.0 + g2_r[...])
                x2_r[at, :] = x2
                h_r[at, :] = (x2 * norm_factor(x2) * (1.0 + g3_r[...])).astype(LOW)

            over_rows(part.size, normed)
            send(x2_r, x2_h, (part,))
            send(h_r, h_h, (part,))
        for names, (lo, n) in zip(need, chunks):
            c.wait(*names)
            at = pl.ds(lo, n)
            h = h_r[...]
            gate, up = nn(h, wg_r[:, at]), nn(h, wu_r[:, at])
            at2 = pl.ds(units + lo, n)
            gu_r[:, at] = gate.astype(LOW)
            gu_r[:, at2] = up.astype(LOW)
            hid_r[:, at] = (gelu_parts(gate)[0] * up).astype(LOW)
            for src, dst, cut in ((gu_r, gu_h, at), (gu_r, gu_h, at2), (hid_r, hid_h, at)):
                send(src, dst, (slice(None), cut))
        c.wait(*out)

    t, n = (rows, width), (rows, units)
    ins = [(a, "hbm"), (x, "hbm"), (g2, "vmem"), (g3, "vmem")]
    ins += [(w, "hbm") for w in weights]
    gu = (rows, 2 * units)
    outs = [(t, F32, "hbm"), (t, LOW, "hbm"), (gu, LOW, "hbm"), (n, LOW, "hbm")]
    w = (width, units)
    scratch = [(t, LOW), (t, LOW), (t, F32), (t, LOW), (w, LOW), (w, LOW)]
    scratch += [(gu, LOW), (n, LOW)]
    copies = 4 * len(parts) + (3 + len(weights)) * len(chunks)
    return streaming(body, ins, outs, scratch, copies)


def project_kernel(u, *weights, at):
    rows, cols = u.shape
    shapes = [w.shape for w in weights]
    width = sum(s[0] for s in shapes)
    groups = row_groups(width)

    def body(u_r, *refs):
        w_h, (o_h, w_r, o_r, sems) = refs[: len(shapes)], refs[len(shapes) :]
        c = Copies(sems)
        names, seen = start_rows(c, "w", w_h, shapes, at, w_r), set()
        for g, (lo, n) in enumerate(groups):
            wait_rows(c, names, lo, lo + n, seen)
            cut = pl.ds(lo, n)
            o_r[:, cut] = nt(u_r[...], w_r[cut, :]).astype(LOW)
            c.start(("out", g), o_r.at[:, cut], o_h.at[:, cut])
        c.wait(*[("out", g) for g in range(len(groups))])

    ins = [(u, "vmem")] + [(w, "hbm") for w in weights]
    outs = [((rows, width), LOW, "hbm")]
    scratch = [((width, cols), LOW), ((rows, width), LOW)]
    return streaming(body, ins, outs, scratch, len(weights) + len(groups))[0]


def ffn_back_kernel(f, x2, dy, g4, gate_up, *weights, at):
    rows, width = x2.shape
    units = gate_up.shape[1] // 2
    shapes = [w.shape for w in weights]
    parts = row_parts(rows)
    chunks = col_chunks(at, units, 1152)

    def body(f_h, x2_h, dy_h, g4_r, gu_h, *refs):
        w_h, refs = refs[: len(shapes)], refs[len(shapes) :]
        y_h, df_h, dg_h, du_h, g_r = refs[:5]
        f_r, x2_r, dy_r, gate_r, up_r, w_r, y_r, df_r, dg_r, du_r, sems = refs[5:]
        c = Copies(sems)
        for i, part in enumerate(parts):
            for name, src, dst in (("f", f_h, f_r), ("x", x2_h, x2_r), ("d", dy_h, dy_r)):
                c.start((name, i), src.at[part], dst.at[part])
        need = []
        for j, (lo, n) in enumerate(chunks):
            names = start_cols(c, "w", j, (lo, n), w_h, shapes, at, w_r)
            cut = pl.ds(lo, n)
            c.start(("gate", j), gu_h.at[:, cut], gate_r.at[:, cut])
            up_at = pl.ds(units + lo, n)
            c.start(("up", j), gu_h.at[:, up_at], up_r.at[:, cut])
            need.append(names + [("gate", j), ("up", j)])
        out = []

        def send(src, dst, cut):
            out.append(("out", len(out)))
            c.start(out[-1], src.at[cut], dst.at[cut])

        total = jnp.zeros((8, width), F32)
        for i, part in enumerate(parts):
            c.wait(("f", i), ("x", i), ("d", i))

            def step(cut, total, first=part.start):
                cut = pl.ds(pl.multiple_of(first + cut.start, 16), cut.size)
                fv, g4v, x2v = wide(f_r[cut, :]), g4_r[...], x2_r[cut, :]
                y_r[cut, :] = (x2v + fv * norm_factor(fv) * (1.0 + g4v)).astype(LOW)
                df, dg = norm_back_rows(fv, g4v, wide(dy_r[cut, :]))
                df_r[cut, :] = df.astype(LOW)
                return total + dg

            total = over_rows(part.size, step, total)
            send(y_r, y_h, (part,))
            send(df_r, df_h, (part,))
        g_r[...] = jnp.sum(total, axis=0, keepdims=True)
        for names, (lo, n) in zip(need, chunks):
            c.wait(*names)
            cut = pl.ds(lo, n)
            dh = nn(df_r[...], w_r[:, cut])
            gl, dgl = gelu_parts(wide(gate_r[:, cut]))
            dg_r[:, cut] = (dh * wide(up_r[:, cut]) * dgl).astype(LOW)
            du_r[:, cut] = (dh * gl).astype(LOW)
            send(dg_r, dg_h, (slice(None), cut))
            send(du_r, du_h, (slice(None), cut))
        c.wait(*out)

    t, n = (rows, width), (rows, units)
    ins = [(v, "hbm") for v in (f, x2, dy)] + [(g4, "vmem")]
    ins += [(v, "hbm") for v in (gate_up, *weights)]
    outs = [(t, LOW, "hbm"), (t, LOW, "hbm"), (n, LOW, "hbm"), (n, LOW, "hbm")]
    outs += [((1, width), F32, "vmem")]
    scratch = [(t, LOW), (t, F32), (t, LOW), (n, LOW), (n, LOW), ((width, units), LOW)]
    scratch += [(t, LOW), (t, LOW), (n, LOW), (n, LOW)]
    copies = 5 * len(parts) + (4 + len(weights)) * len(chunks)
    return streaming(body, ins, outs, scratch, copies)


def ffn_inputs_kernel(dg, du, *weights, gate_at, up_at):
    rows, units = dg.shape
    ng = len(gate_at)
    shapes = [w.shape for w in weights]
    width = sum(s[0] for s in shapes[ng:])
    groups = row_groups(width)

    def body(dg_r, du_r, *refs):
        w_h, (o_h, wg_r, wu_r, o_r, sems) = refs[: len(shapes)], refs[len(shapes) :]
        c = Copies(sems)
        order = sorted(range(len(shapes)), key=lambda i: (gate_at + up_at)[i][0])
        names, seen = [], set()
        for i in order:
            (row, col), s = (gate_at + up_at)[i], shapes[i]
            dst = (wg_r if i < ng else wu_r).at[pl.ds(row, s[0]), pl.ds(col, s[1])]
            c.start(("w", i), w_h[i], dst)
            names.append((row, row + s[0], ("w", i)))
        for g, (lo, n) in enumerate(groups):
            wait_rows(c, names, lo, lo + n, seen)
            cut = pl.ds(lo, n)
            v = nt(dg_r[...], wg_r[cut, :]) + nt(du_r[...], wu_r[cut, :])
            o_r[:, cut] = v.astype(LOW)
            c.start(("out", g), o_r.at[:, cut], o_h.at[:, cut])
        c.wait(*[("out", g) for g in range(len(groups))])

    ins = [(dg, "vmem"), (du, "vmem")] + [(w, "hbm") for w in weights]
    outs = [((rows, width), LOW, "hbm")]
    w = ((width, units), LOW)
    scratch = [w, w, ((rows, width), LOW)]
    return streaming(body, ins, outs, scratch, len(weights) + len(groups))[0]


def outer_kernel(a, b, *got, side, cuts, cost=NO_COST):
    toks, cols = b.shape
    mid = a.shape[1] // 2
    bn = math.gcd(cols, 768)
    chunks = [pl.ds(i, bn) for i in range(0, cols, bn)]
    n, m = len(got), len(cuts)
    at = [sum(cuts[:i]) for i in range(m)]
    step = mid // n if n else 0

    def body(a_h, b_h, *refs):
        got_h, out_h = refs[:n], refs[n : n + m]
        a_r, b_r, got_r, out_r, sems = refs[n + m :]
        c = Copies(sems)
        c.start("a", a_h.at[:, pl.ds(side * mid, mid)], a_r)
        for j, part in enumerate(chunks):
            c.start(("b", j), b_h.at[:, part], b_r.at[:, part])
        for i in range(n):
            c.start(("got", i), got_h[i], got_r.at[pl.ds(i * step, step)])
        c.wait("a")
        for j, part in enumerate(chunks):
            c.wait(("b", j))
            v = tn(a_r[...], b_r[:, part])
            if n:
                if j == 0:
                    c.wait(*[("got", i) for i in range(n)])
                v = v + wide(got_r[:, part])
            out_r[:, part] = v.astype(LOW)
            for i in range(m):
                c.start(
                    ("out", i, j),
                    out_r.at[pl.ds(at[i], cuts[i]), part],
                    out_h[i].at[:, part],
                )
        c.wait(*[("out", i, j) for i in range(m) for j in range(len(chunks))])

    ins = [(v, "hbm") for v in (a, b, *got)]
    outs = [((r, cols), LOW, "hbm") for r in cuts]
    full = (mid, cols)
    scratch = [((toks, mid), LOW), ((toks, cols), LOW)]
    scratch += [(full if n else (16, 128), LOW), (full, LOW)]
    copies = 1 + len(chunks) * (1 + m) + n
    return streaming(body, ins, outs, scratch, copies, cost)


def sum_kernel(s, rx, ry):
    rows, cols = s.shape
    bc = math.gcd(cols, 768)

    def body(s_r, x_r, y_r, o_r):
        o_r[...] = wide(s_r[...]) + wide(x_r[...]) + wide(y_r[...])

    tile = ((rows, bc), lambda j: (0, j))
    ins = [(v, *tile) for v in (s, rx, ry)]
    return kernel(body, (cols // bc,), ins, [((rows, cols), F32, *tile)])[0]


def pass_kernel(s1, s2, gx, gy):
    rows, cols = s1.shape
    h = rows // 2
    bc = math.gcd(cols, 768)

    def body(s1_r, s2_r, gx_r, gy_r, t1_r, t2_r):
        t1_r[:h] = s1_r[:h]
        t1_r[h:] = (wide(s1_r[h:]) + wide(gy_r[...])).astype(LOW)
        t2_r[:h] = (wide(s2_r[:h]) + wide(gx_r[...])).astype(LOW)
        t2_r[h:] = s2_r[h:]

    full, part = ((rows, bc), lambda j: (0, j)), ((h, bc), lambda j: (0, j))
    ins = [(s1, *full), (s2, *full), (gx, *part), (gy, *part)]
    return kernel(body, (cols // bc,), ins, [(s1.shape, LOW, *full)] * 2)


def last_kernel(x, gain, dh1, dx2):
    rows, width = x.shape
    br = min(rows, 128)

    def body(x_r, g_r, d_r, dx_r, o_r, dg_r):
        def step(at, total):
            dv, dg = norm_back_rows(wide(x_r[at, :]), g_r[...], wide(d_r[at, :]))
            o_r[at, :] = dx_r[at, :] + dv
            return total + dg

        @pl.when(pl.program_id(0) == 0)
        def _():
            dg_r[...] = jnp.zeros_like(dg_r)

        total = over_rows(br, step, jnp.zeros((8, width), F32))
        dg_r[...] += jnp.sum(total, axis=0, keepdims=True)

    row = ((br, width), lambda i: (i, 0))
    ins = [(x, *row), (gain, *all_of(gain.shape)), (dh1, *row), (dx2, *row)]
    outs = [((rows, width), F32, *row), ((1, width), F32, *all_of((1, width)))]
    return kernel(body, (rows // br,), ins, outs)


def order_kernel(v, bits, back, ny, nx, factors=False):
    rows, width = v.shape
    blk = width // (2 * ny * nx)
    br = min(rows, 128)
    here = lambda c, y, x: (c * ny + y) * nx + x
    there = lambda c, y, x: (y * 2 + c) * nx + x
    keys = [(c, y, x) for c in range(2) for y in range(ny) for x in range(nx)]
    src, dst = (here, there) if back else (there, here)
    flips = 3 if ny == 2 and nx == 2 else 1

    def body(b_r, v_r, o_r, *f_r):
        def step(at, _):
            rows_ = v_r[at, :]
            if factors:
                f = norm_factor(wide(rows_))
                f_r[0][at, :] = jnp.broadcast_to(f, (f.shape[0], 128))
            cut = lambda j: rows_[:, j * blk : (j + 1) * blk]
            parts = {k: cut(src(*k)) for k in keys}
            for pos in range(flips):
                on = b_r[pos] == 0
                flip = lambda k: tuple(1 - e if i == pos else e for i, e in enumerate(k))
                parts = {k: jnp.where(on, parts[k], parts[flip(k)]) for k in keys}
            o_r[at, :] = jnp.concatenate([parts[k] for k in sorted(keys, key=lambda k: dst(*k))], axis=1)

        over_rows(br, step)

    tile = pl.BlockSpec((br, width), lambda i: (i, 0))
    return pl.pallas_call(
        body,
        grid=(rows // br,),
        in_specs=[pl.BlockSpec(memory_space=pltpu.SMEM), tile],
        out_specs=[tile, pl.BlockSpec((br, 128), lambda i: (i, 0))][: 1 + factors],
        out_shape=[
            jax.ShapeDtypeStruct(v.shape, v.dtype),
            jax.ShapeDtypeStruct((rows, 128), F32),
        ][: 1 + factors],
        cost_estimate=NO_COST,
    )(bits, v)


def keys_back_kernel(own, got, cos, sin, dq):
    qw = dq.shape[1]

    def body(a_r, b_r, c_r, s_r, q_r, o_r):
        v = a_r[...] + wide(b_r[...])
        o_r[:, :qw] = q_r[...]
        o_r[:, qw : qw + HD] = turn_back(v[:, :HD], c_r[...], s_r[...]).astype(LOW)
        o_r[:, qw + HD :] = v[:, HD:].astype(LOW)

    ins = [(v, *all_of(v.shape)) for v in (own, got, cos, sin, dq)]
    shape = (own.shape[0], qw + own.shape[1])
    return kernel(body, (1,), ins, [(shape, LOW, *all_of(shape))])[0]


def make_local(ny, nx, nz):
    square = ny == 2 and nx == 2
    plane = ny * nx

    def order(v, back=False, factors=False):
        bits = jnp.stack([lax.axis_index(a) for a in ("core", "y", "ctx")])
        out = order_kernel(v, bits.astype(jnp.int32), back, ny, nx, factors)
        return out if factors else out[0]

    def row_order(w):
        blk = w.shape[0] // (2 * plane)
        c = lax.axis_index("core")
        out = jnp.zeros_like(w)
        for half in range(2):
            for y in range(ny):
                for x in range(nx):
                    i = (half * ny + y) * nx + x
                    gy, gx = y, x
                    if square:
                        gy, gx = y ^ lax.axis_index("y"), x ^ lax.axis_index("ctx")
                    at = ((gy * 2 + (c ^ half)) * nx + gx) * blk
                    piece = lax.slice_in_dim(w, i * blk, (i + 1) * blk, axis=0)
                    out = lax.dynamic_update_slice_in_dim(out, piece, at, 0)
        return out

    def local(
        layer_input,
        query_weight,
        key_weight,
        value_weight,
        output_weight,
        gate_weight,
        up_weight,
        down_weight,
        attn_in_gain,
        attn_out_gain,
        ffn_in_gain,
        ffn_out_gain,
        out_cotangent,
        segment_ids,
        live_mask,
    ):
        rows, toks, width = layer_input.shape
        blk, qw = query_weight.shape
        kw = key_weight.shape[1]
        qkv_w = qw + 2 * kw
        mid = width // 2
        seq = Order()

        class ZSum:
            def __init__(self, part):
                self.own = lax.psum_scatter(
                    part, "tensor", scatter_dimension=0, tiled=True
                )

            def middle(self):
                (own,) = seq(self.own)
                seq.last = (own,)
                self.out = lax.all_gather(own, "tensor", axis=0, tiled=True)

        class Weight:
            def __init__(self, w):
                self.w = w
                if not square:
                    m = lax.all_gather(w, ("y", "ctx"), axis=0, tiled=True)
                    self.mine, self.other = [m], [to_core(m)]

            def near(self):
                if square:
                    w = self.w
                    self.mine = [w, seq.send(to_ctx, w), seq.send(to_y, w)]
                    self.other = [seq.send(to_core, w)]

            def far(self):
                if square:
                    h = blk // 2
                    wx, wy = seq(*self.mine[1:])
                    self.mine += [seq.send(to_y, wx[:h]), seq.send(to_ctx, wy[h:])]
                    self.other += [seq.send(to_core, wx), seq.send(to_core, wy)]

            def core(self):
                if square:
                    self.mine[3:] = seq(*self.mine[3:])
                    self.other += [seq.send(to_core, d) for d in self.mine[3:]]

        def settle(*values):
            values = seq(*values)
            seq.last = tuple(values)
            return list(values)

        def placed(*weights):
            pieces, where, col = [], [], 0
            for w in weights:
                at = 0
                for p in w.mine + w.other:
                    pieces.append(p)
                    where.append((at, col))
                    at += p.shape[0]
                col += w.w.shape[1]
            return pieces, where

        def packet_plan():
            pieces, plan, full, device = [], [], packet.w.shape[0], 0
            for side in (packet.mine, packet.other):
                at = 0
                for p in side:
                    i, r = 0, p.shape[0]
                    while i < r:
                        d, inside = divmod(at + i, full)
                        d += device
                        if inside < blk:
                            k = min(r - i, blk - inside)
                            plan.append((len(pieces), i, k, d * blk + inside, None))
                        else:
                            k = min(r - i, full - inside)
                            plan.append((len(pieces), i, k, None, d * 16))
                        i += k
                    at += r
                    pieces.append(p)
                device += plane
            return pieces, plan

        gains = jnp.stack([attn_in_gain, attn_out_gain, ffn_in_gain, ffn_out_gain])
        own = [query_weight, key_weight, value_weight, output_weight]
        own = jnp.concatenate(own, axis=1)
        gains = jnp.pad(gains, ((0, 12), (0, own.shape[1] - blk)))
        if square:
            flags = jnp.concatenate([segment_ids, live_mask], axis=0).astype(LOW)
            flags = jnp.pad(flags, ((0, 0), (0, own.shape[1] - toks)))
            gains = jnp.concatenate([gains[:4], flags, gains[6:]], axis=0)
        packet = Weight(jnp.concatenate([own, gains], axis=0))
        index = lax.axis_index("ctx") * toks + jnp.arange(toks, dtype=jnp.int32)
        own_info = jnp.concatenate([segment_ids, live_mask, index[None]], axis=0)

        def positions(info):
            seg_all, live_all, index_all = info[0:1], info[1:2], info[2:3]
            seg_col, index_col = segment_ids.reshape(toks, 1), index.reshape(toks, 1)
            start = jnp.sum((seg_all < seg_col).astype(jnp.int32), axis=1)
            allowed = (
                (index_all <= index_col)
                & (seg_all == seg_col)
                & ((live_all == 1) | (index_all == index_col))
            ).astype(LOW)
            freq = jnp.exp(
                jnp.arange(HD // 2, dtype=F32) * (-2.0 * math.log(10000.0) / HD)
            )
            angle = wide(index - start)[:, None] * freq
            return allowed, jnp.cos(angle), jnp.sin(angle)

        x_raw = layer_input.reshape(toks, width)
        dy_raw = out_cotangent.reshape(toks, width)
        wg, wu, wd = Weight(gate_weight), Weight(up_weight), Weight(down_weight)

        packet.near()
        if not square:
            info = lax.all_gather(own_info, "ctx", axis=1, tiled=True)
        x, factors = seq.run(order, x_raw, factors=True)
        packet.far()
        if square:

            def both_info(mine, wx):
                flags = wx[blk + 4 : blk + 6, :toks].astype(jnp.int32)
                there = mine[2:3] + (1 - 2 * lax.axis_index("ctx")) * toks
                return jnp.concatenate(
                    [mine, jnp.concatenate([flags, there], axis=0)], axis=1
                )

            info = seq.run(both_info, own_info, packet.mine[1])
        allowed, cos, sin = seq.run(positions, info)
        packet.core()
        wg.near()
        pieces, plan = packet_plan()
        h1, q, kv, gain, w_qkv, w_out = seq.run(
            first_kernel, x, factors, cos, sin, *pieces, plan=plan, blk=blk, qw=qw, kw=kw
        )
        g1, g2, g3, g4 = [gain[i : i + 1] for i in range(4)]
        if square:
            kv_got = seq.send(to_ctx, kv)
            wg.far()
            kv_all = seq.run(lambda a, b: jnp.concatenate([a, b], 0), kv, kv_got)
        else:
            kv_all = lax.all_gather(kv, "ctx", axis=0, tiled=True)
        length = kv_all.shape[0]

        o, logs, part = seq.run(attn_kernel, q, kv_all, allowed, w_out)
        za = ZSum(part)
        if square:
            wg.mine[3:] = settle(*wg.mine[3:])
        wu.near()
        wg.core()
        wu.far()
        za.middle()
        if square:
            wu.mine[3:] = settle(*wu.mine[3:])
        wd.near()
        wu.core()
        wd.far()
        gate_p, gate_at = placed(wg)
        up_p, up_at = placed(wu)
        x2, h3, gate_up, hid = seq.run(
            ffn_in_kernel, za.out, x, g2, g3, *gate_p, *up_p, gate_at=gate_at, up_at=up_at
        )
        wd.core()
        down_p, down_at = placed(wd)
        part = seq.run(project_kernel, hid, *down_p, at=down_at)
        zf = ZSum(part)
        zf.middle()
        probs, slopes = seq.run(probs_kernel, q, kv_all, allowed, logs)
        dy = seq.run(order, dy_raw)
        qkv_g = seq.run(row_order, w_qkv)
        g1_g = seq.run(order, jnp.broadcast_to(g1, (16, width)), back=True)[:1]

        y, df, dgate, dup, dg4 = seq.run(
            ffn_back_kernel, zf.out, x2, dy, g4, gate_up, *down_p, at=down_at
        )
        part = seq.run(
            ffn_inputs_kernel, dgate, dup, *gate_p, *up_p, gate_at=gate_at, up_at=up_at
        )
        zd = ZSum(part)

        class Scatter:
            def __init__(self, a, b):
                self.ab = a, b

            def low(self):
                low = seq.run(outer_kernel, *self.ab, side=1, cuts=[mid // 2] * 2)
                self.got = [seq.send(to_core, v) for v in low]

            def first(self):
                h = blk // 2
                cuts = [blk] * 3 + [h, h] if square else [mid]
                self.s = seq.run(outer_kernel, *self.ab, *self.got, side=0, cuts=cuts)
                if square:
                    self.gx = seq.send(to_ctx, self.s[3])
                    self.gy = seq.send(to_y, self.s[4])

            def second(self):
                if not square:
                    self.rest = lax.psum_scatter(
                        self.s[0], ("y", "ctx"), scatter_dimension=0, tiled=True
                    )
                    return
                s1, s2 = seq.run(pass_kernel, *self.s[1:3], self.gx, self.gy)
                self.rest = seq.send(to_ctx, s1), seq.send(to_y, s2)

            def end(self):
                if not square:
                    return wide(self.rest)
                return seq.run(sum_kernel, self.s[0], *self.rest)

        sd, sg, su = Scatter(df, hid), Scatter(h3, dgate), Scatter(h3, dup)
        sd.low()
        sg.low()
        sd.first()
        su.low()
        sg.first()
        zd.middle()
        layer_output = seq.run(order, y, back=True)
        sd.second()
        su.got = settle(*su.got)

        dx2, da, dq, own, other, dg23 = seq.run(
            attn_back_kernel, zd.out, x2, dy, za.out, g3, g2, w_out,
            q, kv_all, probs, slopes, cos, sin, toks=toks,
        )
        if square:
            got = seq.send(to_ctx, other)
        else:
            got = lax.psum_scatter(other, "ctx", scatter_dimension=0, tiled=True)
            own = jnp.zeros_like(own)
        sg.second()
        down_grad = sd.end()
        dqkv = seq.run(keys_back_kernel, own, got, cos, sin, dq)
        part = seq.run(project_kernel, dqkv, qkv_g, at=[(0, 0)])
        z1 = ZSum(part)
        so, sq = Scatter(da, o), Scatter(h1, dqkv)
        su.first()
        so.low()
        sq.low()
        dx2 = seq.run(order, dx2, back=True)
        gate_grad = sg.end()
        su.second()
        z1.middle()
        so.first()
        sq.first()
        up_grad = su.end()
        so.second()
        sq.second()
        input_grad, dg1 = seq.run(last_kernel, x_raw, g1_g, z1.out, dx2)
        dg1 = seq.run(order, jnp.broadcast_to(dg1, (16, width)))[:1]
        dgain = jnp.concatenate([dg1, dg23[:2], dg4], axis=0)
        got = seq.send(to_core, dgain[:, mid:])
        dgain = seq.run(lambda a, b: a[:, :mid] + b, dgain, got)
        if square:
            got = seq.send(to_y, dgain[:, mid // 2 :])
            out_grad, qkv_grad = so.end(), sq.end()
            dgain = seq.run(lambda a, b: a[:, : mid // 2] + b, dgain, got)
            dgain = dgain[:, :blk] + to_ctx(dgain[:, blk:])
        else:
            out_grad, qkv_grad = so.end(), sq.end()
            dgain = lax.psum_scatter(
                dgain, ("y", "ctx"), scatter_dimension=1, tiled=True
            )
        return (
            layer_output.reshape(rows, toks, width),
            input_grad.reshape(rows, toks, width),
            qkv_grad[:, :qw],
            qkv_grad[:, qw : qw + kw],
            qkv_grad[:, qw + kw :],
            out_grad,
            gate_grad,
            up_grad,
            down_grad,
            dgain[0],
            dgain[1],
            dgain[2],
            dgain[3],
        )

    return local


def solution(mesh):
    dp, nx, nz = (mesh.shape[a] for a in ("dp", "ctx", "tensor"))
    fine = Mesh(
        mesh.devices.reshape(dp // 2, 2, nx, nz), ("y", "core", "ctx", "tensor")
    )
    d = ("y", "core")
    w = P(("y", "core", "ctx"), "tensor")
    g = P(("y", "core", "ctx"))
    t = P(d, "ctx", None)
    return jax.shard_map(
        make_local(dp // 2, nx, nz),
        mesh=fine,
        in_specs=(t, w, w, w, w, w, w, w, g, g, g, g, t, P(d, "ctx"), P(d, "ctx")),
        out_specs=(t, t, w, w, w, w, w, w, w, g, g, g, g),
        check_vma=False,
    )
```

```python
import math

import jax
import jax.numpy as jnp
from jax import lax
from jax.experimental import pallas as pl
from jax.experimental.pallas import tpu as pltpu
from jax.sharding import Mesh
from jax.sharding import PartitionSpec as P

HD = 256
NORM_EPSILON = 1e-06
SOFT_CAP = 50.0
MASKED_SCORE = -1e30
SWAP = [(0, 1), (1, 0)]
LOW = jnp.bfloat16
F32 = jnp.float32
VMEM_MB = 56
NO_COST = pl.CostEstimate(flops=0, bytes_accessed=0, transcendentals=0)
LONG = pl.CostEstimate(flops=10**12, bytes_accessed=0, transcendentals=0)


def wide(a):
    return a.astype(F32)


def after(value, *deps):
    return lax.optimization_barrier((value,) + deps)[0]


class Order:
    def __init__(self):
        self.last = ()

    def __call__(self, *values):
        return after(values, *self.last) if self.last else values

    def run(self, fn, *values, **kw):
        out = fn(*self(*values), **kw)
        self.last = (out,)
        return out

    def send(self, move, value):
        (value,) = self(value)
        self.last = (value,)
        return move(value)


def to_ctx(a):
    return lax.ppermute(a, "ctx", SWAP)


def to_y(a):
    return lax.ppermute(a, "y", SWAP)


def to_core(a):
    return lax.ppermute(a, "core", SWAP)


def nn(a, b):
    return jnp.dot(a, b, preferred_element_type=F32)


def nt(a, b):
    return lax.dot_general(a, b, (((1,), (1,)), ((), ())), preferred_element_type=F32)


def tn(a, b):
    return lax.dot_general(a, b, (((0,), (0,)), ((), ())), preferred_element_type=F32)


def norm_factor(v):
    return lax.rsqrt(jnp.mean(v * v, axis=-1, keepdims=True) + NORM_EPSILON)


def over_rows(rows, step, carry=None, block=64):
    block = math.gcd(rows, block)
    at = lambda i: pl.ds(pl.multiple_of(i * block, block), block)
    return lax.fori_loop(0, rows // block, lambda i, c: step(at(i), c), carry)


def fold(v):
    return sum(v[i : i + 8] for i in range(0, v.shape[0], 8))


def norm_back_rows(v, gain, grad):
    r = norm_factor(v)
    w = (1.0 + gain) * grad
    vr = v * r
    dv = r * (w - vr * jnp.mean(vr * w, axis=-1, keepdims=True))
    return dv, fold(grad * vr)


def gelu_parts(u):
    k = math.sqrt(2.0 / math.pi)
    th = jnp.tanh(k * (u + 0.044715 * u * u * u))
    g = 0.5 * u * (1.0 + th)
    dg = 0.5 * (1.0 + th) + 0.5 * u * (1.0 - th * th) * k * (1.0 + 3 * 0.044715 * u * u)
    return g, dg


def turn(v, c, s):
    h = HD // 2
    a, b = v[:, :h], v[:, h:]
    return jnp.concatenate([a * c - b * s, b * c + a * s], axis=1)


def turn_back(v, c, s):
    h = HD // 2
    a, b = v[:, :h], v[:, h:]
    return jnp.concatenate([a * c + b * s, b * c - a * s], axis=1)


def spec(block, index, mode=None):
    return pl.BlockSpec(block, index, pipeline_mode=mode)


def kernel(body, grid, ins, outs, scratch=(), cost=NO_COST):
    return pl.pallas_call(
        body,
        grid=grid,
        in_specs=[spec(*e[1:]) for e in ins],
        out_specs=[spec(*e[2:]) for e in outs],
        out_shape=[jax.ShapeDtypeStruct(*e[:2]) for e in outs],
        scratch_shapes=list(scratch),
        cost_estimate=cost,
        name=body.__qualname__.split(".")[0],
        compiler_params=pltpu.CompilerParams(vmem_limit_bytes=VMEM_MB * 2**20),
    )(*[e[0] for e in ins])


def all_of(shape):
    return tuple(shape), lambda *i: (0,) * len(shape), pl.Buffered(1)


def first_kernel(x, r, cos, sin, *pieces, plan, blk, qw, kw):
    toks, width = x.shape
    wide_w = pieces[0].shape[1]
    cols = qw + 2 * kw
    devices = width // blk
    lanes = -(-blk // 128) * 128
    scale = 1.0 / math.sqrt(HD)
    n = len(pieces)

    def body(x_r, r_r, c_r, s_r, *refs):
        piece_h = refs[:n]
        h_h, q_r, kv_r, g_r, w_h, o_h = refs[n : n + 6]
        h_r, w_r, raw_g_r, sems = refs[n + 6 :]
        c = Copies(sems)
        for k, (p, r0, rows, at, gain_at) in enumerate(plan):
            if at is None:
                src = piece_h[p].at[pl.ds(r0, rows), pl.ds(0, lanes)]
                c.start(("g", k), src, raw_g_r.at[pl.ds(gain_at, rows)])
        for k, (p, r0, rows, at, gain_at) in enumerate(plan):
            if at is not None:
                c.start(("w", k), piece_h[p].at[pl.ds(r0, rows)], w_r.at[pl.ds(at, rows)])
        c.wait(*[k for k in c.known if k[0] == "g"])
        rows16 = raw_g_r[...]
        gains = [rows16[d * 16 : d * 16 + 8, :blk] for d in range(devices)]
        gains = wide(jnp.concatenate(gains, axis=1))
        g_r[...] = gains
        g1 = 1.0 + gains[0:1]

        def normed(at, _):
            h_r[at, :] = (wide(x_r[at, :]) * r_r[at, 0:1] * g1).astype(LOW)

        over_rows(toks, normed)
        c.start("h", h_r, h_h)
        c.wait(*[k for k in c.known if k[0] == "w"])
        c.start("qkv", w_r.at[:, pl.ds(0, cols)], w_h)
        c.start("out", w_r.at[:, pl.ds(cols, wide_w - cols)], o_h)
        raw = nn(h_r[...], w_r[:, :cols])
        co, si = c_r[...], s_r[...]
        for j in range(qw // HD):
            cut = slice(j * HD, (j + 1) * HD)
            q_r[:, cut] = (turn(raw[:, cut], co, si) * scale).astype(LOW)
        for j in range(kw // HD):
            cut = slice(j * HD, (j + 1) * HD)
            k = turn(raw[:, qw + j * HD : qw + (j + 1) * HD], co, si)
            kv_r[:, cut] = k.astype(LOW)
        kv_r[:, kw:] = raw[:, qw + kw :].astype(LOW)
        c.wait("h", "qkv", "out")

    ins = [(v, "vmem") for v in (x, r, cos, sin)] + [(p, "hbm") for p in pieces]
    outs = [
        ((toks, width), LOW, "hbm"),
        ((toks, qw), LOW, "vmem"),
        ((toks, 2 * kw), LOW, "vmem"),
        ((8, width), F32, "vmem"),
        ((width, cols), LOW, "hbm"),
        ((width, wide_w - cols), LOW, "hbm"),
    ]
    scratch = [((toks, width), LOW), ((width, wide_w), LOW), ((16 * devices, lanes), LOW)]
    return streaming(body, ins, outs, scratch, len(plan) + 3, LONG)


def query_block(rows, length):
    return min(rows, 256 if length <= 2048 else 128)


def attn_kernel(q, kv, allowed, w):
    rows, qw = q.shape
    length = kv.shape[0]
    width = w.shape[0]
    qb = query_block(rows, length)
    heads = qw // HD

    def body(q_r, kv_r, m_r, w_r, o_r, t_r, a_r):
        ok = m_r[...] > 0
        k, v = kv_r[:, :HD], kv_r[:, HD:]
        logs = []
        for j in range(heads):
            cut = slice(j * HD, (j + 1) * HD)
            b = jnp.tanh(nt(q_r[:, cut], k) * (1.0 / SOFT_CAP))
            c = jnp.where(ok, SOFT_CAP * b, MASKED_SCORE)
            peak = jnp.max(c, axis=-1, keepdims=True)
            e = jnp.exp(c - peak)
            total = jnp.sum(e, axis=-1, keepdims=True)
            p = (e / total).astype(LOW)
            o_r[:, cut] = nn(p, v).astype(LOW)
            logs.append(jnp.broadcast_to(peak + jnp.log(total), (qb, 128)))
        t_r[...] = jnp.concatenate(logs, axis=1)
        a_r[...] = nt(o_r[...], w_r[...]).astype(LOW)

    row = lambda n: ((qb, n), lambda i: (i, 0))
    ins = [(q, *row(qw)), (kv, *all_of(kv.shape)), (allowed, *row(length))]
    ins += [(w, *all_of(w.shape))]
    outs = [
        ((rows, qw), LOW, *row(qw)),
        ((rows, 128 * heads), F32, *row(128 * heads)),
        ((rows, width), LOW, *row(width)),
    ]
    return kernel(body, (rows // qb,), ins, outs, cost=LONG)


def attn_back_kernel(
    dh3, x2, dy, a, g3, g2, w, q, kv, allowed, logs, cos, sin, toks
):
    rows, width = x2.shape
    qw = q.shape[1]
    length = kv.shape[0]
    qb = query_block(rows, length)
    heads = qw // HD
    other = toks if length == 2 * toks else length
    scale = 1.0 / math.sqrt(HD)

    def body(
        d_r, x_r, dy_r, a_r, g3_r, g2_r, w_r, q_r, kv_r, m_r, t_r, c_r, s_r,
        dx_r, da_r, dq_r, own_r, other_r, dg_r, dkv_r,
    ):
        @pl.when(pl.program_id(0) == 0)
        def _():
            dkv_r[...] = jnp.zeros_like(dkv_r)
            dg_r[...] = jnp.zeros_like(dg_r)

        def step(at, total):
            dv3, dg3 = norm_back_rows(x_r[at, :], g3_r[...], wide(d_r[at, :]))
            dx2 = wide(dy_r[at, :]) + dv3
            dx_r[at, :] = dx2
            da, dg2 = norm_back_rows(wide(a_r[at, :]), g2_r[...], dx2)
            da_r[at, :] = da.astype(LOW)
            return total[0] + dg2, total[1] + dg3

        none = jnp.zeros((8, width), F32)
        dg2, dg3 = over_rows(qb, step, (none, none))
        dg_r[0:1] += jnp.sum(dg2, axis=0, keepdims=True)
        dg_r[1:2] += jnp.sum(dg3, axis=0, keepdims=True)
        do = nn(da_r[...], w_r[...]).astype(LOW)
        ok = m_r[...] > 0
        k, v = kv_r[:, :HD], kv_r[:, HD:]
        c, s = c_r[...], s_r[...]
        dk = dv = 0.0
        for j in range(heads):
            cut = slice(j * HD, (j + 1) * HD)
            qj, doj = q_r[:, cut], do[:, cut]
            b = jnp.tanh(nt(qj, k) * (1.0 / SOFT_CAP))
            logit = jnp.where(ok, SOFT_CAP * b, MASKED_SCORE)
            p = jnp.exp(logit - t_r[:, j * 128 : j * 128 + 1])
            dp = nt(doj, v)
            dc = p * (dp - jnp.sum(p * dp, axis=-1, keepdims=True))
            ds = (dc * (1.0 - b * b)).astype(LOW)
            dq_r[:, cut] = (turn_back(nn(ds, k), c, s) * scale).astype(LOW)
            dk = dk + tn(ds, qj)
            dv = dv + tn(p.astype(LOW), doj)
        dkv_r[:, :HD] += dk
        dkv_r[:, HD:] += dv

        @pl.when(pl.program_id(0) == rows // qb - 1)
        def _():
            own_r[...] = dkv_r[:toks]
            other_r[...] = dkv_r[length - other :].astype(LOW)

    row = lambda n: ((qb, n), lambda i: (i, 0))
    ins = [(v, *row(width)) for v in (dh3, x2, dy, a)]
    ins += [(v, *all_of(v.shape)) for v in (g3, g2, w)]
    ins += [(q, *row(qw)), (kv, *all_of(kv.shape)), (allowed, *row(length))]
    ins += [(logs, *row(128 * heads)), (cos, *row(HD // 2)), (sin, *row(HD // 2))]
    outs = [
        ((rows, width), F32, *row(width)),
        ((rows, width), LOW, *row(width)),
        ((rows, qw), LOW, *row(qw)),
        ((toks, 2 * HD), F32, *all_of((toks, 2 * HD))),
        ((other, 2 * HD), LOW, *all_of((other, 2 * HD))),
        ((8, width), F32, *all_of((8, width))),
    ]
    scratch = [pltpu.VMEM((length, 2 * HD), F32)]
    return kernel(body, (rows // qb,), ins, outs, scratch, LONG)


class Copies:
    def __init__(self, sems):
        self.sems, self.known = sems, {}

    def start(self, name, src, dst):
        self.known[name] = pltpu.make_async_copy(src, dst, self.sems.at[len(self.known)])
        self.known[name].start()

    def wait(self, *names):
        for name in names:
            self.known[name].wait()


def streaming(body, ins, outs, scratch, copies, cost=NO_COST):
    place = {"vmem": pl.BlockSpec(memory_space=pltpu.VMEM), "hbm": pl.BlockSpec(memory_space=pltpu.HBM)}
    return pl.pallas_call(
        body,
        in_specs=[place[p] for _, p in ins],
        out_specs=[place[p] for _, _, p in outs],
        out_shape=[jax.ShapeDtypeStruct(s, d) for s, d, _ in outs],
        scratch_shapes=[pltpu.VMEM(*v) for v in scratch]
        + [pltpu.SemaphoreType.DMA((copies,))],
        cost_estimate=cost,
        name=body.__qualname__.split(".")[0],
        compiler_params=pltpu.CompilerParams(vmem_limit_bytes=VMEM_MB * 2**20),
    )(*[a for a, _ in ins])


def row_parts(rows, block=128):
    return [pl.ds(i, min(block, rows)) for i in range(0, rows, min(block, rows))]


def col_chunks(where, total, most=768):
    starts = sorted({c for _, c in where}) + [total]
    chunks = []
    for lo, hi in zip(starts, starts[1:]):
        while lo < hi:
            n = hi - lo if hi - lo <= most else min(most, -(-(hi - lo) // 2 // 128) * 128)
            chunks.append((lo, n))
            lo += n
    return chunks


def start_cols(c, name, j, chunk, pieces, shapes, where, dst):
    names, (lo, n) = [], chunk
    for i, (p, s, (row, col)) in enumerate(zip(pieces, shapes, where)):
        if col <= lo < col + s[1]:
            src = p.at[:, pl.ds(lo - col, n)]
            c.start((name, j, i), src, dst.at[pl.ds(row, s[0]), pl.ds(lo, n)])
            names.append((name, j, i))
    return names


def start_rows(c, name, pieces, shapes, where, dst):
    names = []
    for i in sorted(range(len(pieces)), key=lambda i: where[i]):
        (row, col), s = where[i], shapes[i]
        c.start((name, i), pieces[i], dst.at[pl.ds(row, s[0]), pl.ds(col, s[1])])
        names.append((row, row + s[0], (name, i)))
    return names


def wait_rows(c, names, lo, hi, seen):
    for first, last, name in names:
        if first < hi and last > lo and name not in seen:
            seen.add(name)
            c.wait(name)


def row_groups(rows, most=768):
    return [(i, min(most, rows - i)) for i in range(0, rows, most)]


def ffn_in_kernel(a, x, g2, g3, *weights, gate_at, up_at):
    rows, width = x.shape
    ng = len(gate_at)
    shapes = [w.shape for w in weights]
    units = shapes[-1][1]
    parts = row_parts(rows)
    chunks = col_chunks(gate_at, units)

    def body(a_h, x_h, g2_r, g3_r, *refs):
        w_h, refs = refs[: len(shapes)], refs[len(shapes) :]
        x2_h, h_h, gu_h, hid_h = refs[:4]
        a_r, x_r, x2_r, h_r, wg_r, wu_r, gu_r, hid_r, sems = refs[4:]
        c = Copies(sems)
        for i, at in enumerate(parts):
            c.start(("a", i), a_h.at[at], a_r.at[at])
            c.start(("x", i), x_h.at[at], x_r.at[at])
        need = []
        for j, chunk in enumerate(chunks):
            names = start_cols(c, "g", j, chunk, w_h[:ng], shapes[:ng], gate_at, wg_r)
            names += start_cols(c, "u", j, chunk, w_h[ng:], shapes[ng:], up_at, wu_r)
            need.append(names)
        out = []

        def send(src, dst, at):
            out.append(("out", len(out)))
            c.start(out[-1], src.at[at], dst.at[at])

        for i, part in enumerate(parts):
            c.wait(("a", i), ("x", i))

            def normed(at, _, first=part.start):
                at = pl.ds(pl.multiple_of(first + at.start, 16), at.size)
                av = wide(a_r[at, :])
                x2 = wide(x_r[at, :]) + av * norm_factor(av) * (1.0 + g2_r[...])
                x2_r[at, :] = x2
                h_r[at, :] = (x2 * norm_factor(x2) * (1.0 + g3_r[...])).astype(LOW)

            over_rows(part.size, normed)
            send(x2_r, x2_h, (part,))
            send(h_r, h_h, (part,))
        for names, (lo, n) in zip(need, chunks):
            c.wait(*names)
            at = pl.ds(lo, n)
            h = h_r[...]
            gate, up = nn(h, wg_r[:, at]), nn(h, wu_r[:, at])
            at2 = pl.ds(units + lo, n)
            gu_r[:, at] = gate.astype(LOW)
            gu_r[:, at2] = up.astype(LOW)
            hid_r[:, at] = (gelu_parts(gate)[0] * up).astype(LOW)
            for src, dst, cut in ((gu_r, gu_h, at), (gu_r, gu_h, at2), (hid_r, hid_h, at)):
                send(src, dst, (slice(None), cut))
        c.wait(*out)

    t, n = (rows, width), (rows, units)
    ins = [(a, "hbm"), (x, "hbm"), (g2, "vmem"), (g3, "vmem")]
    ins += [(w, "hbm") for w in weights]
    gu = (rows, 2 * units)
    outs = [(t, F32, "hbm"), (t, LOW, "hbm"), (gu, LOW, "hbm"), (n, LOW, "hbm")]
    w = (width, units)
    scratch = [(t, LOW), (t, LOW), (t, F32), (t, LOW), (w, LOW), (w, LOW)]
    scratch += [(gu, LOW), (n, LOW)]
    copies = 4 * len(parts) + (3 + len(weights)) * len(chunks)
    return streaming(body, ins, outs, scratch, copies)


def project_kernel(u, *weights, at):
    rows, cols = u.shape
    shapes = [w.shape for w in weights]
    width = sum(s[0] for s in shapes)
    groups = row_groups(width)

    def body(u_r, *refs):
        w_h, (o_h, w_r, o_r, sems) = refs[: len(shapes)], refs[len(shapes) :]
        c = Copies(sems)
        names, seen = start_rows(c, "w", w_h, shapes, at, w_r), set()
        for g, (lo, n) in enumerate(groups):
            wait_rows(c, names, lo, lo + n, seen)
            cut = pl.ds(lo, n)
            o_r[:, cut] = nt(u_r[...], w_r[cut, :]).astype(LOW)
            c.start(("out", g), o_r.at[:, cut], o_h.at[:, cut])
        c.wait(*[("out", g) for g in range(len(groups))])

    ins = [(u, "vmem")] + [(w, "hbm") for w in weights]
    outs = [((rows, width), LOW, "hbm")]
    scratch = [((width, cols), LOW), ((rows, width), LOW)]
    return streaming(body, ins, outs, scratch, len(weights) + len(groups))[0]


def ffn_back_kernel(f, x2, dy, g4, gate_up, *weights, at):
    rows, width = x2.shape
    units = gate_up.shape[1] // 2
    shapes = [w.shape for w in weights]
    parts = row_parts(rows)
    chunks = col_chunks(at, units, 1152)

    def body(f_h, x2_h, dy_h, g4_r, gu_h, *refs):
        w_h, refs = refs[: len(shapes)], refs[len(shapes) :]
        y_h, df_h, dg_h, du_h, g_r = refs[:5]
        f_r, x2_r, dy_r, gate_r, up_r, w_r, y_r, df_r, dg_r, du_r, sems = refs[5:]
        c = Copies(sems)
        for i, part in enumerate(parts):
            for name, src, dst in (("f", f_h, f_r), ("x", x2_h, x2_r), ("d", dy_h, dy_r)):
                c.start((name, i), src.at[part], dst.at[part])
        need = []
        for j, (lo, n) in enumerate(chunks):
            names = start_cols(c, "w", j, (lo, n), w_h, shapes, at, w_r)
            cut = pl.ds(lo, n)
            c.start(("gate", j), gu_h.at[:, cut], gate_r.at[:, cut])
            up_at = pl.ds(units + lo, n)
            c.start(("up", j), gu_h.at[:, up_at], up_r.at[:, cut])
            need.append(names + [("gate", j), ("up", j)])
        out = []

        def send(src, dst, cut):
            out.append(("out", len(out)))
            c.start(out[-1], src.at[cut], dst.at[cut])

        total = jnp.zeros((8, width), F32)
        for i, part in enumerate(parts):
            c.wait(("f", i), ("x", i), ("d", i))

            def step(cut, total, first=part.start):
                cut = pl.ds(pl.multiple_of(first + cut.start, 16), cut.size)
                fv, g4v, x2v = wide(f_r[cut, :]), g4_r[...], x2_r[cut, :]
                y_r[cut, :] = (x2v + fv * norm_factor(fv) * (1.0 + g4v)).astype(LOW)
                df, dg = norm_back_rows(fv, g4v, wide(dy_r[cut, :]))
                df_r[cut, :] = df.astype(LOW)
                return total + dg

            total = over_rows(part.size, step, total)
            send(y_r, y_h, (part,))
            send(df_r, df_h, (part,))
        g_r[...] = jnp.sum(total, axis=0, keepdims=True)
        for names, (lo, n) in zip(need, chunks):
            c.wait(*names)
            cut = pl.ds(lo, n)
            dh = nn(df_r[...], w_r[:, cut])
            gl, dgl = gelu_parts(wide(gate_r[:, cut]))
            dg_r[:, cut] = (dh * wide(up_r[:, cut]) * dgl).astype(LOW)
            du_r[:, cut] = (dh * gl).astype(LOW)
            send(dg_r, dg_h, (slice(None), cut))
            send(du_r, du_h, (slice(None), cut))
        c.wait(*out)

    t, n = (rows, width), (rows, units)
    ins = [(v, "hbm") for v in (f, x2, dy)] + [(g4, "vmem")]
    ins += [(v, "hbm") for v in (gate_up, *weights)]
    outs = [(t, LOW, "hbm"), (t, LOW, "hbm"), (n, LOW, "hbm"), (n, LOW, "hbm")]
    outs += [((1, width), F32, "vmem")]
    scratch = [(t, LOW), (t, F32), (t, LOW), (n, LOW), (n, LOW), ((width, units), LOW)]
    scratch += [(t, LOW), (t, LOW), (n, LOW), (n, LOW)]
    copies = 5 * len(parts) + (4 + len(weights)) * len(chunks)
    return streaming(body, ins, outs, scratch, copies)


def ffn_inputs_kernel(dg, du, *weights, gate_at, up_at):
    rows, units = dg.shape
    ng = len(gate_at)
    shapes = [w.shape for w in weights]
    width = sum(s[0] for s in shapes[ng:])
    groups = row_groups(width)

    def body(dg_r, du_r, *refs):
        w_h, (o_h, wg_r, wu_r, o_r, sems) = refs[: len(shapes)], refs[len(shapes) :]
        c = Copies(sems)
        order = sorted(range(len(shapes)), key=lambda i: (gate_at + up_at)[i][0])
        names, seen = [], set()
        for i in order:
            (row, col), s = (gate_at + up_at)[i], shapes[i]
            dst = (wg_r if i < ng else wu_r).at[pl.ds(row, s[0]), pl.ds(col, s[1])]
            c.start(("w", i), w_h[i], dst)
            names.append((row, row + s[0], ("w", i)))
        for g, (lo, n) in enumerate(groups):
            wait_rows(c, names, lo, lo + n, seen)
            cut = pl.ds(lo, n)
            v = nt(dg_r[...], wg_r[cut, :]) + nt(du_r[...], wu_r[cut, :])
            o_r[:, cut] = v.astype(LOW)
            c.start(("out", g), o_r.at[:, cut], o_h.at[:, cut])
        c.wait(*[("out", g) for g in range(len(groups))])

    ins = [(dg, "vmem"), (du, "vmem")] + [(w, "hbm") for w in weights]
    outs = [((rows, width), LOW, "hbm")]
    w = ((width, units), LOW)
    scratch = [w, w, ((rows, width), LOW)]
    return streaming(body, ins, outs, scratch, len(weights) + len(groups))[0]


def outer_kernel(a, b, *got, side, cuts, cost=NO_COST):
    toks, cols = b.shape
    mid = a.shape[1] // 2
    bn = math.gcd(cols, 768)
    chunks = [pl.ds(i, bn) for i in range(0, cols, bn)]
    n, m = len(got), len(cuts)
    at = [sum(cuts[:i]) for i in range(m)]
    step = mid // n if n else 0

    def body(a_h, b_h, *refs):
        got_h, out_h = refs[:n], refs[n : n + m]
        a_r, b_r, got_r, out_r, sems = refs[n + m :]
        c = Copies(sems)
        c.start("a", a_h.at[:, pl.ds(side * mid, mid)], a_r)
        for j, part in enumerate(chunks):
            c.start(("b", j), b_h.at[:, part], b_r.at[:, part])
        for i in range(n):
            c.start(("got", i), got_h[i], got_r.at[pl.ds(i * step, step)])
        c.wait("a")
        for j, part in enumerate(chunks):
            c.wait(("b", j))
            v = tn(a_r[...], b_r[:, part])
            if n:
                if j == 0:
                    c.wait(*[("got", i) for i in range(n)])
                v = v + wide(got_r[:, part])
            out_r[:, part] = v.astype(LOW)
            for i in range(m):
                c.start(
                    ("out", i, j),
                    out_r.at[pl.ds(at[i], cuts[i]), part],
                    out_h[i].at[:, part],
                )
        c.wait(*[("out", i, j) for i in range(m) for j in range(len(chunks))])

    ins = [(v, "hbm") for v in (a, b, *got)]
    outs = [((r, cols), LOW, "hbm") for r in cuts]
    full = (mid, cols)
    scratch = [((toks, mid), LOW), ((toks, cols), LOW)]
    scratch += [(full if n else (16, 128), LOW), (full, LOW)]
    copies = 1 + len(chunks) * (1 + m) + n
    return streaming(body, ins, outs, scratch, copies, cost)


def sum_kernel(s, rx, ry):
    rows, cols = s.shape
    bc = math.gcd(cols, 768)

    def body(s_r, x_r, y_r, o_r):
        o_r[...] = wide(s_r[...]) + wide(x_r[...]) + wide(y_r[...])

    tile = ((rows, bc), lambda j: (0, j))
    ins = [(v, *tile) for v in (s, rx, ry)]
    return kernel(body, (cols // bc,), ins, [((rows, cols), F32, *tile)])[0]


def pass_kernel(s1, s2, gx, gy):
    rows, cols = s1.shape
    h = rows // 2
    bc = math.gcd(cols, 768)

    def body(s1_r, s2_r, gx_r, gy_r, t1_r, t2_r):
        t1_r[:h] = s1_r[:h]
        t1_r[h:] = (wide(s1_r[h:]) + wide(gy_r[...])).astype(LOW)
        t2_r[:h] = (wide(s2_r[:h]) + wide(gx_r[...])).astype(LOW)
        t2_r[h:] = s2_r[h:]

    full, part = ((rows, bc), lambda j: (0, j)), ((h, bc), lambda j: (0, j))
    ins = [(s1, *full), (s2, *full), (gx, *part), (gy, *part)]
    return kernel(body, (cols // bc,), ins, [(s1.shape, LOW, *full)] * 2)


def last_kernel(x, gain, dh1, dx2):
    rows, width = x.shape
    br = min(rows, 256)

    def body(x_r, g_r, d_r, dx_r, o_r, dg_r):
        def step(at, total):
            dv, dg = norm_back_rows(wide(x_r[at, :]), g_r[...], wide(d_r[at, :]))
            o_r[at, :] = dx_r[at, :] + dv
            return total + dg

        @pl.when(pl.program_id(0) == 0)
        def _():
            dg_r[...] = jnp.zeros_like(dg_r)

        total = over_rows(br, step, jnp.zeros((8, width), F32))
        dg_r[...] += jnp.sum(total, axis=0, keepdims=True)

    row = ((br, width), lambda i: (i, 0))
    ins = [(x, *row), (gain, *all_of(gain.shape)), (dh1, *row), (dx2, *row)]
    outs = [((rows, width), F32, *row), ((1, width), F32, *all_of((1, width)))]
    return kernel(body, (rows // br,), ins, outs)


def order_kernel(v, bits, back, ny, nx, factors=False):
    rows, width = v.shape
    blk = width // (2 * ny * nx)
    br = min(rows, 128)
    here = lambda c, y, x: (c * ny + y) * nx + x
    there = lambda c, y, x: (y * 2 + c) * nx + x
    keys = [(c, y, x) for c in range(2) for y in range(ny) for x in range(nx)]
    src, dst = (here, there) if back else (there, here)
    flips = 3 if ny == 2 and nx == 2 else 1

    def body(b_r, v_r, o_r, *f_r):
        def step(at, _):
            rows_ = v_r[at, :]
            if factors:
                f = norm_factor(wide(rows_))
                f_r[0][at, :] = jnp.broadcast_to(f, (f.shape[0], 128))
            cut = lambda j: rows_[:, j * blk : (j + 1) * blk]
            parts = {k: cut(src(*k)) for k in keys}
            for pos in range(flips):
                on = b_r[pos] == 0
                flip = lambda k: tuple(1 - e if i == pos else e for i, e in enumerate(k))
                parts = {k: jnp.where(on, parts[k], parts[flip(k)]) for k in keys}
            o_r[at, :] = jnp.concatenate([parts[k] for k in sorted(keys, key=lambda k: dst(*k))], axis=1)

        over_rows(br, step)

    tile = pl.BlockSpec((br, width), lambda i: (i, 0))
    return pl.pallas_call(
        body,
        grid=(rows // br,),
        in_specs=[pl.BlockSpec(memory_space=pltpu.SMEM), tile],
        out_specs=[tile, pl.BlockSpec((br, 128), lambda i: (i, 0))][: 1 + factors],
        out_shape=[
            jax.ShapeDtypeStruct(v.shape, v.dtype),
            jax.ShapeDtypeStruct((rows, 128), F32),
        ][: 1 + factors],
        cost_estimate=NO_COST,
    )(bits, v)


def keys_back_kernel(own, got, cos, sin, dq):
    qw = dq.shape[1]

    def body(a_r, b_r, c_r, s_r, q_r, o_r):
        v = a_r[...] + wide(b_r[...])
        o_r[:, :qw] = q_r[...]
        o_r[:, qw : qw + HD] = turn_back(v[:, :HD], c_r[...], s_r[...]).astype(LOW)
        o_r[:, qw + HD :] = v[:, HD:].astype(LOW)

    ins = [(v, *all_of(v.shape)) for v in (own, got, cos, sin, dq)]
    shape = (own.shape[0], qw + own.shape[1])
    return kernel(body, (1,), ins, [(shape, LOW, *all_of(shape))])[0]


def make_local(ny, nx, nz):
    square = ny == 2 and nx == 2
    plane = ny * nx

    def order(v, back=False, factors=False):
        bits = jnp.stack([lax.axis_index(a) for a in ("core", "y", "ctx")])
        out = order_kernel(v, bits.astype(jnp.int32), back, ny, nx, factors)
        return out if factors else out[0]

    def row_order(w):
        blk = w.shape[0] // (2 * plane)
        c = lax.axis_index("core")
        out = jnp.zeros_like(w)
        for half in range(2):
            for y in range(ny):
                for x in range(nx):
                    i = (half * ny + y) * nx + x
                    gy, gx = y, x
                    if square:
                        gy, gx = y ^ lax.axis_index("y"), x ^ lax.axis_index("ctx")
                    at = ((gy * 2 + (c ^ half)) * nx + gx) * blk
                    piece = lax.slice_in_dim(w, i * blk, (i + 1) * blk, axis=0)
                    out = lax.dynamic_update_slice_in_dim(out, piece, at, 0)
        return out

    def local(
        layer_input,
        query_weight,
        key_weight,
        value_weight,
        output_weight,
        gate_weight,
        up_weight,
        down_weight,
        attn_in_gain,
        attn_out_gain,
        ffn_in_gain,
        ffn_out_gain,
        out_cotangent,
        segment_ids,
        live_mask,
    ):
        rows, toks, width = layer_input.shape
        blk, qw = query_weight.shape
        kw = key_weight.shape[1]
        qkv_w = qw + 2 * kw
        mid = width // 2
        seq = Order()

        class ZSum:
            def __init__(self, part):
                self.own = lax.psum_scatter(
                    part, "tensor", scatter_dimension=0, tiled=True
                )

            def middle(self):
                (own,) = seq(self.own)
                seq.last = (own,)
                self.out = lax.all_gather(own, "tensor", axis=0, tiled=True)

        class Weight:
            def __init__(self, w):
                self.w = w
                if not square:
                    m = lax.all_gather(w, ("y", "ctx"), axis=0, tiled=True)
                    self.mine, self.other = [m], [to_core(m)]

            def near(self):
                if square:
                    w = self.w
                    self.mine = [w, seq.send(to_ctx, w), seq.send(to_y, w)]
                    self.other = [seq.send(to_core, w)]

            def far(self):
                if square:
                    h = blk // 2
                    wx, wy = seq(*self.mine[1:])
                    self.mine += [seq.send(to_y, wx[:h]), seq.send(to_ctx, wy[h:])]
                    self.other += [seq.send(to_core, wx), seq.send(to_core, wy)]

            def core(self):
                if square:
                    self.mine[3:] = seq(*self.mine[3:])
                    self.other += [seq.send(to_core, d) for d in self.mine[3:]]

        def settle(*values):
            values = seq(*values)
            seq.last = tuple(values)
            return list(values)

        def placed(*weights):
            pieces, where, col = [], [], 0
            for w in weights:
                at = 0
                for p in w.mine + w.other:
                    pieces.append(p)
                    where.append((at, col))
                    at += p.shape[0]
                col += w.w.shape[1]
            return pieces, where

        def packet_plan():
            pieces, plan, full, device = [], [], packet.w.shape[0], 0
            for side in (packet.mine, packet.other):
                at = 0
                for p in side:
                    i, r = 0, p.shape[0]
                    while i < r:
                        d, inside = divmod(at + i, full)
                        d += device
                        if inside < blk:
                            k = min(r - i, blk - inside)
                            plan.append((len(pieces), i, k, d * blk + inside, None))
                        else:
                            k = min(r - i, full - inside)
                            plan.append((len(pieces), i, k, None, d * 16))
                        i += k
                    at += r
                    pieces.append(p)
                device += plane
            return pieces, plan

        gains = jnp.stack([attn_in_gain, attn_out_gain, ffn_in_gain, ffn_out_gain])
        own = [query_weight, key_weight, value_weight, output_weight]
        own = jnp.concatenate(own, axis=1)
        gains = jnp.pad(gains, ((0, 12), (0, own.shape[1] - blk)))
        if square:
            flags = jnp.concatenate([segment_ids, live_mask], axis=0).astype(LOW)
            flags = jnp.pad(flags, ((0, 0), (0, own.shape[1] - toks)))
            gains = jnp.concatenate([gains[:4], flags, gains[6:]], axis=0)
        packet = Weight(jnp.concatenate([own, gains], axis=0))
        index = lax.axis_index("ctx") * toks + jnp.arange(toks, dtype=jnp.int32)
        own_info = jnp.concatenate([segment_ids, live_mask, index[None]], axis=0)

        def positions(info):
            seg_all, live_all, index_all = info[0:1], info[1:2], info[2:3]
            seg_col, index_col = segment_ids.reshape(toks, 1), index.reshape(toks, 1)
            start = jnp.sum((seg_all < seg_col).astype(jnp.int32), axis=1)
            allowed = (
                (index_all <= index_col)
                & (seg_all == seg_col)
                & ((live_all == 1) | (index_all == index_col))
            ).astype(LOW)
            freq = jnp.exp(
                jnp.arange(HD // 2, dtype=F32) * (-2.0 * math.log(10000.0) / HD)
            )
            angle = wide(index - start)[:, None] * freq
            return allowed, jnp.cos(angle), jnp.sin(angle)

        x_raw = layer_input.reshape(toks, width)
        dy_raw = out_cotangent.reshape(toks, width)
        wg, wu, wd = Weight(gate_weight), Weight(up_weight), Weight(down_weight)

        packet.near()
        if not square:
            info = lax.all_gather(own_info, "ctx", axis=1, tiled=True)
        x, factors = seq.run(order, x_raw, factors=True)
        packet.far()
        if square:

            def both_info(mine, wx):
                flags = wx[blk + 4 : blk + 6, :toks].astype(jnp.int32)
                there = mine[2:3] + (1 - 2 * lax.axis_index("ctx")) * toks
                return jnp.concatenate(
                    [mine, jnp.concatenate([flags, there], axis=0)], axis=1
                )

            info = seq.run(both_info, own_info, packet.mine[1])
        allowed, cos, sin = seq.run(positions, info)
        packet.core()
        wg.near()
        pieces, plan = packet_plan()
        h1, q, kv, gain, w_qkv, w_out = seq.run(
            first_kernel, x, factors, cos, sin, *pieces, plan=plan, blk=blk, qw=qw, kw=kw
        )
        g1, g2, g3, g4 = [gain[i : i + 1] for i in range(4)]
        if square:
            kv_got = seq.send(to_ctx, kv)
            wg.far()
            kv_all = seq.run(lambda a, b: jnp.concatenate([a, b], 0), kv, kv_got)
        else:
            kv_all = lax.all_gather(kv, "ctx", axis=0, tiled=True)
        length = kv_all.shape[0]

        o, logs, part = seq.run(attn_kernel, q, kv_all, allowed, w_out)
        za = ZSum(part)
        if square:
            wg.mine[3:] = settle(*wg.mine[3:])
        wu.near()
        wg.core()
        wu.far()
        za.middle()
        if square:
            wu.mine[3:] = settle(*wu.mine[3:])
        wd.near()
        wu.core()
        wd.far()
        gate_p, gate_at = placed(wg)
        up_p, up_at = placed(wu)
        x2, h3, gate_up, hid = seq.run(
            ffn_in_kernel, za.out, x, g2, g3, *gate_p, *up_p, gate_at=gate_at, up_at=up_at
        )
        wd.core()
        down_p, down_at = placed(wd)
        part = seq.run(project_kernel, hid, *down_p, at=down_at)
        zf = ZSum(part)
        zf.middle()
        dy = seq.run(order, dy_raw)
        qkv_g = seq.run(row_order, w_qkv)
        g1_g = seq.run(order, jnp.broadcast_to(g1, (16, width)), back=True)[:1]

        y, df, dgate, dup, dg4 = seq.run(
            ffn_back_kernel, zf.out, x2, dy, g4, gate_up, *down_p, at=down_at
        )
        part = seq.run(
            ffn_inputs_kernel, dgate, dup, *gate_p, *up_p, gate_at=gate_at, up_at=up_at
        )
        zd = ZSum(part)

        class Scatter:
            def __init__(self, a, b):
                self.ab = a, b

            def low(self):
                low = seq.run(outer_kernel, *self.ab, side=1, cuts=[mid // 2] * 2)
                self.got = [seq.send(to_core, v) for v in low]

            def first(self):
                h = blk // 2
                cuts = [blk] * 3 + [h, h] if square else [mid]
                self.s = seq.run(outer_kernel, *self.ab, *self.got, side=0, cuts=cuts)
                if square:
                    self.gx = seq.send(to_ctx, self.s[3])
                    self.gy = seq.send(to_y, self.s[4])

            def second(self):
                if not square:
                    self.rest = lax.psum_scatter(
                        self.s[0], ("y", "ctx"), scatter_dimension=0, tiled=True
                    )
                    return
                s1, s2 = seq.run(pass_kernel, *self.s[1:3], self.gx, self.gy)
                self.rest = seq.send(to_ctx, s1), seq.send(to_y, s2)

            def end(self):
                if not square:
                    return wide(self.rest)
                return seq.run(sum_kernel, self.s[0], *self.rest)

        sd, sg, su = Scatter(df, hid), Scatter(h3, dgate), Scatter(h3, dup)
        sd.low()
        sg.low()
        sd.first()
        su.low()
        sg.first()
        zd.middle()
        layer_output = seq.run(order, y, back=True)
        sd.second()
        su.got = settle(*su.got)

        dx2, da, dq, own, other, dg23 = seq.run(
            attn_back_kernel, zd.out, x2, dy, za.out, g3, g2, w_out,
            q, kv_all, allowed, logs, cos, sin, toks=toks,
        )
        if square:
            got = seq.send(to_ctx, other)
        else:
            got = lax.psum_scatter(other, "ctx", scatter_dimension=0, tiled=True)
            own = jnp.zeros_like(own)
        sg.second()
        down_grad = sd.end()
        dqkv = seq.run(keys_back_kernel, own, got, cos, sin, dq)
        part = seq.run(project_kernel, dqkv, qkv_g, at=[(0, 0)])
        z1 = ZSum(part)
        so, sq = Scatter(da, o), Scatter(h1, dqkv)
        su.first()
        so.low()
        sq.low()
        dx2 = seq.run(order, dx2, back=True)
        gate_grad = sg.end()
        su.second()
        z1.middle()
        so.first()
        sq.first()
        up_grad = su.end()
        so.second()
        sq.second()
        input_grad, dg1 = seq.run(last_kernel, x_raw, g1_g, z1.out, dx2)
        dg1 = seq.run(order, jnp.broadcast_to(dg1, (16, width)))[:1]
        dgain = jnp.concatenate([dg1, dg23[:2], dg4], axis=0)
        got = seq.send(to_core, dgain[:, mid:])
        dgain = seq.run(lambda a, b: a[:, :mid] + b, dgain, got)
        if square:
            got = seq.send(to_y, dgain[:, mid // 2 :])
            out_grad, qkv_grad = so.end(), sq.end()
            dgain = seq.run(lambda a, b: a[:, : mid // 2] + b, dgain, got)
            dgain = dgain[:, :blk] + to_ctx(dgain[:, blk:])
        else:
            out_grad, qkv_grad = so.end(), sq.end()
            dgain = lax.psum_scatter(
                dgain, ("y", "ctx"), scatter_dimension=1, tiled=True
            )
        return (
            layer_output.reshape(rows, toks, width),
            input_grad.reshape(rows, toks, width),
            qkv_grad[:, :qw],
            qkv_grad[:, qw : qw + kw],
            qkv_grad[:, qw + kw :],
            out_grad,
            gate_grad,
            up_grad,
            down_grad,
            dgain[0],
            dgain[1],
            dgain[2],
            dgain[3],
        )

    return local


def solution(mesh):
    dp, nx, nz = (mesh.shape[a] for a in ("dp", "ctx", "tensor"))
    fine = Mesh(
        mesh.devices.reshape(dp // 2, 2, nx, nz), ("y", "core", "ctx", "tensor")
    )
    d = ("y", "core")
    w = P(("y", "core", "ctx"), "tensor")
    g = P(("y", "core", "ctx"))
    t = P(d, "ctx", None)
    return jax.shard_map(
        make_local(dp // 2, nx, nz),
        mesh=fine,
        in_specs=(t, w, w, w, w, w, w, w, g, g, g, g, t, P(d, "ctx"), P(d, "ctx")),
        out_specs=(t, t, w, w, w, w, w, w, w, g, g, g, g),
        check_vma=False,
    )
```
